256 devices in a mesh: seq: 32 (over y, x, core), dp: 8 (over z).
Axes of the slice: x: 4, y: 4, z: 8, core: 2. Of those that a mesh axis runs over, the one named last changes fastest.
Arguments:
- tokens: bfloat16 [8, 8192, 2048], P('dp', 'seq'), may hold values from -6 to 6
- w_qkv: bfloat16 [2048, 3, 1024], P('seq'), may hold values from -0.125 to 0.125
- weight_table: float32 [16, 8], replicated, may hold values from 0.3 to 3
- weight_index: int32 [8, 64, 6], P('dp', 'seq'), may hold values from 0 to 15
- cotangent: bfloat16 [8, 8192, 1024], P('dp', 'seq'), may hold values from -6 to 6
Outputs:
- attn_out: bfloat16 [8, 8192, 1024], P('dp', 'seq')
- grad_w: float32 [2048, 3, 1024], P('seq')
The draws below stay inside these ranges and needn't reach their ends.
All inputs are finite; a program needn't handle non-finite values.
Results may differ from the reference program's by a relative error of at most 0.02.
Values may be sent and summed in bfloat16 or wider, within the bound.
No kernel may reach another device: no remote copies, remote signals or barrier semaphores. Data moves between devices by JAX's collectives and lax.ppermute only.
A program may use at most 128 MiB of HBM per device.

```python
import math
import jax
import jax.numpy as jnp
from jax import lax

D = 2048
HEADS = 8
HEAD = 128
TOK_DEV = 256
QB = 128
NW = 16
HD = 1024
DOCS = 8
LEN = 8192
TREE = 5
N_SEQ = 32


def plant(values, rng, least, high):
    longest = values.shape.index(max(values.shape))
    spots = []
    for shift in (0, 1):
        where = [jax.random.randint(jax.random.fold_in(rng, axis), (), 0, length) for axis, length in enumerate(values.shape)]
        where[longest] = (where[longest] + shift) % values.shape[longest]
        spots.append(tuple(where))
    return values.at[spots[0]].set(least).at[spots[1]].set(high)


def spiked(result, own_key, source, target, blocks, factor):
    def block_of(axis_at):
        return (jnp.arange(result.shape[axis_at]) // (result.shape[axis_at] // blocks)).reshape((-1,) + (1,) * (result.ndim - 1 - axis_at))

    first = jax.random.permutation(own_key, blocks)[block_of(target)]
    second = (block_of(target) + blocks // 2) % blocks
    return jnp.where((block_of(source) == first) | (block_of(source) == second), factor * result, result)


def shard_levels(own_key, extent, split, least, largest):
    gain, own = 1.0, jax.random.fold_in(own_key, 6)
    for dim, shards_of in split:
        heights = jnp.exp(jax.random.uniform(jax.random.fold_in(own, dim), (shards_of,), jnp.float32, least / len(split), largest / len(split)))
        gain = gain * jnp.repeat(heights, extent[dim] // shards_of).reshape([-1 if axis == dim else 1 for axis in range(len(extent))])
    return gain


def scatter_about(stream_key, shape, scale, reach, cuts=(), dtype=jnp.bfloat16):
    drawn = jax.random.normal(stream_key, shape, jnp.float32) * scale
    if len(cuts) > 0:
        drawn = shard_levels(stream_key, shape, cuts, -0.22, 0.18) * drawn
    return jnp.clip(drawn, min=-reach, max=reach).astype(dtype)


def noise_with(key, shape, width, reach, split, heavy, kind=jnp.bfloat16):
    result = width * jax.random.normal(key, shape, jnp.float32)
    if split:
        result = result * shard_levels(key, shape, split, -0.22, 0.18)
    return jnp.clip(spiked(result, jax.random.fold_in(key, 3), *heavy), -reach, reach).astype(kind)


def setup_inputs(seed: int = 0) -> dict:
    streams_of = jax.random.split(jax.random.key(seed), 6)
    tokens = noise_with(streams_of[0], (DOCS, LEN, D), 1.0, 6.0, ((0, 8), (1, 32)), (1, 2, 32, 2.75))
    w_qkv = scatter_about(streams_of[1], (D, 3, HD), D ** -0.5, 0.125, ((0, 32),))
    weight_table = jnp.clip(jnp.exp(jax.random.uniform(streams_of[2], (NW, HEADS), jnp.float32, math.log(0.3), math.log(3.0))), 0.3, 3.0)
    weight_index = plant(jax.random.randint(streams_of[3], (DOCS, LEN // QB, TREE + 1), 0, NW), jax.random.fold_in(streams_of[3], 1), 0, NW - 1).astype(jnp.int32)
    cotangent = scatter_about(streams_of[4], (DOCS, LEN, HD), 1.0, 6.0, ((0, 8), (1, 32)))
    return {"tokens": tokens, "w_qkv": w_qkv, "weight_table": weight_table, "weight_index": weight_index, "cotangent": cotangent}


def product(pattern, left_op, right_op):
    return jnp.einsum(pattern, left_op.astype(jnp.float32), right_op.astype(jnp.float32))

def block_pass(queries, keys_bf, values_bf, upstream, local_scale, level_coef, level_states):
    block_len = queries.shape[0]
    causal = jnp.arange(block_len)[:, None] >= jnp.arange(block_len)[None, :]
    row_scale = jnp.transpose(local_scale)[:, :, None]
    raw_scores = product('thd,shd->hts', queries, keys_bf)
    scores = jnp.where(causal[None], raw_scores * row_scale, 0.0).astype(jnp.bfloat16)
    local_out = product('hts,she->the', scores, values_bf)
    far_terms = product('thd,hdle->thle', queries, level_states)
    attended = (local_out + lax.optimization_barrier(jnp.sum(far_terms * level_coef[..., None], axis=2))).astype(jnp.bfloat16)
    raw_grads = product('the,she->hts', upstream, values_bf)
    dscores = jnp.where(causal[None], raw_grads * row_scale, 0.0).astype(jnp.bfloat16)
    far_grads = product('the,hdle->thld', upstream, level_states)
    grad_q = product('hts,shd->thd', dscores, keys_bf) + lax.optimization_barrier(jnp.sum(far_grads * level_coef[..., None], axis=2))
    grad_k = product('hts,thd->shd', dscores, queries)
    grad_v = product('hts,the->she', scores, upstream)
    scaled = (queries.astype(jnp.float32)[:, :, None, :] * level_coef[..., None]).astype(jnp.bfloat16)
    level_grads = product('thld,the->hlde', scaled, upstream)
    return (attended.reshape(block_len, -1), grad_q, grad_k, grad_v, level_grads)

def one_document(inputs, chosen, upstream_all, flat_weights, weight_table):
    block_count = N_SEQ
    block_len = TOK_DEV
    head_count = HEADS
    head_dim = HEAD
    inner_width = HEADS * HEAD
    projected = jnp.dot(inputs, flat_weights, preferred_element_type=jnp.float32).astype(jnp.bfloat16)
    projected = projected.reshape(block_count, block_len, 3, head_count, head_dim)
    queries = projected[:, :, 0]
    keys_bf = projected[:, :, 1]
    values_bf = projected[:, :, 2]
    weights_tok = jnp.repeat(weight_table[chosen], QB, axis=0)
    weights_tok = weights_tok.reshape(block_count, block_len, TREE + 1, head_count)
    states = product('pshd,pshe->phde', keys_bf, values_bf)
    block_ids = jnp.arange(block_count)
    level_list = []
    flag_list = []
    for level_no in range(1, TREE + 1):
        half_span = 2 ** (level_no - 1)
        grouped = states.reshape(block_count // (2 * half_span), 2, half_span, head_count, head_dim, head_dim)
        left_sum = lax.optimization_barrier(jnp.sum(grouped[:, 0], axis=1))
        level_list.append(jnp.repeat(left_sum, 2 * half_span, axis=0))
        flag_list.append((block_ids // half_span % 2).astype(jnp.float32) / math.sqrt(head_dim * half_span * block_len))
    level_states = jnp.stack(level_list, axis=3).astype(jnp.bfloat16)
    scale_level = jnp.stack(flag_list, axis=1)
    level_coef = jnp.transpose(weights_tok[:, :, 1:], (0, 1, 3, 2)) * scale_level[:, None, None, :]
    local_scale = weights_tok[:, :, 0] / math.sqrt(head_dim * block_len)
    upstream = upstream_all.reshape(block_count, block_len, head_count, head_dim)
    results = lax.map(lambda pieces: block_pass(*pieces), (queries, keys_bf, values_bf, upstream, local_scale, level_coef, level_states))
    level_grads = results[4]
    running = jnp.zeros((block_count, head_count, head_dim, head_dim), jnp.float32)
    for level_no in range(1, TREE + 1):
        half_span = 2 ** (level_no - 1)
        grouped = level_grads[:, :, level_no - 1].reshape(block_count // (2 * half_span), 2, half_span, head_count, head_dim, head_dim)
        right_sum = lax.optimization_barrier(jnp.sum(grouped[:, 1], axis=1))
        placed = jnp.stack([right_sum, jnp.zeros_like(right_sum)], axis=1)
        placed = jnp.broadcast_to(placed[:, :, None], (block_count // (2 * half_span), 2, half_span, head_count, head_dim, head_dim))
        running = running + placed.reshape(block_count, head_count, head_dim, head_dim)
    state_grads = running.astype(jnp.bfloat16)
    grad_k = results[2] + product('pshe,phde->pshd', values_bf, state_grads)
    grad_v = results[3] + product('pshd,phde->pshe', keys_bf, state_grads)
    qkv_grads = jnp.stack([results[1], grad_k, grad_v], axis=2).astype(jnp.bfloat16)
    qkv_grads = qkv_grads.reshape(block_count, block_len, 3 * inner_width)
    attended = results[0].reshape(block_count * block_len, inner_width)
    return (attended, qkv_grads)

def reference(tokens, w_qkv, weight_table, weight_index, cotangent):
    flat_weights = w_qkv.reshape(D, 3 * HEADS * HEAD)

    def per_doc(running, pieces):
        inputs, chosen, upstream = pieces
        attended, qkv_grads = one_document(inputs, chosen, upstream, flat_weights, weight_table)

        def per_block(summed, couple):
            partial_value = jnp.dot(couple[0].T, couple[1], preferred_element_type=jnp.float32)
            rounded = lax.optimization_barrier(partial_value.astype(jnp.bfloat16))
            return (summed + rounded.astype(jnp.float32), None)
        running, ignored = lax.scan(per_block, running, (inputs.reshape(N_SEQ, TOK_DEV, D), qkv_grads))
        return (running, attended)
    anchor = jnp.zeros((D, 3 * HEADS * HEAD), jnp.float32)
    grad_w, attn_out = lax.scan(per_doc, anchor, (tokens, weight_index, cotangent))
    return (attn_out, grad_w.reshape(D, 3, HEADS * HEAD))
```

```python
import math

import jax
import jax.numpy as jnp
from jax import lax
from jax.experimental import pallas as pl
from jax.experimental.pallas import tpu as pltpu
from jax.sharding import Mesh, PartitionSpec as P

BF = jnp.bfloat16
F32 = jnp.float32
HEAD = 128
QB = 128
BLOCK = 256
D = 2048
COLS = 768
HALF = 384
VMEM_LIMIT = 50 * 1024 * 1024


def shift(value, axis, size, step):
    return lax.ppermute(value, axis, [(i, (i - step) % size) for i in range(size)])


def swap(value, axis, size, mask):
    return lax.ppermute(value, axis, [(i, i ^ mask) for i in range(size)])


def dot(a, b, ca, cb):
    return lax.dot_general(a, b, (((ca,), (cb,)), ((), ())), preferred_element_type=F32)


def smem():
    return pl.BlockSpec(memory_space=pltpu.SMEM)


def vmem():
    return pl.BlockSpec(memory_space=pltpu.VMEM)


def call(kernel, args, n_smem, outs, scratch=(), flops=0, nbytes=0):
    return pl.pallas_call(
        kernel,
        out_shape=outs,
        in_specs=[smem()] * n_smem + [vmem()] * (len(args) - n_smem),
        out_specs=[vmem()] * len(outs),
        scratch_shapes=list(scratch),
        compiler_params=pltpu.CompilerParams(vmem_limit_bytes=VMEM_LIMIT),
        cost_estimate=pl.CostEstimate(flops=flops, bytes_accessed=nbytes, transcendentals=0),
    )(*args)


def level_coef(pos, idx, table, blk, group, level, head):
    cs = blk // 2
    y, x, core, zl = pos[0], pos[1], pos[2], pos[4]
    row = idx[blk, group * 6 + level]
    lam = table[row, (core * 2 + zl) * 2 + head]
    if level == 0:
        return lam * (1.0 / math.sqrt(HEAD * BLOCK))
    bit = [(core + cs) & 1, x & 1, (x >> 1) & 1, y & 1, (y >> 1) & 1][level - 1]
    return lam * bit.astype(F32) * (1.0 / math.sqrt(HEAD * 2 ** (level - 1) * BLOCK))


def project_kernel(pos, idx, table, *refs):
    toks = refs[0:4]
    cots = refs[4:8]
    a_parts = refs[8:13]
    b_parts = refs[13:18]
    qkv, s1, x0, g1, m2, m3, m4, m5, w = refs[18:]
    y, x, core = pos[0], pos[1], pos[2]

    def place(part, first, yy, xx, col):
        for cs in range(2):
            row = (yy * 4 + xx) * 128 + ((core + cs) & 1) * 64
            row = pl.multiple_of(row, 64)
            w[pl.ds(row, 64), col : col + HALF] = part[first + cs * 64 : first + cs * 64 + 64, :]

    for slot in range(4):
        xx = (x + slot) & 3
        yy = (y + slot) & 3
        far = slot // 2
        for dist, part in ((0, 0), (1, 1), (3, 2)):
            place(a_parts[part], slot * 128, (y + dist) & 3, xx, 0)
            place(b_parts[part], slot * 128, yy, (x + dist) & 3, HALF)
        place(a_parts[3 + far], (slot % 2) * 128, (y + 2) & 3, xx, 0)
        place(b_parts[3 + far], (slot % 2) * 128, yy, (x + 2) & 3, HALF)

    for blk in range(4):
        for part in range(3):
            cols = slice(part * 256, part * 256 + 256)
            qkv[blk, :, cols] = dot(toks[blk][...], w[:, cols], 1, 0).astype(BF)

    for zs in range(2):
        for h in range(2):
            lanes = slice(h * HEAD, h * HEAD + HEAD)
            total = None
            sums = [None] * 4
            for cs in range(2):
                blk = cs * 2 + zs
                keys = qkv[blk, :, 256 + h * HEAD : 256 + h * HEAD + HEAD]
                vals = qkv[blk, :, 512 + h * HEAD : 512 + h * HEAD + HEAD]
                state = dot(keys, vals, 0, 0)
                s1[blk, h] = state.astype(BF)
                total = state if total is None else total + state
                first = None
                for g in range(2):
                    rows = slice(g * QB, g * QB + QB)
                    outer = dot(qkv[blk, rows, lanes], cots[blk][rows, lanes], 0, 0)
                    term = outer * level_coef(pos, idx, table, blk, g, 1, h)
                    first = term if first is None else first + term
                    for k in range(4):
                        term = outer * level_coef(pos, idx, table, blk, g, k + 2, h)
                        sums[k] = term if sums[k] is None else sums[k] + term
                g1[blk, h] = first
            x0[zs, h] = total.astype(BF)
            m2[zs, h] = sums[0]
            m3[zs, h] = sums[1]
            m4[zs, h] = sums[2].astype(BF)
            m5[zs, h] = sums[3].astype(BF)


def local_kernel(pos, idx, table, qkv, c0, c1, c2, c3, loc):
    cots = (c0, c1, c2, c3)
    rows = lax.broadcasted_iota(jnp.int32, (BLOCK, BLOCK), 0)
    cols = lax.broadcasted_iota(jnp.int32, (BLOCK, BLOCK), 1)
    causal = rows >= cols
    upper = rows < QB
    for blk in range(4):
        for h in range(2):
            q = qkv[blk, :, h * HEAD : h * HEAD + HEAD]
            k = qkv[blk, :, 256 + h * HEAD : 256 + h * HEAD + HEAD]
            v = qkv[blk, :, 512 + h * HEAD : 512 + h * HEAD + HEAD]
            c = cots[blk][:, h * HEAD : h * HEAD + HEAD]
            scale = jnp.where(
                upper,
                level_coef(pos, idx, table, blk, 0, 0, h),
                level_coef(pos, idx, table, blk, 1, 0, h),
            )
            scale = jnp.where(causal, scale, 0.0)
            scores = (dot(q, k, 1, 1) * scale).astype(BF)
            dscores = (dot(c, v, 1, 1) * scale).astype(BF)
            loc[blk, :, h * HEAD : h * HEAD + HEAD] = dot(dscores, k, 1, 0)
            loc[blk, :, 256 + h * HEAD : 256 + h * HEAD + HEAD] = dot(dscores, q, 0, 0)
            loc[blk, :, 512 + h * HEAD : 512 + h * HEAD + HEAD] = dot(scores, c, 0, 0)
            loc[blk, :, 768 + h * HEAD : 768 + h * HEAD + HEAD] = dot(scores, v, 1, 0)


def finish_kernel(pos, idx, table, *refs):
    toks = refs[0:4]
    cots = refs[4:8]
    qkv, loc, s1, g1 = refs[8:12]
    cx1, cx2, cx3, cy1, cy2, cy3 = refs[12:18]
    own, r1, r2, r3 = refs[18:22]
    attn, pa, pb, grads = refs[22:]
    y, x, core, zh = pos[0], pos[1], pos[2], pos[3]
    for zs in range(2):
        for h in range(2):
            far = [
                None,
                cx1[zs, h].astype(F32),
                cx2[zs, h].astype(F32) + cx3[zs, h].astype(F32),
                cy1[zs, h].astype(F32),
                cy2[zs, h].astype(F32) + cy3[zs, h].astype(F32),
            ]
            chip = own[zs, h].astype(F32) + r1[zs, h].astype(F32)
            chip = chip + r2[zs, h].astype(F32) + r3[zs, h].astype(F32)
            for cs in range(2):
                blk = cs * 2 + zs
                other = (1 - cs) * 2 + zs
                far[0] = s1[other, h].astype(F32)
                grad = (chip + g1[other, h]).astype(BF)
                qs = slice(h * HEAD, h * HEAD + HEAD)
                ks = slice(256 + h * HEAD, 256 + h * HEAD + HEAD)
                vs = slice(512 + h * HEAD, 512 + h * HEAD + HEAD)
                ats = slice(768 + h * HEAD, 768 + h * HEAD + HEAD)
                for g in range(2):
                    rows = slice(g * QB, g * QB + QB)
                    mixed = None
                    for level in range(1, 6):
                        term = far[level - 1] * level_coef(pos, idx, table, blk, g, level, h)
                        mixed = term if mixed is None else mixed + term
                    mixed = mixed.astype(BF)
                    out = loc[blk, rows, ats] + dot(qkv[blk, rows, qs], mixed, 1, 0)
                    attn[blk, rows, qs] = out.astype(BF)
                    dq = loc[blk, rows, qs] + dot(cots[blk][rows, qs], mixed, 1, 1)
                    grads[blk, rows, qs] = dq.astype(BF)
                dk = loc[blk, :, ks] + dot(qkv[blk, :, vs], grad, 1, 1)
                grads[blk, :, ks] = dk.astype(BF)
                dv = loc[blk, :, vs] + dot(qkv[blk, :, ks], grad, 1, 0)
                grads[blk, :, vs] = dv.astype(BF)

    for tile in range(8):
        part = None
        for blk in range(4):
            term = dot(toks[blk][:, tile * 256 : tile * 256 + 256], grads[blk], 0, 0)
            part = term if part is None else part + term
        part = part.astype(BF)
        for sub in range(2):
            chip_at = tile * 2 + sub
            dy = (chip_at // 4 - y) & 3
            dx = (chip_at % 4 - x) & 3
            for c in range(2):
                for piece in range(4):
                    row = ((c + core) & 1) * 64 + ((piece - zh) & 3) * 16
                    row = pl.multiple_of(row, 16)
                    at = sub * 128 + c * 64 + piece * 16
                    pa[dy, dx, pl.ds(row, 16), :] = part[at : at + 16, :HALF]
                    pb[dx, dy, pl.ds(row, 16), :] = part[at : at + 16, HALF:]


def place_kernel(pos, a00, a01, a10, a11, e0, e1, e2, e3, attn_out, grad_w):
    core, zh, zl = pos[2], pos[3], pos[4]
    attns = ((a00, a01), (a10, a11))
    for cs in range(2):
        for zs in range(2):
            group = ((core + cs) & 1) * 2 + ((zl + zs) & 1)
            lane = pl.multiple_of(group * 256, 256)
            attn_out[:, pl.ds(lane, 256)] = attns[cs][zs][...]
            for step, part in enumerate((e0, e1, e2, e3)):
                row = pl.multiple_of(((zh + step) & 3) * 16, 16)
                for third in range(3):
                    grad_w[third, pl.ds(row, 16), pl.ds(lane, 256)] = part[
                        zs, cs, :, third * 256 : third * 256 + 256
                    ].astype(F32)


def gather_ring(chunk, first, second):
    near = [chunk] + [shift(chunk, first, 4, step) for step in (1, 2, 3)]
    mine = jnp.concatenate(near, axis=0)
    ahead = shift(mine, second, 4, 1)
    behind = shift(mine, second, 4, 3)
    far_low = shift(behind[:256], second, 4, 3)
    far_high = shift(ahead[256:], second, 4, 1)
    return [mine, ahead, behind, far_low, far_high]


def add(*parts):
    total = parts[0].astype(F32)
    for part in parts[1:]:
        total = total + part.astype(F32)
    return total.astype(BF)


def scatter_ring(parts, first, second):
    low = shift(parts[2, :2], first, 4, 3)
    high = shift(parts[2, 2:], first, 4, 1)
    onward = jnp.concatenate([add(parts[1, :2], low), parts[1, 2:]], axis=0)
    backward = jnp.concatenate([parts[3, :2], add(parts[3, 2:], high)], axis=0)
    total = add(parts[0], shift(onward, first, 4, 3), shift(backward, first, 4, 1))
    return add(total[0], *[shift(total[step], second, 4, -step) for step in (1, 2, 3)])


def per_device(tokens, w_qkv, weight_table, weight_index, cotangent):
    y, x, core = lax.axis_index("y"), lax.axis_index("x"), lax.axis_index("core")
    zh, zl = lax.axis_index("zh"), lax.axis_index("zl")
    pos = jnp.stack([y, x, core, zh, zl]).astype(jnp.int32)
    inputs = tokens[0]

    tok01 = swap(inputs, "zl", 2, 1)
    tok10 = swap(inputs, "core", 2, 1)
    tok11 = swap(tok01, "core", 2, 1)
    toks = [inputs, tok01, tok10, tok11]

    planes = jnp.transpose(w_qkv, (1, 0, 2)).reshape(3, 64, 2, 2, 256)
    planes = lax.dynamic_index_in_dim(planes, zl, axis=3, keepdims=False)

    def columns_of(c):
        picked = lax.dynamic_index_in_dim(planes, c, axis=2, keepdims=False)
        return jnp.concatenate([picked[0], picked[1], picked[2]], axis=1)

    chunk = jnp.concatenate([columns_of(core), swap(columns_of(1 - core), "core", 2, 1)], axis=0)
    a_parts = gather_ring(chunk[:, :HALF], "x", "y")
    b_parts = gather_ring(chunk[:, HALF:], "y", "x")

    ups = cotangent[0].reshape(BLOCK, 2, 2, 256)
    up_own = lax.dynamic_index_in_dim(ups, zl, axis=2, keepdims=False)
    up_z = lax.dynamic_index_in_dim(ups, 1 - zl, axis=2, keepdims=False)
    ups = jnp.stack([up_own, swap(up_z, "zl", 2, 1)], axis=0)
    kept = lax.dynamic_index_in_dim(ups, core, axis=2, keepdims=False)
    given = swap(lax.dynamic_index_in_dim(ups, 1 - core, axis=2, keepdims=False), "core", 2, 1)
    cots = [kept[0], kept[1], given[0], given[1]]

    rows = weight_index.reshape(1, 12)
    rows = jnp.concatenate([rows, swap(rows, "zl", 2, 1)], axis=0)
    idx = jnp.concatenate([rows, swap(rows, "core", 2, 1)], axis=0)
    scalars = [pos, idx, weight_table]

    square = (2, 2, HEAD, HEAD)
    qkv, s1, x0, g1, m2, m3, m4, m5 = call(
        project_kernel,
        scalars + toks + cots + a_parts + b_parts,
        3,
        [
            jax.ShapeDtypeStruct((4, BLOCK, COLS), BF),
            jax.ShapeDtypeStruct((4, 2, HEAD, HEAD), BF),
            jax.ShapeDtypeStruct(square, BF),
            jax.ShapeDtypeStruct((4, 2, HEAD, HEAD), F32),
            jax.ShapeDtypeStruct(square, F32),
            jax.ShapeDtypeStruct(square, F32),
            jax.ShapeDtypeStruct(square, BF),
            jax.ShapeDtypeStruct(square, BF),
        ],
        scratch=[pltpu.VMEM((D, COLS), BF)],
        flops=2 * 1024 * D * COLS,
        nbytes=10 << 20,
    )

    cx = [swap(x0, "x", 4, mask) for mask in (1, 2, 3)]
    dy = [swap(m, "y", 4, mask) for mask, m in ((1, m4), (2, m5), (3, m5))]
    (loc,) = call(
        local_kernel,
        scalars + [qkv] + cots,
        3,
        [jax.ShapeDtypeStruct((4, BLOCK, 1024), F32)],
        flops=8 * 6 * 2 * BLOCK * BLOCK * HEAD,
        nbytes=8 << 20,
    )
    x1 = add(x0, *cx)
    cy = [swap(x1, "y", 4, mask) for mask in (1, 2, 3)]
    high = dy[0].astype(F32) + dy[1].astype(F32) + dy[2].astype(F32)
    near = (high + m2).astype(BF)
    wide = (high + m3).astype(BF)
    dx = [swap(m, "x", 4, mask) for mask, m in ((1, near), (2, wide), (3, wide))]

    attn, pa, pb = call(
        finish_kernel,
        scalars + toks + cots + [qkv, loc, s1, g1] + cx + cy + [high.astype(BF)] + dx,
        3,
        [
            jax.ShapeDtypeStruct((4, BLOCK, 256), BF),
            jax.ShapeDtypeStruct((4, 4, 128, HALF), BF),
            jax.ShapeDtypeStruct((4, 4, 128, HALF), BF),
        ],
        scratch=[pltpu.VMEM((4, BLOCK, COLS), BF)],
        flops=2 * 1024 * D * COLS,
        nbytes=12 << 20,
    )

    mine_a = scatter_ring(pa, "y", "x")
    mine_b = scatter_ring(pb, "x", "y")
    chip_sum = jnp.concatenate([mine_a, mine_b], axis=1)
    pair = jnp.stack([chip_sum[:64], swap(chip_sum[64:], "core", 2, 1)], axis=0)
    summed = add(pair[:, :16], *[
        shift(pair[:, 16 * step : 16 * step + 16], "zh", 4, -step) for step in (1, 2, 3)
    ])
    both = jnp.stack([summed, swap(summed, "zl", 2, 1)], axis=0)
    ends = [both] + [shift(both, "zh", 4, step) for step in (1, 2, 3)]

    own_block = attn[:2]
    from_core = swap(attn[2:], "core", 2, 1)
    to_z = jnp.stack([own_block[1], from_core[1]], axis=0)
    from_z = swap(to_z, "zl", 2, 1)

    attn_out, grad_w = call(
        place_kernel,
        [pos, own_block[0], from_z[0], from_core[0], from_z[1]] + ends,
        1,
        [
            jax.ShapeDtypeStruct((BLOCK, 1024), BF),
            jax.ShapeDtypeStruct((3, 64, 1024), F32),
        ],
    )
    return attn_out[None], jnp.transpose(grad_w, (1, 0, 2))


def solution(mesh):
    grid = Mesh(mesh.devices.reshape(4, 4, 2, 4, 2), ("y", "x", "core", "zh", "zl"))
    seq, dp = ("y", "x", "core"), ("zh", "zl")
    return jax.shard_map(
        per_device,
        mesh=grid,
        in_specs=(P(dp, seq, None), P(seq, None, None), P(), P(dp, seq, None), P(dp, seq, None)),
        out_specs=(P(dp, seq, None), P(seq, None, None)),
        check_vma=False,
    )
```

```python
import math

import jax
import jax.numpy as jnp
from jax import lax
from jax.experimental import pallas as pl
from jax.experimental.pallas import tpu as pltpu
from jax.sharding import Mesh, PartitionSpec as P

BF = jnp.bfloat16
F32 = jnp.float32
HEAD = 128
QB = 128
BLOCK = 256
D = 2048
COLS = 768
HALF = 384
MIB = 1024 * 1024
SETS = 0x66
HALVES = 0xB4


def shift(value, axis, size, step):
    return lax.ppermute(value, axis, [(i, (i - step) % size) for i in range(size)])


def swap(value, axis, size, mask):
    return lax.ppermute(value, axis, [(i, i ^ mask) for i in range(size)])


def same_set_neighbour(value):
    return lax.ppermute(value, "dp", [(z, (z + 1 if z % 2 else z - 1) % 8) for z in range(8)])


def same_set_far(value):
    return lax.ppermute(value, "dp", [(z, ((7 if SETS >> z & 1 else 3) - z) % 8) for z in range(8)])


def after(value, *others):
    return lax.optimization_barrier((value, *others))[0]


def dot(a, b, ca, cb):
    return lax.dot_general(a, b, (((ca,), (cb,)), ((), ())), preferred_element_type=F32)


def smem():
    return pl.BlockSpec(memory_space=pltpu.SMEM)


def vmem():
    return pl.BlockSpec(memory_space=pltpu.VMEM)


def call(kernel, args, n_smem, outs, scratch=(), grant=16, flops=0, nbytes=0):
    return pl.pallas_call(
        kernel,
        out_shape=[jax.ShapeDtypeStruct(*out) for out in outs],
        in_specs=[smem()] * n_smem + [vmem()] * (len(args) - n_smem),
        out_specs=[vmem()] * len(outs),
        scratch_shapes=list(scratch),
        compiler_params=pltpu.CompilerParams(vmem_limit_bytes=grant * MIB),
        cost_estimate=pl.CostEstimate(flops=flops, bytes_accessed=nbytes, transcendentals=0),
    )(*args)


def lanes(start):
    return pl.ds(pl.multiple_of(start, HEAD), HEAD)


def level_coef(pos, idx, table, blk, group, level, head):
    cs = blk // 2
    y, x, core = pos[0], pos[1], pos[2]
    row = idx[blk, group * 6 + level]
    lam = table[row, (core * 2 + pos[4]) * 2 + head]
    if level == 0:
        return lam * (1.0 / math.sqrt(HEAD * BLOCK))
    bit = [(core + cs) & 1, x & 1, (x >> 1) & 1, y & 1, (y >> 1) & 1][level - 1]
    return lam * bit.astype(F32) * (1.0 / math.sqrt(HEAD * 2 ** (level - 1) * BLOCK))


def prepare_kernel(pos, w, cot, w_own, w_core, c_own, c_z):
    core, kind = pos[2], pos[4]
    mine = pl.multiple_of((core * 2 + kind) * 256, 256)
    other = pl.multiple_of(((1 - core) * 2 + kind) * 256, 256)
    for third in range(3):
        at = slice(third * 256, third * 256 + 256)
        w_own[:, at] = w[third, :, pl.ds(mine, 256)]
        w_core[:, at] = w[third, :, pl.ds(other, 256)]
    c_own[0] = cot[:, pl.ds(mine, 256)]
    c_own[1] = cot[:, pl.ds(other, 256)]
    c_z[0] = cot[:, pl.ds(pl.multiple_of((core * 2 + 1 - kind) * 256, 256), 256)]
    c_z[1] = cot[:, pl.ds(pl.multiple_of(((1 - core) * 2 + 1 - kind) * 256, 256), 256)]


def project_kernel(pos, idx, table, *refs):
    toks = refs[0:4]
    c_own, c_z, c_core = refs[4:7]
    a_parts = refs[7:12]
    b_parts = refs[12:17]
    qkv, cots, s1, x0, g1, m2, m3, m4, m5, w = refs[17:]
    y, x, core = pos[0], pos[1], pos[2]

    def place(part, first, yy, xx, col):
        for cs in range(2):
            row = (yy * 4 + xx) * 128 + ((core + cs) & 1) * 64
            row = pl.multiple_of(row, 64)
            w[pl.ds(row, 64), col : col + HALF] = part[first + cs * 64 : first + cs * 64 + 64, :]

    for slot in range(4):
        xx = (x + slot) & 3
        yy = (y + slot) & 3
        far = slot // 2
        for dist, part in ((0, 0), (1, 1), (3, 2)):
            place(a_parts[part], slot * 128, (y + dist) & 3, xx, 0)
            place(b_parts[part], slot * 128, yy, (x + dist) & 3, HALF)
        place(a_parts[3 + far], (slot % 2) * 128, (y + 2) & 3, xx, 0)
        place(b_parts[3 + far], (slot % 2) * 128, yy, (x + 2) & 3, HALF)
    cots[0] = c_own[0]
    cots[1] = c_z[0]
    cots[2] = c_core[0]
    cots[3] = c_core[1]

    @pl.loop(0, 3)
    def _(part):
        cols = pl.ds(pl.multiple_of(part * 256, 256), 256)
        for blk in range(4):
            qkv[blk, :, cols] = dot(toks[blk][...], w[:, cols], 1, 0).astype(BF)

    @pl.loop(0, 4)
    def _(step):
        zs, h = step // 2, step % 2
        total = None
        sums = [None] * 4
        for cs in range(2):
            blk = cs * 2 + zs
            state = dot(qkv[blk, :, lanes(256 + h * HEAD)], qkv[blk, :, lanes(512 + h * HEAD)], 0, 0)
            s1[blk, h] = state.astype(BF)
            total = state if total is None else total + state
            first = None
            for g in range(2):
                rows = slice(g * QB, g * QB + QB)
                outer = dot(qkv[blk, rows, lanes(h * HEAD)], cots[blk, rows, lanes(h * HEAD)], 0, 0)
                term = outer * level_coef(pos, idx, table, cs * 2 + zs, g, 1, h)
                first = term if first is None else first + term
                for k in range(4):
                    term = outer * level_coef(pos, idx, table, blk, g, k + 2, h)
                    sums[k] = term if sums[k] is None else sums[k] + term
            g1[blk, h] = first
        x0[zs, h] = total.astype(BF)
        m2[zs, h] = sums[0]
        m3[zs, h] = sums[1]
        m4[zs, h] = sums[2].astype(BF)
        m5[zs, h] = sums[3].astype(BF)


def local_kernel(pos, idx, table, qkv, cots, loc):
    rows = lax.broadcasted_iota(jnp.int32, (BLOCK, BLOCK), 0)
    cols = lax.broadcasted_iota(jnp.int32, (BLOCK, BLOCK), 1)
    causal = rows >= cols
    upper = rows < QB

    @pl.loop(0, 8)
    def _(step):
        blk, h = step // 2, step % 2
        q = qkv[blk, :, lanes(h * HEAD)]
        k = qkv[blk, :, lanes(256 + h * HEAD)]
        v = qkv[blk, :, lanes(512 + h * HEAD)]
        c = cots[blk, :, lanes(h * HEAD)]
        scale = jnp.where(
            upper,
            level_coef(pos, idx, table, blk, 0, 0, h),
            level_coef(pos, idx, table, blk, 1, 0, h),
        )
        scale = jnp.where(causal, scale, 0.0)
        scores = (dot(q, k, 1, 1) * scale).astype(BF)
        dscores = (dot(c, v, 1, 1) * scale).astype(BF)
        loc[blk, :, lanes(h * HEAD)] = dot(dscores, k, 1, 0)
        loc[blk, :, lanes(256 + h * HEAD)] = dot(dscores, q, 0, 0)
        loc[blk, :, lanes(512 + h * HEAD)] = dot(scores, c, 0, 0)
        loc[blk, :, lanes(768 + h * HEAD)] = dot(scores, v, 1, 0)


def finish_kernel(pos, idx, table, *refs):
    toks = refs[0:4]
    cots, qkv, loc, s1, g1 = refs[4:9]
    cx1, cx2, cx3, cy1, cy2, cy3 = refs[9:15]
    own, r1, r2, r3 = refs[15:19]
    attn, pa, pb, grads = refs[19:]
    y, x, core, half = pos[0], pos[1], pos[2], pos[5]

    @pl.loop(0, 4)
    def _(step):
        zs, h = step // 2, step % 2
        far = [
            None,
            cx1[zs, h].astype(F32),
            cx2[zs, h].astype(F32) + cx3[zs, h].astype(F32),
            cy1[zs, h].astype(F32),
            cy2[zs, h].astype(F32) + cy3[zs, h].astype(F32),
        ]
        chip = own[zs, h].astype(F32) + r1[zs, h].astype(F32)
        chip = chip + r2[zs, h].astype(F32) + r3[zs, h].astype(F32)
        qs, ks = lanes(h * HEAD), lanes(256 + h * HEAD)
        vs, ats = lanes(512 + h * HEAD), lanes(768 + h * HEAD)
        for cs in range(2):
            blk = cs * 2 + zs
            other = (1 - cs) * 2 + zs
            far[0] = s1[other, h].astype(F32)
            grad = (chip + g1[other, h]).astype(BF)
            for g in range(2):
                rows = slice(g * QB, g * QB + QB)
                mixed = None
                for level in range(1, 6):
                    term = far[level - 1] * level_coef(pos, idx, table, blk, g, level, h)
                    mixed = term if mixed is None else mixed + term
                mixed = mixed.astype(BF)
                out = loc[blk, rows, ats] + dot(qkv[blk, rows, qs], mixed, 1, 0)
                attn[blk, rows, qs] = out.astype(BF)
                dq = loc[blk, rows, qs] + dot(cots[blk, rows, qs], mixed, 1, 1)
                grads[blk, rows, qs] = dq.astype(BF)
            dk = loc[blk, :, ks] + dot(qkv[blk, :, vs], grad, 1, 1)
            grads[blk, :, ks] = dk.astype(BF)
            dv = loc[blk, :, vs] + dot(qkv[blk, :, ks], grad, 1, 0)
            grads[blk, :, vs] = dv.astype(BF)

    @pl.loop(0, 8)
    def _(tile):
        part = None
        for blk in range(4):
            cols = pl.ds(pl.multiple_of(tile * 256, 256), 256)
            term = dot(toks[blk][:, cols], grads[blk], 0, 0)
            part = term if part is None else part + term
        part = part.astype(BF)
        for sub in range(2):
            chip_at = tile * 2 + sub
            dy = (chip_at // 4 - y) & 3
            dx = (chip_at % 4 - x) & 3
            for c in range(2):
                for piece in range(2):
                    row = ((c + core) & 1) * 64 + ((piece + half) & 1) * 32
                    row = pl.multiple_of(row, 32)
                    at = sub * 128 + c * 64 + piece * 32
                    pa[dy, dx, pl.ds(row, 32), :] = part[at : at + 32, :HALF]
                    pb[dx, dy, pl.ds(row, 32), :] = part[at : at + 32, HALF:]


def place_kernel(pos, own, from_core, from_z, mine, near, theirs, attn_out, grad_w):
    core, kind = pos[2], pos[4]
    attns = ((own, from_z.at[0]), (from_core.at[0], from_z.at[1]))
    halves = (pos[5], pos[6])
    for cs in range(2):
        for zs in range(2):
            group = ((core + cs) & 1) * 2 + ((kind + zs) & 1)
            lane = pl.ds(pl.multiple_of(group * 256, 256), 256)
            attn_out[:, lane] = attns[cs][zs][0] if zs == 0 and cs == 0 else attns[cs][zs][...]
            for piece in range(2):
                part = (mine, near)[piece] if zs == 0 else theirs.at[piece]
                row = pl.ds(pl.multiple_of(((halves[zs] + piece) & 1) * 32, 32), 32)
                for third in range(3):
                    grad_w[third, row, lane] = part[
                        cs, :, third * 256 : third * 256 + 256
                    ].astype(F32)


def add(*parts):
    total = parts[0].astype(F32)
    for part in parts[1:]:
        total = total + part.astype(F32)
    return total.astype(BF)


def scatter_ring(parts, first, second):
    low = shift(parts[2, :2], first, 4, 3)
    high = shift(parts[2, 2:], first, 4, 1)
    onward = jnp.concatenate([add(parts[1, :2], low), parts[1, 2:]], axis=0)
    backward = jnp.concatenate([parts[3, :2], add(parts[3, 2:], high)], axis=0)
    total = add(parts[0], shift(onward, first, 4, 3), shift(backward, first, 4, 1))
    return add(total[0], *[shift(total[step], second, 4, -step) for step in (1, 2, 3)])


def per_device(tokens, w_qkv, weight_table, weight_index, cotangent):
    y, x, core = lax.axis_index("y"), lax.axis_index("x"), lax.axis_index("core")
    z = lax.axis_index("dp")
    pos = jnp.stack(
        [y, x, core, z, (SETS >> z) & 1, (HALVES >> z) & 1, (HALVES >> (z ^ 1)) & 1]
    ).astype(jnp.int32)
    inputs = tokens[0]

    rows = weight_index.reshape(1, 12)
    rows = jnp.concatenate([rows, swap(rows, "dp", 8, 1)], axis=0)
    idx = jnp.concatenate([rows, swap(rows, "core", 2, 1)], axis=0)
    scalars = [pos, idx, weight_table]

    w_own, w_core, c_own, c_z = call(
        prepare_kernel,
        [pos, jnp.transpose(w_qkv, (1, 0, 2)), cotangent[0]],
        1,
        [((64, COLS), BF), ((64, COLS), BF), ((2, BLOCK, 256), BF), ((2, BLOCK, 256), BF)],
        grant=4,
        nbytes=2 * MIB,
    )

    chunk = jnp.concatenate([w_own, swap(w_core, "core", 2, 1)], axis=0)
    a_own, b_own = chunk[:, :HALF], chunk[:, HALF:]
    a_mine = jnp.concatenate([a_own] + [shift(a_own, "x", 4, step) for step in (1, 2, 3)], axis=0)
    b_mine = jnp.concatenate([b_own] + [shift(b_own, "y", 4, step) for step in (1, 2, 3)], axis=0)
    a_ahead, a_behind = shift(a_mine, "y", 4, 1), shift(a_mine, "y", 4, 3)
    b_ahead, b_behind = shift(b_mine, "x", 4, 1), shift(b_mine, "x", 4, 3)
    a_parts = [a_mine, a_ahead, a_behind]
    a_parts += [shift(a_behind[:256], "y", 4, 3), shift(a_ahead[256:], "y", 4, 1)]
    b_parts = [b_mine, b_ahead, b_behind]
    b_parts += [shift(b_behind[:256], "x", 4, 3), shift(b_ahead[256:], "x", 4, 1)]

    tok01 = swap(inputs, "dp", 8, 1)
    from_z = swap(c_z, "dp", 8, 1)
    tok10 = swap(after(inputs, a_mine, b_mine), "core", 2, 1)
    tok11 = swap(after(tok01, a_behind, b_behind), "core", 2, 1)
    to_core = jnp.stack([c_own[1], after(from_z, a_behind, b_behind)[1]], axis=0)
    c_core = swap(to_core, "core", 2, 1)
    toks = [inputs, tok01, tok10, tok11]

    square = (2, 2, HEAD, HEAD)
    wide = (4, 2, HEAD, HEAD)
    qkv, cots, s1, x0, g1, m2, m3, m4, m5 = call(
        project_kernel,
        scalars + toks + [c_own, from_z, c_core] + a_parts + b_parts,
        3,
        [
            ((4, BLOCK, COLS), BF),
            ((4, BLOCK, 256), BF),
            (wide, BF),
            (square, BF),
            (wide, F32),
            (square, F32),
            (square, F32),
            (square, BF),
            (square, BF),
        ],
        scratch=[pltpu.VMEM((D, COLS), BF)],
        grant=22,
        flops=2 * 1024 * D * COLS,
        nbytes=10 * MIB,
    )

    cx = [swap(x0, "x", 4, mask) for mask in (1, 2, 3)]
    dy = [swap(m, "y", 4, mask) for mask, m in ((1, m4), (2, m5), (3, m5))]
    (loc,) = call(
        local_kernel,
        scalars + [qkv, cots],
        3,
        [((4, BLOCK, 1024), F32)],
        grant=12,
        flops=8 * 6 * 2 * BLOCK * BLOCK * HEAD,
        nbytes=8 * MIB,
    )
    x1 = add(x0, *cx)
    cy = [swap(x1, "y", 4, mask) for mask in (1, 2, 3)]
    high = dy[0].astype(F32) + dy[1].astype(F32) + dy[2].astype(F32)
    near = (high + m2).astype(BF)
    far = (high + m3).astype(BF)
    dx = [swap(m, "x", 4, mask) for mask, m in ((1, near), (2, far), (3, far))]

    attn, pa, pb = call(
        finish_kernel,
        scalars + toks + [cots, qkv, loc, s1, g1] + cx + cy + [high.astype(BF)] + dx,
        3,
        [((4, BLOCK, 256), BF), ((4, 4, 128, HALF), BF), ((4, 4, 128, HALF), BF)],
        scratch=[pltpu.VMEM((4, BLOCK, COLS), BF)],
        grant=24,
        flops=2 * 1024 * D * COLS,
        nbytes=12 * MIB,
    )

    mine_a = scatter_ring(pa, "y", "x")
    mine_b = scatter_ring(pb, "x", "y")
    chip_sum = jnp.concatenate([mine_a, mine_b], axis=1)
    pair = jnp.stack([chip_sum[:64], swap(chip_sum[64:], "core", 2, 1)], axis=0)
    mine = add(pair[:, :32], same_set_neighbour(pair[:, 32:]))
    mine = add(mine, same_set_far(mine))
    near = same_set_neighbour(mine)
    theirs = swap(jnp.stack([mine, near], axis=0), "dp", 8, 1)

    from_core = swap(attn[2:], "core", 2, 1)
    back = swap(jnp.stack([attn[1], from_core[1]], axis=0), "dp", 8, 1)

    attn_out, grad_w = call(
        place_kernel,
        [pos, attn, from_core, back, mine, near, theirs],
        1,
        [((BLOCK, 1024), BF), ((3, 64, 1024), F32)],
        grant=6,
        nbytes=3 * MIB,
    )
    return attn_out[None], jnp.transpose(grad_w, (1, 0, 2))


def solution(mesh):
    grid = Mesh(mesh.devices.reshape(4, 4, 2, 8), ("y", "x", "core", "dp"))
    seq = ("y", "x", "core")
    return jax.shard_map(
        per_device,
        mesh=grid,
        in_specs=(P("dp", seq, None), P(seq, None, None), P(), P("dp", seq, None), P("dp", seq, None)),
        out_specs=(P("dp", seq, None), P(seq, None, None)),
        check_vma=False,
    )
```

```python
import math

import jax
import jax.numpy as jnp
from jax import lax
from jax.experimental import pallas as pl
from jax.experimental.pallas import tpu as pltpu
from jax.sharding import Mesh, PartitionSpec as P

BF = jnp.bfloat16
F32 = jnp.float32
HEAD = 128
QB = 128
BLOCK = 256
D = 2048
COLS = 768
MIB = 1024 * 1024
SETS = 0x66
HALVES = 0xB4


def ring(value, phase, step):
    pairs = []
    for y in range(4):
        for x in range(4):
            for core in range(2):
                at = (y, (x - step) % 4) if core == phase else ((y - step) % 4, x)
                pairs.append(((y * 4 + x) * 2 + core, (at[0] * 4 + at[1]) * 2 + core))
    return lax.ppermute(value, ("y", "x", "core"), pairs)


def swap(value, axis, size, mask):
    return lax.ppermute(value, axis, [(i, i ^ mask) for i in range(size)])


def same_set_neighbour(value):
    return lax.ppermute(value, "dp", [(z, (z + 1 if z % 2 else z - 1) % 8) for z in range(8)])


def same_set_far(value):
    return lax.ppermute(value, "dp", [(z, ((7 if SETS >> z & 1 else 3) - z) % 8) for z in range(8)])


def after(value, *others):
    return lax.optimization_barrier((value, *others))[0]


def dot(a, b, ca, cb):
    return lax.dot_general(a, b, (((ca,), (cb,)), ((), ())), preferred_element_type=F32)


def smem():
    return pl.BlockSpec(memory_space=pltpu.SMEM)


def vmem():
    return pl.BlockSpec(memory_space=pltpu.VMEM)


def call(kernel, args, n_smem, outs, scratch=(), grant=16, flops=0, nbytes=0):
    return pl.pallas_call(
        kernel,
        out_shape=[jax.ShapeDtypeStruct(*out) for out in outs],
        in_specs=[smem()] * n_smem + [vmem()] * (len(args) - n_smem),
        out_specs=[vmem()] * len(outs),
        scratch_shapes=list(scratch),
        compiler_params=pltpu.CompilerParams(vmem_limit_bytes=grant * MIB),
        cost_estimate=pl.CostEstimate(flops=flops, bytes_accessed=nbytes, transcendentals=0),
    )(*args)


def lanes(start):
    return pl.ds(pl.multiple_of(start, HEAD), HEAD)


def level_coef(pos, idx, table, blk, group, level, head):
    cs = blk // 2
    y, x, core = pos[0], pos[1], pos[2]
    row = idx[blk, group * 6 + level]
    lam = table[row, (core * 2 + pos[4]) * 2 + head]
    if level == 0:
        return lam * (1.0 / math.sqrt(HEAD * BLOCK))
    bit = [(core + cs) & 1, x & 1, (x >> 1) & 1, y & 1, (y >> 1) & 1][level - 1]
    return lam * bit.astype(F32) * (1.0 / math.sqrt(HEAD * 2 ** (level - 1) * BLOCK))


def prepare_kernel(pos, w, w_own, w_core):
    core, kind = pos[2], pos[4]
    mine = pl.multiple_of((core * 2 + kind) * 256, 256)
    other = pl.multiple_of(((1 - core) * 2 + kind) * 256, 256)
    for third in range(3):
        at = slice(third * 256, third * 256 + 256)
        w_own[:, at] = w[third, :, pl.ds(mine, 256)]
        w_core[:, at] = w[third, :, pl.ds(other, 256)]


def split_kernel(pos, cot, c_own, c_z):
    core, kind = pos[2], pos[4]
    for cs in range(2):
        for zs, out in enumerate((c_own, c_z)):
            group = ((core + cs) & 1) * 2 + ((kind + zs) & 1)
            out[cs] = cot[:, pl.ds(pl.multiple_of(group * 256, 256), 256)]


def project_kernel(pos, idx, table, *refs):
    toks = refs[0:4]
    c_own, c_z, c_core = refs[4:7]
    mine, ahead, behind, far_low, far_high = refs[7:12]
    qkv, cots, s1, x0, g1, m2, m3, m4, m5, w = refs[12:]
    y, x, core = pos[0], pos[1], pos[2]

    def place(part, first, slot, dist):
        yy = (y + dist + core * (slot - dist)) & 3
        xx = (x + slot + core * (dist - slot)) & 3
        for cs in range(2):
            row = pl.multiple_of((yy * 4 + xx) * 128 + ((core + cs) & 1) * 64, 64)
            w[pl.ds(row, 64), :] = part[first + cs * 64 : first + cs * 64 + 64, :]

    for slot in range(4):
        place(mine, slot * 128, slot, 0)
        place(ahead, slot * 128, slot, 1)
        place(behind, slot * 128, slot, 3)
        place((far_low, far_high)[slot // 2], (slot % 2) * 128, slot, 2)
    cots[0] = c_own[0]
    cots[1] = c_z[0]
    cots[2] = c_core[0]
    cots[3] = c_core[1]

    @pl.loop(0, 3)
    def _(part):
        cols = pl.ds(pl.multiple_of(part * 256, 256), 256)
        for blk in range(4):
            qkv[blk, :, cols] = dot(toks[blk][...], w[:, cols], 1, 0).astype(BF)

    @pl.loop(0, 4)
    def _(step):
        zs, h = step // 2, step % 2
        total = None
        sums = [None] * 4
        for cs in range(2):
            blk = cs * 2 + zs
            state = dot(qkv[blk, :, lanes(256 + h * HEAD)], qkv[blk, :, lanes(512 + h * HEAD)], 0, 0)
            s1[blk, h] = state.astype(BF)
            total = state if total is None else total + state
            first = None
            for g in range(2):
                rows = slice(g * QB, g * QB + QB)
                outer = dot(qkv[blk, rows, lanes(h * HEAD)], cots[blk, rows, lanes(h * HEAD)], 0, 0)
                term = outer * level_coef(pos, idx, table, cs * 2 + zs, g, 1, h)
                first = term if first is None else first + term
                for k in range(4):
                    term = outer * level_coef(pos, idx, table, blk, g, k + 2, h)
                    sums[k] = term if sums[k] is None else sums[k] + term
            g1[blk, h] = first
        x0[zs, h] = total.astype(BF)
        m2[zs, h] = sums[0]
        m3[zs, h] = sums[1]
        m4[zs, h] = sums[2].astype(BF)
        m5[zs, h] = sums[3].astype(BF)


def local_kernel(pos, idx, table, qkv, cots, loc):
    rows = lax.broadcasted_iota(jnp.int32, (BLOCK, BLOCK), 0)
    cols = lax.broadcasted_iota(jnp.int32, (BLOCK, BLOCK), 1)
    causal = rows >= cols
    upper = rows < QB

    @pl.loop(0, 8)
    def _(step):
        blk, h = step // 2, step % 2
        q = qkv[blk, :, lanes(h * HEAD)]
        k = qkv[blk, :, lanes(256 + h * HEAD)]
        v = qkv[blk, :, lanes(512 + h * HEAD)]
        c = cots[blk, :, lanes(h * HEAD)]
        scale = jnp.where(
            upper,
            level_coef(pos, idx, table, blk, 0, 0, h),
            level_coef(pos, idx, table, blk, 1, 0, h),
        )
        scale = jnp.where(causal, scale, 0.0)
        scores = (dot(q, k, 1, 1) * scale).astype(BF)
        dscores = (dot(c, v, 1, 1) * scale).astype(BF)
        loc[blk, :, lanes(h * HEAD)] = dot(dscores, k, 1, 0)
        loc[blk, :, lanes(256 + h * HEAD)] = dot(dscores, q, 0, 0)
        loc[blk, :, lanes(512 + h * HEAD)] = dot(scores, c, 0, 0)
        loc[blk, :, lanes(768 + h * HEAD)] = dot(scores, v, 1, 0)


def gradient_pair(pos, toks, grads, dist, first, store):
    y, x, core, half = pos[0], pos[1], pos[2], pos[5]
    at = []
    for slot in (first, first + 1):
        yy = (y + dist + core * (slot - dist)) & 3
        xx = (x + slot + core * (dist - slot)) & 3
        at.append(lanes((yy * 4 + xx) * 128))
    part = None
    for blk in range(4):
        rows = jnp.concatenate([toks[blk][:, at[0]], toks[blk][:, at[1]]], axis=1)
        term = dot(rows, grads[blk], 0, 0)
        part = term if part is None else part + term
    part = part.astype(BF)
    for sub in range(2):
        for c in range(2):
            for piece in range(2):
                row = ((c + core) & 1) * 64 + ((piece + half) & 1) * 32
                start = sub * 128 + c * 64 + piece * 32
                store(sub, pl.ds(pl.multiple_of(row, 32), 32), part[start : start + 32])


def finish_kernel(pos, idx, table, *refs):
    toks = refs[0:4]
    cots, qkv, loc, s1, g1 = refs[4:9]
    cx1, cx2, cx3, cy1, cy2, cy3 = refs[9:15]
    own, r1, r2, r3 = refs[15:19]
    attn, grads, low, high = refs[19:]

    @pl.loop(0, 4)
    def _(step):
        zs, h = step // 2, step % 2
        far = [
            None,
            cx1[zs, h].astype(F32),
            cx2[zs, h].astype(F32) + cx3[zs, h].astype(F32),
            cy1[zs, h].astype(F32),
            cy2[zs, h].astype(F32) + cy3[zs, h].astype(F32),
        ]
        chip = own[zs, h].astype(F32) + r1[zs, h].astype(F32)
        chip = chip + r2[zs, h].astype(F32) + r3[zs, h].astype(F32)
        qs, ks = lanes(h * HEAD), lanes(256 + h * HEAD)
        vs, ats = lanes(512 + h * HEAD), lanes(768 + h * HEAD)
        for cs in range(2):
            blk = cs * 2 + zs
            other = (1 - cs) * 2 + zs
            far[0] = s1[other, h].astype(F32)
            grad = (chip + g1[other, h]).astype(BF)
            for g in range(2):
                rows = slice(g * QB, g * QB + QB)
                mixed = None
                for level in range(1, 6):
                    term = far[level - 1] * level_coef(pos, idx, table, blk, g, level, h)
                    mixed = term if mixed is None else mixed + term
                mixed = mixed.astype(BF)
                out = loc[blk, rows, ats] + dot(qkv[blk, rows, qs], mixed, 1, 0)
                attn[blk, rows, qs] = out.astype(BF)
                dq = loc[blk, rows, qs] + dot(cots[blk, rows, qs], mixed, 1, 1)
                grads[blk, rows, qs] = dq.astype(BF)
            dk = loc[blk, :, ks] + dot(qkv[blk, :, vs], grad, 1, 1)
            grads[blk, :, ks] = dk.astype(BF)
            dv = loc[blk, :, vs] + dot(qkv[blk, :, ks], grad, 1, 0)
            grads[blk, :, vs] = dv.astype(BF)

    for first, out in ((0, low), (2, high)):

        def store(sub, rows, value, out=out):
            out[sub, rows, :] = value

        gradient_pair(pos, toks, grads, 2, first, store)


def gradient_kernel(pos, t0, t1, t2, t3, grads, own, onward, backward):
    toks = (t0, t1, t2, t3)

    @pl.loop(0, 2)
    def _(pair):
        for dist, out in ((1, onward), (3, backward), (0, own)):

            def store(sub, rows, value, out=out):
                out[pair * 2 + sub, rows, :] = value

            gradient_pair(pos, toks, grads, dist, pair * 2, store)


def place_kernel(pos, own, from_core, from_z, mine, near, theirs, attn_out, grad_w):
    core, kind = pos[2], pos[4]
    attns = ((own, from_z.at[0]), (from_core.at[0], from_z.at[1]))
    halves = (pos[5], pos[6])
    for cs in range(2):
        for zs in range(2):
            group = ((core + cs) & 1) * 2 + ((kind + zs) & 1)
            lane = pl.ds(pl.multiple_of(group * 256, 256), 256)
            attn_out[:, lane] = attns[cs][zs][0] if zs == 0 and cs == 0 else attns[cs][zs][...]
            for piece in range(2):
                part = (mine, near)[piece] if zs == 0 else theirs.at[piece]
                row = pl.ds(pl.multiple_of(((halves[zs] + piece) & 1) * 32, 32), 32)
                for third in range(3):
                    grad_w[third, row, lane] = part[
                        cs, :, third * 256 : third * 256 + 256
                    ].astype(F32)


def add(*parts):
    total = parts[0].astype(F32)
    for part in parts[1:]:
        total = total + part.astype(F32)
    return total.astype(BF)


def per_device(tokens, w_qkv, weight_table, weight_index, cotangent):
    y, x, core = lax.axis_index("y"), lax.axis_index("x"), lax.axis_index("core")
    z = lax.axis_index("dp")
    pos = jnp.stack(
        [y, x, core, z, (SETS >> z) & 1, (HALVES >> z) & 1, (HALVES >> (z ^ 1)) & 1]
    ).astype(jnp.int32)
    inputs = tokens[0]

    rows = weight_index.reshape(1, 12)
    rows = jnp.concatenate([rows, swap(rows, "dp", 8, 1)], axis=0)
    idx = jnp.concatenate([rows, swap(rows, "core", 2, 1)], axis=0)
    scalars = [pos, idx, weight_table]

    w_own, w_core = call(
        prepare_kernel,
        [pos, jnp.transpose(w_qkv, (1, 0, 2))],
        1,
        [((64, COLS), BF), ((64, COLS), BF)],
        grant=48,
        nbytes=MIB,
    )

    chunk = jnp.concatenate([w_own, swap(w_core, "core", 2, 1)], axis=0)
    mine = jnp.concatenate([chunk] + [ring(chunk, 0, step) for step in (1, 2, 3)], axis=0)
    ahead, behind = ring(mine, 1, 1), ring(mine, 1, 3)
    far_low, far_high = ring(behind[:256], 1, 3), ring(ahead[256:], 1, 1)

    tok01 = swap(inputs, "dp", 8, 1)
    c_own, c_z = call(
        split_kernel,
        [pos, after(cotangent[0], chunk)],
        1,
        [((2, BLOCK, 256), BF), ((2, BLOCK, 256), BF)],
        grant=48,
        nbytes=MIB,
    )
    from_z = swap(c_z, "dp", 8, 1)
    tok10 = swap(after(inputs, mine), "core", 2, 1)
    tok11 = swap(after(tok01, behind), "core", 2, 1)
    to_core = jnp.stack([c_own[1], after(from_z, behind)[1]], axis=0)
    c_core = swap(to_core, "core", 2, 1)
    toks = [inputs, tok01, tok10, tok11]

    square = (2, 2, HEAD, HEAD)
    wide = (4, 2, HEAD, HEAD)
    qkv, cots, s1, x0, g1, m2, m3, m4, m5 = call(
        project_kernel,
        scalars + toks + [c_own, from_z, c_core, mine, ahead, behind, far_low, far_high],
        3,
        [
            ((4, BLOCK, COLS), BF),
            ((4, BLOCK, 256), BF),
            (wide, BF),
            (square, BF),
            (wide, F32),
            (square, F32),
            (square, F32),
            (square, BF),
            (square, BF),
        ],
        scratch=[pltpu.VMEM((D, COLS), BF)],
        grant=48,
        flops=2 * 1024 * D * COLS,
        nbytes=10 * MIB,
    )

    cx = [swap(x0, "x", 4, mask) for mask in (1, 2, 3)]
    dy = [swap(m, "y", 4, mask) for mask, m in ((1, m4), (2, m5), (3, m5))]
    (loc,) = call(
        local_kernel,
        scalars + [qkv, cots],
        3,
        [((4, BLOCK, 1024), F32)],
        grant=12,
        flops=8 * 6 * 2 * BLOCK * BLOCK * HEAD,
        nbytes=8 * MIB,
    )
    x1 = add(x0, *cx)
    cy = [swap(x1, "y", 4, mask) for mask in (1, 2, 3)]
    high = dy[0].astype(F32) + dy[1].astype(F32) + dy[2].astype(F32)
    near = (high + m2).astype(BF)
    far = (high + m3).astype(BF)
    dx = [swap(m, "x", 4, mask) for mask, m in ((1, near), (2, far), (3, far))]

    attn, grads, low, high = call(
        finish_kernel,
        scalars + toks + [cots, qkv, loc, s1, g1] + cx + cy + [high.astype(BF)] + dx,
        3,
        [
            ((4, BLOCK, 256), BF),
            ((4, BLOCK, COLS), BF),
            ((2, 128, COLS), BF),
            ((2, 128, COLS), BF),
        ],
        grant=24,
        flops=1024 * D * COLS,
        nbytes=12 * MIB,
    )
    low, high = ring(low, 1, 3), ring(high, 1, 1)
    own, onward, backward = call(
        gradient_kernel,
        [pos] + toks + [grads],
        1,
        [((4, 128, COLS), BF)] * 3,
        grant=24,
        flops=2 * 1024 * D * COLS,
        nbytes=9 * MIB,
    )
    onward = jnp.concatenate([add(onward[:2], low), onward[2:]], axis=0)
    backward = jnp.concatenate([backward[:2], add(backward[2:], high)], axis=0)
    from_core = swap(attn[2:], "core", 2, 1)
    total = add(own, ring(onward, 1, 3), ring(backward, 1, 1))
    back = swap(jnp.stack([attn[1], from_core[1]], axis=0), "dp", 8, 1)
    chip_sum = add(total[0], *[ring(total[step], 0, -step) for step in (1, 2, 3)])
    pair = jnp.stack([chip_sum[:64], swap(chip_sum[64:], "core", 2, 1)], axis=0)
    mine = add(pair[:, :32], same_set_neighbour(pair[:, 32:]))
    mine = add(mine, same_set_far(mine))
    near = same_set_neighbour(mine)
    theirs = swap(jnp.stack([mine, near], axis=0), "dp", 8, 1)

    attn_out, grad_w = call(
        place_kernel,
        [pos, attn, from_core, back, mine, near, theirs],
        1,
        [((BLOCK, 1024), BF), ((3, 64, 1024), F32)],
        grant=6,
        nbytes=3 * MIB,
    )
    return attn_out[None], jnp.transpose(grad_w, (1, 0, 2))


def solution(mesh):
    grid = Mesh(mesh.devices.reshape(4, 4, 2, 8), ("y", "x", "core", "dp"))
    seq = ("y", "x", "core")
    return jax.shard_map(
        per_device,
        mesh=grid,
        in_specs=(P("dp", seq, None), P(seq, None, None), P(), P("dp", seq, None), P("dp", seq, None)),
        out_specs=(P("dp", seq, None), P(seq, None, None)),
        check_vma=False,
    )
```

```python
import functools
import math

import jax
import jax.numpy as jnp
from jax import lax
from jax.experimental import pallas as pl
from jax.experimental.pallas import tpu as pltpu
from jax.sharding import Mesh, PartitionSpec as P

BF = jnp.bfloat16
F32 = jnp.float32
HEAD = 128
QB = 128
BLOCK = 256
D = 2048
COLS = 768
MIB = 1024 * 1024
SETS = 0x66
HALVES = 0xB4


def ring(value, phase, step):
    pairs = []
    for y in range(4):
        for x in range(4):
            for core in range(2):
                at = (y, (x - step) % 4) if core == phase else ((y - step) % 4, x)
                pairs.append(((y * 4 + x) * 2 + core, (at[0] * 4 + at[1]) * 2 + core))
    return lax.ppermute(value, ("y", "x", "core"), pairs)


def swap(value, axis, size, mask):
    return lax.ppermute(value, axis, [(i, i ^ mask) for i in range(size)])


def same_set_neighbour(value):
    return lax.ppermute(value, "dp", [(z, (z + 1 if z % 2 else z - 1) % 8) for z in range(8)])


def same_set_far(value):
    return lax.ppermute(value, "dp", [(z, ((7 if SETS >> z & 1 else 3) - z) % 8) for z in range(8)])


def after(value, *others):
    return lax.optimization_barrier((value, *others))[0]


def hold(value, *others):
    anywhere = pl.BlockSpec(memory_space=pl.ANY)
    return pl.pallas_call(
        lambda *refs: None,
        out_shape=jax.ShapeDtypeStruct(value.shape, value.dtype),
        in_specs=[anywhere] * (1 + len(others)),
        out_specs=anywhere,
        input_output_aliases={0: 0},
    )(value, *others)


def dot(a, b, ca, cb):
    return lax.dot_general(a, b, (((ca,), (cb,)), ((), ())), preferred_element_type=F32)


def smem():
    return pl.BlockSpec(memory_space=pltpu.SMEM)


def vmem():
    return pl.BlockSpec(memory_space=pltpu.VMEM)


def call(kernel, args, n_smem, outs, scratch=(), grant=16, flops=0, nbytes=0, n_any=0):
    return pl.pallas_call(
        kernel,
        out_shape=[jax.ShapeDtypeStruct(*out) for out in outs],
        in_specs=[smem()] * n_smem
        + [vmem()] * (len(args) - n_smem - n_any)
        + [pl.BlockSpec(memory_space=pl.ANY)] * n_any,
        out_specs=[vmem()] * len(outs),
        scratch_shapes=list(scratch),
        compiler_params=pltpu.CompilerParams(vmem_limit_bytes=grant * MIB),
        cost_estimate=pl.CostEstimate(flops=flops, bytes_accessed=nbytes, transcendentals=0),
    )(*args)


def lanes(start):
    return pl.ds(pl.multiple_of(start, HEAD), HEAD)


def level_coef(pos, idx, table, blk, group, level, head):
    cs = blk // 2
    y, x, core = pos[0], pos[1], pos[2]
    row = idx[blk, group * 6 + level]
    lam = table[row, (core * 2 + pos[4]) * 2 + head]
    if level == 0:
        return lam * (1.0 / math.sqrt(HEAD * BLOCK))
    bit = [(core + cs) & 1, x & 1, (x >> 1) & 1, y & 1, (y >> 1) & 1][level - 1]
    return lam * bit.astype(F32) * (1.0 / math.sqrt(HEAD * 2 ** (level - 1) * BLOCK))


def prepare_kernel(pos, w, w_own, w_core, sems):
    core, kind = pos[2], pos[4]
    copies = []
    for n, out in enumerate((w_core, w_own)):
        group = ((1 - core if n == 0 else core) * 2 + kind) * 256
        for third in range(3):
            src = w.at[third, :, pl.ds(pl.multiple_of(group, 256), 256)]
            dst = out.at[:, pl.ds(third * 256, 256)]
            copies.append(pltpu.make_async_copy(src, dst, sems.at[n * 3 + third]))
    for copy in copies:
        copy.start()
    for copy in copies:
        copy.wait()


def split_kernel(pos, cot, c_own, c_z):
    core, kind = pos[2], pos[4]
    for cs in range(2):
        for zs, out in enumerate((c_own, c_z)):
            group = ((core + cs) & 1) * 2 + ((kind + zs) & 1)
            out[cs] = cot[:, pl.ds(pl.multiple_of(group * 256, 256), 256)]


def project_kernel(pos, idx, table, *refs):
    c_own, c_z, c_core = refs[4:7]
    parts = (refs[7:9], refs[9:11], refs[13:15], refs[11:13])
    qkv, cots, s1, x0, g1, m2, m3, m4, m5, w, toks, sems = refs[15:]
    y, x, core = pos[0], pos[1], pos[2]
    copies = []

    def bring(src, dst):
        copies.append(pltpu.make_async_copy(src, dst, sems.at[len(copies)]))
        copies[-1].start()

    for slot in range(4):
        for dist in range(4):
            yy = (y + dist + core * (slot - dist)) & 3
            xx = (x + slot + core * (dist - slot)) & 3
            for cs in range(2):
                row = pl.multiple_of((yy * 4 + xx) * 128 + ((core + cs) & 1) * 64, 64)
                start = (slot % 2) * 128 + cs * 64
                bring(parts[dist][slot // 2].at[pl.ds(start, 64)], w.at[pl.ds(row, 64)])
    for blk in range(4):
        bring(refs[blk], toks.at[blk])
    for blk, src in enumerate((c_own.at[0], c_z.at[0], c_core.at[0], c_core.at[1])):
        bring(src, cots.at[blk])
    for copy in copies:
        copy.wait()

    @pl.loop(0, 3)
    def _(part):
        cols = pl.ds(pl.multiple_of(part * 256, 256), 256)
        for blk in range(4):
            qkv[blk, :, cols] = dot(toks[blk], w[:, cols], 1, 0).astype(BF)

    @pl.loop(0, 4)
    def _(step):
        zs, h = step // 2, step % 2
        total = None
        sums = [None] * 4
        for cs in range(2):
            blk = cs * 2 + zs
            state = dot(qkv[blk, :, lanes(256 + h * HEAD)], qkv[blk, :, lanes(512 + h * HEAD)], 0, 0)
            s1[blk, h] = state.astype(BF)
            total = state if total is None else total + state
            first = None
            for g in range(2):
                rows = slice(g * QB, g * QB + QB)
                outer = dot(qkv[blk, rows, lanes(h * HEAD)], cots[blk, rows, lanes(h * HEAD)], 0, 0)
                term = outer * level_coef(pos, idx, table, cs * 2 + zs, g, 1, h)
                first = term if first is None else first + term
                for k in range(4):
                    term = outer * level_coef(pos, idx, table, blk, g, k + 2, h)
                    sums[k] = term if sums[k] is None else sums[k] + term
            g1[blk, h] = first
        x0[zs, h] = total.astype(BF)
        m2[zs, h] = sums[0]
        m3[zs, h] = sums[1]
        m4[zs, h] = sums[2].astype(BF)
        m5[zs, h] = sums[3].astype(BF)


def local_kernel(pos, idx, table, qkv, cots, loc):
    rows = lax.broadcasted_iota(jnp.int32, (BLOCK, BLOCK), 0)
    cols = lax.broadcasted_iota(jnp.int32, (BLOCK, BLOCK), 1)
    causal = rows >= cols
    upper = rows < QB

    @pl.loop(0, 8)
    def _(step):
        blk, h = step // 2, step % 2
        q = qkv[blk, :, lanes(h * HEAD)]
        k = qkv[blk, :, lanes(256 + h * HEAD)]
        v = qkv[blk, :, lanes(512 + h * HEAD)]
        c = cots[blk, :, lanes(h * HEAD)]
        scale = jnp.where(
            upper,
            level_coef(pos, idx, table, blk, 0, 0, h),
            level_coef(pos, idx, table, blk, 1, 0, h),
        )
        scale = jnp.where(causal, scale, 0.0)
        scores = (dot(q, k, 1, 1) * scale).astype(BF)
        dscores = (dot(c, v, 1, 1) * scale).astype(BF)
        loc[blk, :, lanes(h * HEAD)] = dot(dscores, k, 1, 0)
        loc[blk, :, lanes(256 + h * HEAD)] = dot(dscores, q, 0, 0)
        loc[blk, :, lanes(512 + h * HEAD)] = dot(scores, c, 0, 0)
        loc[blk, :, lanes(768 + h * HEAD)] = dot(scores, v, 1, 0)


def gradient_pair(pos, toks, grads, dist, first, store):
    y, x, core, half = pos[0], pos[1], pos[2], pos[5]
    at = []
    for slot in (first, first + 1):
        yy = (y + dist + core * (slot - dist)) & 3
        xx = (x + slot + core * (dist - slot)) & 3
        at.append(lanes((yy * 4 + xx) * 128))
    part = None
    for blk in range(4):
        rows = jnp.concatenate([toks[blk][:, at[0]], toks[blk][:, at[1]]], axis=1)
        term = dot(rows, grads[blk], 0, 0)
        part = term if part is None else part + term
    part = part.astype(BF)
    for sub in range(2):
        for c in range(2):
            for piece in range(2):
                row = ((c + core) & 1) * 64 + ((piece + half) & 1) * 32
                start = sub * 128 + c * 64 + piece * 32
                store(sub, pl.ds(pl.multiple_of(row, 32), 32), part[start : start + 32])


def finish_kernel(pos, idx, table, *refs):
    toks = refs[0:4]
    cots, qkv, loc, s1, g1 = refs[4:9]
    cx1, cx2, cx3, cy1, cy2, cy3 = refs[9:15]
    own, r1, r2, r3 = refs[15:19]
    attn, grads, low, high = refs[19:]

    @pl.loop(0, 4)
    def _(step):
        zs, h = step // 2, step % 2
        far = [
            None,
            cx1[zs, h].astype(F32),
            cx2[zs, h].astype(F32) + cx3[zs, h].astype(F32),
            cy1[zs, h].astype(F32),
            cy2[zs, h].astype(F32) + cy3[zs, h].astype(F32),
        ]
        chip = own[zs, h].astype(F32) + r1[zs, h].astype(F32)
        chip = chip + r2[zs, h].astype(F32) + r3[zs, h].astype(F32)
        qs, ks = lanes(h * HEAD), lanes(256 + h * HEAD)
        vs, ats = lanes(512 + h * HEAD), lanes(768 + h * HEAD)
        for cs in range(2):
            blk = cs * 2 + zs
            other = (1 - cs) * 2 + zs
            far[0] = s1[other, h].astype(F32)
            grad = (chip + g1[other, h]).astype(BF)
            for g in range(2):
                rows = slice(g * QB, g * QB + QB)
                mixed = None
                for level in range(1, 6):
                    term = far[level - 1] * level_coef(pos, idx, table, blk, g, level, h)
                    mixed = term if mixed is None else mixed + term
                mixed = mixed.astype(BF)
                out = loc[blk, rows, ats] + dot(qkv[blk, rows, qs], mixed, 1, 0)
                attn[blk, rows, qs] = out.astype(BF)
                dq = loc[blk, rows, qs] + dot(cots[blk, rows, qs], mixed, 1, 1)
                grads[blk, rows, qs] = dq.astype(BF)
            dk = loc[blk, :, ks] + dot(qkv[blk, :, vs], grad, 1, 1)
            grads[blk, :, ks] = dk.astype(BF)
            dv = loc[blk, :, vs] + dot(qkv[blk, :, ks], grad, 1, 0)
            grads[blk, :, vs] = dv.astype(BF)

    for first, out in ((0, low), (2, high)):

        def store(sub, rows, value, out=out):
            out[sub, rows, :] = value

        gradient_pair(pos, toks, grads, 2, first, store)


def gradient_kernel(dists, pos, t0, t1, t2, t3, grads, _, *outs):
    toks = (t0, t1, t2, t3)

    @pl.loop(0, 2)
    def _(pair):
        for dist, out in zip(dists, outs):

            def store(sub, rows, value, out=out):
                out[pair * 2 + sub, rows, :] = value

            gradient_pair(pos, toks, grads, dist, pair * 2, store)


def total_kernel(pos, own, r1, r2, attn, from_core, from_z, t0, t1, t2, t3, attn_out):
    core, kind = pos[2], pos[4]
    for slot, out in enumerate((t0, t1, t2, t3)):
        total = own[slot].astype(F32) + r1[slot].astype(F32) + r2[slot].astype(F32)
        out[...] = total.astype(BF)
    attns = ((attn.at[0], from_z.at[0]), (from_core.at[0], from_z.at[1]))
    for cs in range(2):
        for zs in range(2):
            group = ((core + cs) & 1) * 2 + ((kind + zs) & 1)
            attn_out[:, pl.ds(pl.multiple_of(group * 256, 256), 256)] = attns[cs][zs][...]


def place_kernel(pos, mine, near, theirs, grad_w):
    core, kind = pos[2], pos[4]
    halves = (pos[5], pos[6])
    for cs in range(2):
        for zs in range(2):
            group = ((core + cs) & 1) * 2 + ((kind + zs) & 1)
            lane = pl.ds(pl.multiple_of(group * 256, 256), 256)
            for piece in range(2):
                part = (mine, near)[piece] if zs == 0 else theirs.at[piece]
                row = pl.ds(pl.multiple_of(((halves[zs] + piece) & 1) * 32, 32), 32)
                for third in range(3):
                    grad_w[third, row, lane] = part[
                        cs, :, third * 256 : third * 256 + 256
                    ].astype(F32)


def add(*parts):
    total = parts[0].astype(F32)
    for part in parts[1:]:
        total = total + part.astype(F32)
    return total.astype(BF)


def per_device(tokens, w_qkv, weight_table, weight_index, cotangent):
    y, x, core = lax.axis_index("y"), lax.axis_index("x"), lax.axis_index("core")
    z = lax.axis_index("dp")
    pos = jnp.stack(
        [y, x, core, z, (SETS >> z) & 1, (HALVES >> z) & 1, (HALVES >> (z ^ 1)) & 1]
    ).astype(jnp.int32)
    inputs = tokens[0]

    rows = weight_index.reshape(1, 12)
    rows = jnp.concatenate([rows, swap(rows, "dp", 8, 1)], axis=0)
    idx = jnp.concatenate([rows, swap(rows, "core", 2, 1)], axis=0)
    scalars = [pos, idx, weight_table]

    w_own, w_core = call(
        prepare_kernel,
        [pos, jnp.transpose(w_qkv, (1, 0, 2))],
        1,
        [((64, COLS), BF), ((64, COLS), BF)],
        scratch=[pltpu.SemaphoreType.DMA((6,))],
        grant=48,
        nbytes=MIB,
        n_any=1,
    )

    chunk = jnp.concatenate([w_own, swap(w_core, "core", 2, 1)], axis=0)
    near = [chunk] + [ring(chunk, 0, step) for step in (1, 2, 3)]
    mine = [jnp.concatenate(near[:2], axis=0), jnp.concatenate(near[2:], axis=0)]
    ahead = [ring(part, 1, 1) for part in mine]
    behind = [ring(part, 1, 3) for part in mine]
    far = [ring(behind[0], 1, 3), ring(ahead[1], 1, 1)]

    tok01 = hold(swap(inputs, "dp", 8, 1), *far)
    c_own, c_z = call(
        split_kernel,
        [pos, after(cotangent[0], chunk)],
        1,
        [((2, BLOCK, 256), BF), ((2, BLOCK, 256), BF)],
        grant=48,
        nbytes=MIB,
    )
    from_z = swap(c_z, "dp", 8, 1)
    tok10 = swap(after(inputs, *mine), "core", 2, 1)
    tok11 = swap(tok01, "core", 2, 1)
    to_core = jnp.stack([c_own[1], from_z[1]], axis=0)
    c_core = swap(to_core, "core", 2, 1)
    toks = [inputs, tok01, tok10, tok11]

    square = (2, 2, HEAD, HEAD)
    wide = (4, 2, HEAD, HEAD)
    qkv, cots, s1, x0, g1, m2, m3, m4, m5 = call(
        project_kernel,
        scalars + toks + [c_own, from_z, c_core] + mine + ahead + behind + far,
        3,
        [
            ((4, BLOCK, COLS), BF),
            ((4, BLOCK, 256), BF),
            (wide, BF),
            (square, BF),
            (wide, F32),
            (square, F32),
            (square, F32),
            (square, BF),
            (square, BF),
        ],
        scratch=[
            pltpu.VMEM((D, COLS), BF),
            pltpu.VMEM((4, BLOCK, D), BF),
            pltpu.SemaphoreType.DMA((40,)),
        ],
        grant=52,
        flops=2 * 1024 * D * COLS,
        nbytes=10 * MIB,
        n_any=15,
    )

    cx = [swap(x0, "x", 4, mask) for mask in (1, 2, 3)]
    dy = [swap(m, "y", 4, mask) for mask, m in ((1, m4), (2, m5), (3, m5))]
    (loc,) = call(
        local_kernel,
        scalars + [qkv, cots],
        3,
        [((4, BLOCK, 1024), F32)],
        grant=12,
        flops=8 * 6 * 2 * BLOCK * BLOCK * HEAD,
        nbytes=8 * MIB,
    )
    x1 = add(x0, *cx)
    cy = [swap(x1, "y", 4, mask) for mask in (1, 2, 3)]
    high = dy[0].astype(F32) + dy[1].astype(F32) + dy[2].astype(F32)
    near = (high + m2).astype(BF)
    far = (high + m3).astype(BF)
    dx = [swap(m, "x", 4, mask) for mask, m in ((1, near), (2, far), (3, far))]

    attn, grads, low, high = call(
        finish_kernel,
        scalars + toks + [cots, qkv, loc, s1, g1] + cx + cy + [high.astype(BF)] + dx,
        3,
        [
            ((4, BLOCK, 256), BF),
            ((4, BLOCK, COLS), BF),
            ((2, 128, COLS), BF),
            ((2, 128, COLS), BF),
        ],
        grant=24,
        flops=1024 * D * COLS,
        nbytes=12 * MIB,
    )
    low, high = ring(low, 1, 3), ring(high, 1, 1)
    from_core = swap(attn[2:], "core", 2, 1)
    onward, backward = call(
        functools.partial(gradient_kernel, (1, 3)),
        [pos] + toks + [grads, from_core],
        1,
        [((4, 128, COLS), BF)] * 2,
        grant=20,
        flops=1024 * D * COLS,
        nbytes=9 * MIB,
        n_any=1,
    )
    onward = jnp.concatenate([add(onward[:2], low), onward[2:]], axis=0)
    backward = jnp.concatenate([backward[:2], add(backward[2:], high)], axis=0)
    onward, backward = ring(onward, 1, 3), ring(backward, 1, 1)
    back = swap(jnp.stack([attn[1], from_core[1]], axis=0), "dp", 8, 1)
    (own,) = call(
        functools.partial(gradient_kernel, (0,)),
        [pos] + toks + [grads, from_core],
        1,
        [((4, 128, COLS), BF)],
        grant=20,
        flops=1024 * 512 * COLS,
        nbytes=9 * MIB,
        n_any=1,
    )
    *total, attn_out = call(
        total_kernel,
        [pos, own, onward, backward, attn, from_core, back],
        1,
        [((128, COLS), BF)] * 4 + [((BLOCK, 1024), BF)],
        grant=10,
        nbytes=4 * MIB,
    )
    chip_sum = add(total[0], *[ring(total[step], 0, -step) for step in (1, 2, 3)])
    pair = jnp.stack([chip_sum[:64], swap(chip_sum[64:], "core", 2, 1)], axis=0)
    mine = add(pair[:, :32], same_set_neighbour(pair[:, 32:]))
    mine = add(mine, same_set_far(mine))
    near = same_set_neighbour(mine)
    theirs = swap(jnp.stack([mine, near], axis=0), "dp", 8, 1)

    (grad_w,) = call(
        place_kernel,
        [pos, mine, near, theirs],
        1,
        [((3, 64, 1024), F32)],
        grant=6,
        nbytes=3 * MIB,
    )
    return attn_out[None], jnp.transpose(grad_w, (1, 0, 2))


def solution(mesh):
    grid = Mesh(mesh.devices.reshape(4, 4, 2, 8), ("y", "x", "core", "dp"))
    seq = ("y", "x", "core")
    return jax.shard_map(
        per_device,
        mesh=grid,
        in_specs=(P("dp", seq, None), P(seq, None, None), P(), P("dp", seq, None), P("dp", seq, None)),
        out_specs=(P("dp", seq, None), P(seq, None, None)),
        check_vma=False,
    )
```

```python
import functools
import math

import jax
import jax.numpy as jnp
from jax import lax
from jax.experimental import pallas as pl
from jax.experimental.pallas import tpu as pltpu
from jax.sharding import Mesh, PartitionSpec as P

BF = jnp.bfloat16
F32 = jnp.float32
HEAD = 128
QB = 128
BLOCK = 256
D = 2048
COLS = 768
MIB = 1024 * 1024
SETS = 0x66
HALVES = 0xB4


def ring(value, phase, step):
    pairs = []
    for y in range(4):
        for x in range(4):
            for core in range(2):
                at = (y, (x - step) % 4) if core == phase else ((y - step) % 4, x)
                pairs.append(((y * 4 + x) * 2 + core, (at[0] * 4 + at[1]) * 2 + core))
    return lax.ppermute(value, ("y", "x", "core"), pairs)


def swap(value, axis, size, mask):
    return lax.ppermute(value, axis, [(i, i ^ mask) for i in range(size)])


def same_set_neighbour(value):
    return lax.ppermute(value, "dp", [(z, (z + 1 if z % 2 else z - 1) % 8) for z in range(8)])


def same_set_far(value):
    return lax.ppermute(value, "dp", [(z, ((7 if SETS >> z & 1 else 3) - z) % 8) for z in range(8)])


def after(value, *others):
    return lax.optimization_barrier((value, *others))[0]


def hold(value, *others):
    anywhere = pl.BlockSpec(memory_space=pl.ANY)
    return pl.pallas_call(
        lambda *refs: None,
        out_shape=jax.ShapeDtypeStruct(value.shape, value.dtype),
        in_specs=[anywhere] * (1 + len(others)),
        out_specs=anywhere,
        input_output_aliases={0: 0},
    )(value, *others)


def dot(a, b, ca, cb):
    return lax.dot_general(a, b, (((ca,), (cb,)), ((), ())), preferred_element_type=F32)


def smem():
    return pl.BlockSpec(memory_space=pltpu.SMEM)


def vmem():
    return pl.BlockSpec(memory_space=pltpu.VMEM)


def call(kernel, args, n_smem, outs, scratch=(), grant=16, flops=0, nbytes=0, n_any=0, outs_any=False):
    return pl.pallas_call(
        kernel,
        out_shape=[jax.ShapeDtypeStruct(*out) for out in outs],
        in_specs=[smem()] * n_smem
        + [vmem()] * (len(args) - n_smem - n_any)
        + [pl.BlockSpec(memory_space=pl.ANY)] * n_any,
        out_specs=[pl.BlockSpec(memory_space=pl.ANY) if outs_any else vmem()] * len(outs),
        scratch_shapes=list(scratch),
        compiler_params=pltpu.CompilerParams(vmem_limit_bytes=grant * MIB),
        cost_estimate=pl.CostEstimate(flops=flops, bytes_accessed=nbytes, transcendentals=0),
    )(*args)


def lanes(start):
    return pl.ds(pl.multiple_of(start, HEAD), HEAD)


def level_coef(pos, idx, table, blk, group, level, head):
    cs = blk // 2
    y, x, core = pos[0], pos[1], pos[2]
    row = idx[blk, group * 6 + level]
    lam = table[row, (core * 2 + pos[4]) * 2 + head]
    if level == 0:
        return lam * (1.0 / math.sqrt(HEAD * BLOCK))
    bit = [(core + cs) & 1, x & 1, (x >> 1) & 1, y & 1, (y >> 1) & 1][level - 1]
    return lam * bit.astype(F32) * (1.0 / math.sqrt(HEAD * 2 ** (level - 1) * BLOCK))


def prepare_kernel(pos, w, tok, cot, w_own, w_core, to_z, c_own, c_core, sems):
    core, kind = pos[2], pos[4]
    copies = []

    def columns(cs, zs):
        group = ((core + cs) & 1) * 2 + ((kind + zs) & 1)
        return pl.ds(pl.multiple_of(group * 256, 256), 256)

    def bring(src, dst):
        copies.append(pltpu.make_async_copy(src, dst, sems.at[len(copies)]))
        copies[-1].start()

    bring(tok, to_z.at[:, pl.ds(0, D)])
    for cs, out in ((1, w_core), (0, w_own)):
        for third in range(3):
            bring(w.at[third, :, columns(cs, 0)], out.at[:, pl.ds(third * 256, 256)])
    for cs, out in enumerate((c_own, c_core)):
        bring(cot.at[:, columns(cs, 0)], out)
        bring(cot.at[:, columns(cs, 1)], to_z.at[:, pl.ds(D + cs * 256, 256)])
    for copy in copies:
        copy.wait()


def project_kernel(pos, idx, table, *refs):
    c_own, c_core = refs[4:6]
    parts = (refs[6:8], refs[8:10], refs[12:14], refs[10:12])
    qkv, cots, s1, x0, g1, m2, m3, m4, m5, w, toks, sems = refs[14:]
    y, x, core = pos[0], pos[1], pos[2]
    copies = []

    def bring(src, dst):
        copies.append(pltpu.make_async_copy(src, dst, sems.at[len(copies)]))
        copies[-1].start()

    for slot in range(4):
        for dist in range(4):
            yy = (y + dist + core * (slot - dist)) & 3
            xx = (x + slot + core * (dist - slot)) & 3
            for cs in range(2):
                row = pl.multiple_of((yy * 4 + xx) * 128 + ((core + cs) & 1) * 64, 64)
                start = (slot % 2) * 128 + cs * 64
                bring(parts[dist][slot // 2].at[pl.ds(start, 64)], w.at[pl.ds(row, 64)])
    for blk in range(4):
        bring(refs[blk].at[:, pl.ds(0, D)], toks.at[blk])
    near, across = refs[1].at[:, pl.ds(D, 256)], refs[3].at[:, pl.ds(D + 256, 256)]
    for blk, src in enumerate((c_own, near, c_core, across)):
        bring(src, cots.at[blk])
    for copy in copies:
        copy.wait()

    @pl.loop(0, 3)
    def _(part):
        cols = pl.ds(pl.multiple_of(part * 256, 256), 256)
        for blk in range(4):
            qkv[blk, :, cols] = dot(toks[blk], w[:, cols], 1, 0).astype(BF)

    @pl.loop(0, 4)
    def _(step):
        zs, h = step // 2, step % 2
        total = None
        sums = [None] * 4
        for cs in range(2):
            blk = cs * 2 + zs
            state = dot(qkv[blk, :, lanes(256 + h * HEAD)], qkv[blk, :, lanes(512 + h * HEAD)], 0, 0)
            s1[blk, h] = state.astype(BF)
            total = state if total is None else total + state
            first = None
            for g in range(2):
                rows = slice(g * QB, g * QB + QB)
                outer = dot(qkv[blk, rows, lanes(h * HEAD)], cots[blk, rows, lanes(h * HEAD)], 0, 0)
                term = outer * level_coef(pos, idx, table, cs * 2 + zs, g, 1, h)
                first = term if first is None else first + term
                for k in range(4):
                    term = outer * level_coef(pos, idx, table, blk, g, k + 2, h)
                    sums[k] = term if sums[k] is None else sums[k] + term
            g1[blk, h] = first
        x0[zs, h] = total.astype(BF)
        m2[zs, h] = sums[0]
        m3[zs, h] = sums[1]
        m4[zs, h] = sums[2].astype(BF)
        m5[zs, h] = sums[3].astype(BF)


def local_kernel(pos, idx, table, qkv, cots, loc):
    rows = lax.broadcasted_iota(jnp.int32, (BLOCK, BLOCK), 0)
    cols = lax.broadcasted_iota(jnp.int32, (BLOCK, BLOCK), 1)
    causal = rows >= cols
    upper = rows < QB

    @pl.loop(0, 8)
    def _(step):
        blk, h = step // 2, step % 2
        q = qkv[blk, :, lanes(h * HEAD)]
        k = qkv[blk, :, lanes(256 + h * HEAD)]
        v = qkv[blk, :, lanes(512 + h * HEAD)]
        c = cots[blk, :, lanes(h * HEAD)]
        scale = jnp.where(
            upper,
            level_coef(pos, idx, table, blk, 0, 0, h),
            level_coef(pos, idx, table, blk, 1, 0, h),
        )
        scale = jnp.where(causal, scale, 0.0)
        scores = (dot(q, k, 1, 1) * scale).astype(BF)
        dscores = (dot(c, v, 1, 1) * scale).astype(BF)
        loc[blk, :, lanes(h * HEAD)] = dot(dscores, k, 1, 0)
        loc[blk, :, lanes(256 + h * HEAD)] = dot(dscores, q, 0, 0)
        loc[blk, :, lanes(512 + h * HEAD)] = dot(scores, c, 0, 0)
        loc[blk, :, lanes(768 + h * HEAD)] = dot(scores, v, 1, 0)


def gradient_pair(pos, toks, grads, dist, first, store):
    y, x, core, half = pos[0], pos[1], pos[2], pos[5]
    at = []
    for slot in (first, first + 1):
        yy = (y + dist + core * (slot - dist)) & 3
        xx = (x + slot + core * (dist - slot)) & 3
        at.append(lanes((yy * 4 + xx) * 128))
    part = None
    for blk in range(4):
        rows = jnp.concatenate([toks[blk][:, at[0]], toks[blk][:, at[1]]], axis=1)
        term = dot(rows, grads[blk], 0, 0)
        part = term if part is None else part + term
    part = part.astype(BF)
    for sub in range(2):
        for c in range(2):
            for piece in range(2):
                row = ((c + core) & 1) * 64 + ((piece + half) & 1) * 32
                start = sub * 128 + c * 64 + piece * 32
                store(sub, pl.ds(pl.multiple_of(row, 32), 32), part[start : start + 32])


def finish_kernel(pos, idx, table, *refs):
    toks = refs[0:4]
    cots, qkv, loc, s1, g1 = refs[4:9]
    cx1, cx2, cx3, cy1, cy2, cy3 = refs[9:15]
    own, r1, r2, r3 = refs[15:19]
    attn, grads, low, high = refs[19:]

    @pl.loop(0, 4)
    def _(step):
        zs, h = step // 2, step % 2
        far = [
            None,
            cx1[zs, h].astype(F32),
            cx2[zs, h].astype(F32) + cx3[zs, h].astype(F32),
            cy1[zs, h].astype(F32),
            cy2[zs, h].astype(F32) + cy3[zs, h].astype(F32),
        ]
        chip = own[zs, h].astype(F32) + r1[zs, h].astype(F32)
        chip = chip + r2[zs, h].astype(F32) + r3[zs, h].astype(F32)
        qs, ks = lanes(h * HEAD), lanes(256 + h * HEAD)
        vs, ats = lanes(512 + h * HEAD), lanes(768 + h * HEAD)
        for cs in range(2):
            blk = cs * 2 + zs
            other = (1 - cs) * 2 + zs
            far[0] = s1[other, h].astype(F32)
            grad = (chip + g1[other, h]).astype(BF)
            for g in range(2):
                rows = slice(g * QB, g * QB + QB)
                mixed = None
                for level in range(1, 6):
                    term = far[level - 1] * level_coef(pos, idx, table, blk, g, level, h)
                    mixed = term if mixed is None else mixed + term
                mixed = mixed.astype(BF)
                out = loc[blk, rows, ats] + dot(qkv[blk, rows, qs], mixed, 1, 0)
                attn[blk, rows, qs] = out.astype(BF)
                dq = loc[blk, rows, qs] + dot(cots[blk, rows, qs], mixed, 1, 1)
                grads[blk, rows, qs] = dq.astype(BF)
            dk = loc[blk, :, ks] + dot(qkv[blk, :, vs], grad, 1, 1)
            grads[blk, :, ks] = dk.astype(BF)
            dv = loc[blk, :, vs] + dot(qkv[blk, :, ks], grad, 1, 0)
            grads[blk, :, vs] = dv.astype(BF)

    for first, out in ((0, low), (2, high)):

        def store(sub, rows, value, out=out):
            out[sub, rows, :] = value

        gradient_pair(pos, toks, grads, 2, first, store)


def gradient_kernel(dists, pos, t0, t1, t2, t3, grads, _, *outs):
    toks = (t0, t1, t2, t3)

    @pl.loop(0, 2)
    def _(pair):
        for dist, out in zip(dists, outs):

            def store(sub, rows, value, out=out):
                out[pair * 2 + sub, rows, :] = value

            gradient_pair(pos, toks, grads, dist, pair * 2, store)


def total_kernel(pos, own, r1, r2, attn, from_core, from_z, t0, t1, t2, t3, attn_out):
    core, kind = pos[2], pos[4]
    for slot, out in enumerate((t0, t1, t2, t3)):
        total = own[slot].astype(F32) + r1[slot].astype(F32) + r2[slot].astype(F32)
        out[...] = total.astype(BF)
    attns = ((attn.at[0], from_z.at[0]), (from_core.at[0], from_z.at[1]))
    for cs in range(2):
        for zs in range(2):
            group = ((core + cs) & 1) * 2 + ((kind + zs) & 1)
            attn_out[:, pl.ds(pl.multiple_of(group * 256, 256), 256)] = attns[cs][zs][...]


def place_kernel(pos, mine, near, theirs, beyond, grad_w):
    core, kind = pos[2], pos[4]
    halves = (pos[5], pos[6])
    for cs in range(2):
        for zs in range(2):
            group = ((core + cs) & 1) * 2 + ((kind + zs) & 1)
            lane = pl.ds(pl.multiple_of(group * 256, 256), 256)
            for piece in range(2):
                part = ((mine, near), (theirs, beyond))[zs][piece]
                row = pl.ds(pl.multiple_of(((halves[zs] + piece) & 1) * 32, 32), 32)
                for third in range(3):
                    grad_w[third, row, lane] = part[
                        cs, :, third * 256 : third * 256 + 256
                    ].astype(F32)


def add(*parts):
    total = parts[0].astype(F32)
    for part in parts[1:]:
        total = total + part.astype(F32)
    return total.astype(BF)


def per_device(tokens, w_qkv, weight_table, weight_index, cotangent):
    y, x, core = lax.axis_index("y"), lax.axis_index("x"), lax.axis_index("core")
    z = lax.axis_index("dp")
    pos = jnp.stack(
        [y, x, core, z, (SETS >> z) & 1, (HALVES >> z) & 1, (HALVES >> (z ^ 1)) & 1]
    ).astype(jnp.int32)
    inputs = tokens[0]

    rows = weight_index.reshape(1, 12)
    rows = jnp.concatenate([rows, swap(rows, "dp", 8, 1)], axis=0)
    idx = jnp.concatenate([rows, swap(rows, "core", 2, 1)], axis=0)
    scalars = [pos, idx, weight_table]

    w_own, w_core, to_z, c_own, c_core = call(
        prepare_kernel,
        [pos, jnp.transpose(w_qkv, (1, 0, 2)), inputs, cotangent[0]],
        1,
        [
            ((64, COLS), BF),
            ((64, COLS), BF),
            ((BLOCK, D + 512), BF),
            ((BLOCK, 256), BF),
            ((BLOCK, 256), BF),
        ],
        scratch=[pltpu.SemaphoreType.DMA((11,))],
        grant=48,
        nbytes=4 * MIB,
        n_any=3,
        outs_any=True,
    )

    chunk = jnp.concatenate([w_own, swap(w_core, "core", 2, 1)], axis=0)
    near = [chunk] + [ring(chunk, 0, step) for step in (1, 2, 3)]
    mine = [jnp.concatenate(near[:2], axis=0), jnp.concatenate(near[2:], axis=0)]
    ahead = [ring(part, 1, 1) for part in mine]
    behind = [ring(part, 1, 3) for part in mine]
    far = [ring(behind[0], 1, 3), ring(ahead[1], 1, 1)]

    c_core = swap(c_core, "core", 2, 1)
    tok10 = swap(inputs, "core", 2, 1)
    tok01 = hold(swap(to_z, "dp", 8, 1), tok10, c_core, idx, *far, *ahead, *behind)
    tok11 = swap(tok01, "core", 2, 1)
    toks = [inputs, tok01, tok10, tok11]

    square = (2, 2, HEAD, HEAD)
    wide = (4, 2, HEAD, HEAD)
    qkv, cots, s1, x0, g1, m2, m3, m4, m5 = call(
        project_kernel,
        scalars + toks + [c_own, c_core] + mine + ahead + behind + far,
        3,
        [
            ((4, BLOCK, COLS), BF),
            ((4, BLOCK, 256), BF),
            (wide, BF),
            (square, BF),
            (wide, F32),
            (square, F32),
            (square, F32),
            (square, BF),
            (square, BF),
        ],
        scratch=[
            pltpu.VMEM((D, COLS), BF),
            pltpu.VMEM((4, BLOCK, D), BF),
            pltpu.SemaphoreType.DMA((40,)),
        ],
        grant=52,
        flops=2 * 1024 * D * COLS,
        nbytes=10 * MIB,
        n_any=14,
    )

    cx = [swap(x0, "x", 4, mask) for mask in (1, 2, 3)]
    dy = [swap(m, "y", 4, mask) for mask, m in ((1, m4), (2, m5), (3, m5))]
    (loc,) = call(
        local_kernel,
        scalars + [qkv, cots],
        3,
        [((4, BLOCK, 1024), F32)],
        grant=12,
        flops=8 * 6 * 2 * BLOCK * BLOCK * HEAD,
        nbytes=8 * MIB,
    )
    x1 = add(x0, *cx)
    cy = [swap(x1, "y", 4, mask) for mask in (1, 2, 3)]
    high = dy[0].astype(F32) + dy[1].astype(F32) + dy[2].astype(F32)
    near = (high + m2).astype(BF)
    far = (high + m3).astype(BF)
    dx = [swap(m, "x", 4, mask) for mask, m in ((1, near), (2, far), (3, far))]

    attn, grads, low, high = call(
        finish_kernel,
        scalars + toks + [cots, qkv, loc, s1, g1] + cx + cy + [high.astype(BF)] + dx,
        3,
        [
            ((4, BLOCK, 256), BF),
            ((4, BLOCK, COLS), BF),
            ((2, 128, COLS), BF),
            ((2, 128, COLS), BF),
        ],
        grant=24,
        flops=1024 * D * COLS,
        nbytes=12 * MIB,
    )
    low, high = ring(low, 1, 3), ring(high, 1, 1)
    from_core = swap(attn[2:], "core", 2, 1)
    onward, backward = call(
        functools.partial(gradient_kernel, (1, 3)),
        [pos] + toks + [grads, from_core],
        1,
        [((4, 128, COLS), BF)] * 2,
        grant=20,
        flops=1024 * D * COLS,
        nbytes=9 * MIB,
        n_any=1,
    )
    onward = jnp.concatenate([add(onward[:2], low), onward[2:]], axis=0)
    backward = jnp.concatenate([backward[:2], add(backward[2:], high)], axis=0)
    onward, backward = ring(onward, 1, 3), ring(backward, 1, 1)
    back = swap(jnp.stack([attn[1], from_core[1]], axis=0), "dp", 8, 1)
    (own,) = call(
        functools.partial(gradient_kernel, (0,)),
        [pos] + toks + [grads, from_core],
        1,
        [((4, 128, COLS), BF)],
        grant=20,
        flops=1024 * 512 * COLS,
        nbytes=9 * MIB,
        n_any=1,
    )
    *total, attn_out = call(
        total_kernel,
        [pos, own, onward, backward, attn, from_core, back],
        1,
        [((128, COLS), BF)] * 4 + [((BLOCK, 1024), BF)],
        grant=10,
        nbytes=4 * MIB,
    )
    chip_sum = add(total[0], *[ring(total[step], 0, -step) for step in (1, 2, 3)])
    pair = jnp.stack([chip_sum[:64], swap(chip_sum[64:], "core", 2, 1)], axis=0)
    mine = add(pair[:, :32], same_set_neighbour(pair[:, 32:]))
    mine = add(mine, same_set_far(mine))
    near = same_set_neighbour(mine)
    theirs = swap(mine, "dp", 8, 1)
    beyond = swap(near, "dp", 8, 1)

    (grad_w,) = call(
        place_kernel,
        [pos, mine, near, theirs, beyond],
        1,
        [((3, 64, 1024), F32)],
        grant=6,
        nbytes=3 * MIB,
    )
    return attn_out[None], jnp.transpose(grad_w, (1, 0, 2))


def solution(mesh):
    grid = Mesh(mesh.devices.reshape(4, 4, 2, 8), ("y", "x", "core", "dp"))
    seq = ("y", "x", "core")
    return jax.shard_map(
        per_device,
        mesh=grid,
        in_specs=(P("dp", seq, None), P(seq, None, None), P(), P("dp", seq, None), P("dp", seq, None)),
        out_specs=(P("dp", seq, None), P(seq, None, None)),
        check_vma=False,
    )
```

```python
import functools
import math

import jax
import jax.numpy as jnp
from jax import lax
from jax.experimental import pallas as pl
from jax.experimental.pallas import tpu as pltpu
from jax.sharding import Mesh, PartitionSpec as P

BF = jnp.bfloat16
F32 = jnp.float32
HEAD = 128
QB = 128
BLOCK = 256
D = 2048
COLS = 768
MIB = 1024 * 1024
SETS = 0x66
HALVES = 0xB4


def ring(value, phase, step):
    pairs = []
    for y in range(4):
        for x in range(4):
            for core in range(2):
                at = (y, (x - step) % 4) if core == phase else ((y - step) % 4, x)
                pairs.append(((y * 4 + x) * 2 + core, (at[0] * 4 + at[1]) * 2 + core))
    return lax.ppermute(value, ("y", "x", "core"), pairs)


def swap(value, axis, size, mask):
    return lax.ppermute(value, axis, [(i, i ^ mask) for i in range(size)])


def same_set_neighbour(value):
    return lax.ppermute(value, "dp", [(z, (z + 1 if z % 2 else z - 1) % 8) for z in range(8)])


def same_set_far(value):
    return lax.ppermute(value, "dp", [(z, ((7 if SETS >> z & 1 else 3) - z) % 8) for z in range(8)])


def behind_all(value, others, index):
    zero = sum(other[0, 0].astype(F32) for other in others) * 0.0
    zero = zero + (index[-1, -1] < 0).astype(F32)
    return (value.astype(F32) + zero).astype(value.dtype)


def dot(a, b, ca, cb):
    return lax.dot_general(a, b, (((ca,), (cb,)), ((), ())), preferred_element_type=F32)


def smem():
    return pl.BlockSpec(memory_space=pltpu.SMEM)


def vmem():
    return pl.BlockSpec(memory_space=pltpu.VMEM)


def call(kernel, args, n_smem, outs, scratch=(), grant=16, flops=0, nbytes=0, n_any=0):
    return pl.pallas_call(
        kernel,
        out_shape=[jax.ShapeDtypeStruct(*out) for out in outs],
        in_specs=[smem()] * n_smem
        + [vmem()] * (len(args) - n_smem - n_any)
        + [pl.BlockSpec(memory_space=pl.ANY)] * n_any,
        out_specs=[vmem()] * len(outs),
        scratch_shapes=list(scratch),
        compiler_params=pltpu.CompilerParams(vmem_limit_bytes=grant * MIB),
        cost_estimate=pl.CostEstimate(flops=flops, bytes_accessed=nbytes, transcendentals=0),
    )(*args)


def lanes(start):
    return pl.ds(pl.multiple_of(start, HEAD), HEAD)


def level_coef(pos, idx, table, blk, group, level, head):
    cs = blk // 2
    y, x, core = pos[0], pos[1], pos[2]
    row = idx[blk, group * 6 + level]
    lam = table[row, (core * 2 + pos[4]) * 2 + head]
    if level == 0:
        return lam * (1.0 / math.sqrt(HEAD * BLOCK))
    bit = [(core + cs) & 1, x & 1, (x >> 1) & 1, y & 1, (y >> 1) & 1][level - 1]
    return lam * bit.astype(F32) * (1.0 / math.sqrt(HEAD * 2 ** (level - 1) * BLOCK))


def prepare_kernel(pos, w, w_own, w_core):
    core, kind = pos[2], pos[4]
    mine = pl.multiple_of((core * 2 + kind) * 256, 256)
    other = pl.multiple_of(((1 - core) * 2 + kind) * 256, 256)
    for third in range(3):
        at = slice(third * 256, third * 256 + 256)
        w_own[:, at] = w[third, :, pl.ds(mine, 256)]
        w_core[:, at] = w[third, :, pl.ds(other, 256)]


def split_kernel(pos, cot, own, to_core, to_z):
    core, kind = pos[2], pos[4]

    def columns(cs, zs):
        group = ((core + cs) & 1) * 2 + ((kind + zs) & 1)
        return cot[:, pl.ds(pl.multiple_of(group * 256, 256), 256)]

    own[...] = columns(0, 0)
    to_core[...] = columns(1, 0)
    to_z[:, :256] = columns(0, 1)
    to_z[:, 256:] = columns(1, 1)


def project_blocks(pos, idx, table, toks, w, zs, qkv, cots, s1, x0, g1, sums_out):
    for part in range(3):
        cols = slice(part * 256, part * 256 + 256)
        for cs in range(2):
            qkv[cs][:, cols] = dot(toks[cs][...], w[:, cols], 1, 0).astype(BF)
    for h in range(2):
        qs = slice(h * HEAD, h * HEAD + HEAD)
        ks = slice(256 + h * HEAD, 256 + h * HEAD + HEAD)
        vs = slice(512 + h * HEAD, 512 + h * HEAD + HEAD)
        total = None
        sums = [None] * 4
        for cs in range(2):
            blk = cs * 2 + zs
            state = dot(qkv[cs][:, ks], qkv[cs][:, vs], 0, 0)
            s1[cs][h] = state.astype(BF)
            total = state if total is None else total + state
            first = None
            for g in range(2):
                rows = slice(g * QB, g * QB + QB)
                outer = dot(qkv[cs][rows, qs], cots[cs][rows, qs], 0, 0)
                term = outer * level_coef(pos, idx, table, blk, g, 1, h)
                first = term if first is None else first + term
                for k in range(4):
                    term = outer * level_coef(pos, idx, table, blk, g, k + 2, h)
                    sums[k] = term if sums[k] is None else sums[k] + term
            g1[cs][h] = first
        x0[h] = total.astype(BF)
        for out, value in zip(sums_out, sums):
            out[h] = value.astype(out.dtype)


def first_kernel(pos, idx, table, t0, t1, c_own, c_core, *refs):
    parts = (refs[0:2], refs[2:4], refs[6:8], refs[4:6])
    qkv, cots, s1, x0, g1, m2, m3, m4, m5, w = refs[8:]
    y, x, core = pos[0], pos[1], pos[2]
    for slot in range(4):
        for dist in range(4):
            yy = (y + dist + core * (slot - dist)) & 3
            xx = (x + slot + core * (dist - slot)) & 3
            for cs in range(2):
                row = pl.multiple_of((yy * 4 + xx) * 128 + ((core + cs) & 1) * 64, 64)
                start = (slot % 2) * 128 + cs * 64
                w[pl.ds(row, 64), :] = parts[dist][slot // 2][start : start + 64, :]
    cots[0] = c_own[...]
    cots[1] = c_core[...]

    def both(ref):
        return ref.at[0], ref.at[1]

    project_blocks(
        pos, idx, table, (t0, t1), w, 0, both(qkv), both(cots), both(s1), x0, both(g1), (m2, m3, m4, m5)
    )


def second_kernel(pos, idx, table, t0, t1, c_near, c_across, w, *refs):
    firsts, outs = refs[:9], refs[9:]
    for n, (src, out) in enumerate(zip(firsts, outs)):
        if n in (0, 1, 2, 4):
            out[0] = src[0]
            out[2] = src[1]
        else:
            out[0] = src[...]
    qkv, cots, s1, x0, g1, m2, m3, m4, m5 = outs
    cots[1] = c_near[...]
    cots[3] = c_across[...]

    def both(ref):
        return ref.at[1], ref.at[3]

    project_blocks(
        pos,
        idx,
        table,
        (t0, t1),
        w,
        1,
        both(qkv),
        both(cots),
        both(s1),
        x0.at[1],
        both(g1),
        (m2.at[1], m3.at[1], m4.at[1], m5.at[1]),
    )


def local_kernel(pos, idx, table, qkv, cots, loc):
    rows = lax.broadcasted_iota(jnp.int32, (BLOCK, BLOCK), 0)
    cols = lax.broadcasted_iota(jnp.int32, (BLOCK, BLOCK), 1)
    causal = rows >= cols
    upper = rows < QB

    @pl.loop(0, 4)
    def _(blk):
        for h in range(2):
            qs = slice(h * HEAD, h * HEAD + HEAD)
            ks = slice(256 + h * HEAD, 256 + h * HEAD + HEAD)
            vs = slice(512 + h * HEAD, 512 + h * HEAD + HEAD)
            q, k, v, c = qkv[blk, :, qs], qkv[blk, :, ks], qkv[blk, :, vs], cots[blk, :, qs]
            scale = jnp.where(
                upper,
                level_coef(pos, idx, table, blk, 0, 0, h),
                level_coef(pos, idx, table, blk, 1, 0, h),
            )
            scale = jnp.where(causal, scale, 0.0)
            scores = (dot(q, k, 1, 1) * scale).astype(BF)
            dscores = (dot(c, v, 1, 1) * scale).astype(BF)
            loc[blk, :, qs] = dot(dscores, k, 1, 0)
            loc[blk, :, ks] = dot(dscores, q, 0, 0)
            loc[blk, :, vs] = dot(scores, c, 0, 0)
            loc[blk, :, 768 + h * HEAD : 768 + h * HEAD + HEAD] = dot(scores, v, 1, 0)


def gradient_pair(pos, toks, grads, dist, first, store):
    y, x, core, half = pos[0], pos[1], pos[2], pos[5]
    at = []
    for slot in (first, first + 1):
        yy = (y + dist + core * (slot - dist)) & 3
        xx = (x + slot + core * (dist - slot)) & 3
        at.append(lanes((yy * 4 + xx) * 128))
    part = None
    for blk in range(4):
        rows = jnp.concatenate([toks[blk][:, at[0]], toks[blk][:, at[1]]], axis=1)
        term = dot(rows, grads[blk], 0, 0)
        part = term if part is None else part + term
    part = part.astype(BF)
    for sub in range(2):
        for c in range(2):
            for piece in range(2):
                row = ((c + core) & 1) * 64 + ((piece + half) & 1) * 32
                start = sub * 128 + c * 64 + piece * 32
                store(sub, pl.ds(pl.multiple_of(row, 32), 32), part[start : start + 32])


def finish_kernel(pos, idx, table, *refs):
    toks = refs[0:4]
    cots, qkv, loc, s1, g1 = refs[4:9]
    cx1, cx2, cx3, cy1, cy2, cy3 = refs[9:15]
    own, r1, r2, r3 = refs[15:19]
    attn, grads, low, high = refs[19:]

    @pl.loop(0, 4)
    def _(step):
        zs, h = step // 2, step % 2
        far = [
            None,
            cx1[zs, h].astype(F32),
            cx2[zs, h].astype(F32) + cx3[zs, h].astype(F32),
            cy1[zs, h].astype(F32),
            cy2[zs, h].astype(F32) + cy3[zs, h].astype(F32),
        ]
        chip = own[zs, h].astype(F32) + r1[zs, h].astype(F32)
        chip = chip + r2[zs, h].astype(F32) + r3[zs, h].astype(F32)
        qs, ks = lanes(h * HEAD), lanes(256 + h * HEAD)
        vs, ats = lanes(512 + h * HEAD), lanes(768 + h * HEAD)
        for cs in range(2):
            blk = cs * 2 + zs
            other = (1 - cs) * 2 + zs
            far[0] = s1[other, h].astype(F32)
            grad = (chip + g1[other, h]).astype(BF)
            for g in range(2):
                rows = slice(g * QB, g * QB + QB)
                mixed = None
                for level in range(1, 6):
                    term = far[level - 1] * level_coef(pos, idx, table, blk, g, level, h)
                    mixed = term if mixed is None else mixed + term
                mixed = mixed.astype(BF)
                out = loc[blk, rows, ats] + dot(qkv[blk, rows, qs], mixed, 1, 0)
                attn[blk, rows, qs] = out.astype(BF)
                dq = loc[blk, rows, qs] + dot(cots[blk, rows, qs], mixed, 1, 1)
                grads[blk, rows, qs] = dq.astype(BF)
            dk = loc[blk, :, ks] + dot(qkv[blk, :, vs], grad, 1, 1)
            grads[blk, :, ks] = dk.astype(BF)
            dv = loc[blk, :, vs] + dot(qkv[blk, :, ks], grad, 1, 0)
            grads[blk, :, vs] = dv.astype(BF)

    for first, out in ((0, low), (2, high)):

        def store(sub, rows, value, out=out):
            out[sub, rows, :] = value

        gradient_pair(pos, toks, grads, 2, first, store)


def gradient_kernel(dists, pos, t0, t1, t2, t3, grads, _, *outs):
    toks = (t0, t1, t2, t3)

    @pl.loop(0, 2)
    def _(pair):
        for dist, out in zip(dists, outs):

            def store(sub, rows, value, out=out):
                out[pair * 2 + sub, rows, :] = value

            gradient_pair(pos, toks, grads, dist, pair * 2, store)


def total_kernel(pos, own, r1, r2, attn, from_core, from_z, t0, t1, t2, t3, attn_out):
    core, kind = pos[2], pos[4]
    for slot, out in enumerate((t0, t1, t2, t3)):
        total = own[slot].astype(F32) + r1[slot].astype(F32) + r2[slot].astype(F32)
        out[...] = total.astype(BF)
    attns = ((attn.at[0], from_z.at[0]), (from_core.at[0], from_z.at[1]))
    for cs in range(2):
        for zs in range(2):
            group = ((core + cs) & 1) * 2 + ((kind + zs) & 1)
            attn_out[:, pl.ds(pl.multiple_of(group * 256, 256), 256)] = attns[cs][zs][...]


def place_kernel(pos, mine, near, theirs, beyond, grad_w):
    core, kind = pos[2], pos[4]
    halves = (pos[5], pos[6])
    for cs in range(2):
        for zs in range(2):
            group = ((core + cs) & 1) * 2 + ((kind + zs) & 1)
            lane = pl.ds(pl.multiple_of(group * 256, 256), 256)
            for piece in range(2):
                part = ((mine, near), (theirs, beyond))[zs][piece]
                row = pl.ds(pl.multiple_of(((halves[zs] + piece) & 1) * 32, 32), 32)
                for third in range(3):
                    grad_w[third, row, lane] = part[
                        cs, :, third * 256 : third * 256 + 256
                    ].astype(F32)


def add(*parts):
    total = parts[0].astype(F32)
    for part in parts[1:]:
        total = total + part.astype(F32)
    return total.astype(BF)


def per_device(tokens, w_qkv, weight_table, weight_index, cotangent):
    y, x, core = lax.axis_index("y"), lax.axis_index("x"), lax.axis_index("core")
    z = lax.axis_index("dp")
    pos = jnp.stack(
        [y, x, core, z, (SETS >> z) & 1, (HALVES >> z) & 1, (HALVES >> (z ^ 1)) & 1]
    ).astype(jnp.int32)
    inputs = tokens[0]

    rows = weight_index.reshape(1, 12)
    rows = jnp.concatenate([rows, swap(rows, "dp", 8, 1)], axis=0)
    idx = jnp.concatenate([rows, swap(rows, "core", 2, 1)], axis=0)
    scalars = [pos, idx, weight_table]

    w_own, w_core = call(
        prepare_kernel,
        [pos, jnp.transpose(w_qkv, (1, 0, 2))],
        1,
        [((64, COLS), BF)] * 2,
        grant=58,
        nbytes=MIB,
    )
    c_own, c_core, c_z = call(
        split_kernel,
        [pos, cotangent[0]],
        1,
        [((BLOCK, 256), BF)] * 2 + [((BLOCK, 512), BF)],
        grant=58,
        nbytes=MIB,
    )

    chunk = jnp.concatenate([w_own, swap(w_core, "core", 2, 1)], axis=0)
    near = [chunk] + [ring(chunk, 0, step) for step in (1, 2, 3)]
    mine = [jnp.concatenate(near[:2], axis=0), jnp.concatenate(near[2:], axis=0)]
    ahead = [ring(part, 1, 1) for part in mine]
    behind = [ring(part, 1, 3) for part in mine]
    far = [ring(behind[0], 1, 3), ring(ahead[1], 1, 1)]

    c_core = swap(c_core, "core", 2, 1)
    c_z = swap(c_z, "dp", 8, 1)
    c_near, c_across = c_z[:, :256], swap(c_z[:, 256:], "core", 2, 1)
    tok10 = swap(inputs, "core", 2, 1)
    tok01 = behind_all(swap(inputs, "dp", 8, 1), [c_across, c_core, *far, ahead[0], behind[1]], idx)
    tok11 = swap(tok01, "core", 2, 1)
    toks = [inputs, tok01, tok10, tok11]

    tile = (HEAD, HEAD)
    *firsts, w_all = call(
        first_kernel,
        scalars + [inputs, tok10, c_own, c_core] + mine + ahead + behind + far,
        3,
        [
            ((2, BLOCK, COLS), BF),
            ((2, BLOCK, 256), BF),
            ((2, 2) + tile, BF),
            ((2,) + tile, BF),
            ((2, 2) + tile, F32),
            ((2,) + tile, F32),
            ((2,) + tile, F32),
            ((2,) + tile, BF),
            ((2,) + tile, BF),
            ((D, COLS), BF),
        ],
        grant=58,
        flops=1024 * D * COLS,
        nbytes=10 * MIB,
    )
    qkv, cots, s1, x0, g1, m2, m3, m4, m5 = call(
        second_kernel,
        scalars + [tok01, tok11, c_near, c_across, w_all] + firsts,
        3,
        [
            ((4, BLOCK, COLS), BF),
            ((4, BLOCK, 256), BF),
            ((4, 2) + tile, BF),
            ((2, 2) + tile, BF),
            ((4, 2) + tile, F32),
            ((2, 2) + tile, F32),
            ((2, 2) + tile, F32),
            ((2, 2) + tile, BF),
            ((2, 2) + tile, BF),
        ],
        grant=58,
        flops=1024 * D * COLS,
        nbytes=10 * MIB,
    )

    cx = [swap(x0, "x", 4, mask) for mask in (1, 2, 3)]
    dy = [swap(m, "y", 4, mask) for mask, m in ((1, m4), (2, m5), (3, m5))]
    (loc,) = call(
        local_kernel,
        scalars + [qkv, cots],
        3,
        [((4, BLOCK, 1024), F32)],
        grant=12,
        flops=8 * 6 * 2 * BLOCK * BLOCK * HEAD,
        nbytes=8 * MIB,
    )
    x1 = add(x0, *cx)
    cy = [swap(x1, "y", 4, mask) for mask in (1, 2, 3)]
    high = dy[0].astype(F32) + dy[1].astype(F32) + dy[2].astype(F32)
    near = (high + m2).astype(BF)
    far = (high + m3).astype(BF)
    dx = [swap(m, "x", 4, mask) for mask, m in ((1, near), (2, far), (3, far))]

    attn, grads, low, high = call(
        finish_kernel,
        scalars + toks + [cots, qkv, loc, s1, g1] + cx + cy + [high.astype(BF)] + dx,
        3,
        [
            ((4, BLOCK, 256), BF),
            ((4, BLOCK, COLS), BF),
            ((2, 128, COLS), BF),
            ((2, 128, COLS), BF),
        ],
        grant=24,
        flops=1024 * D * COLS,
        nbytes=12 * MIB,
    )
    low, high = ring(low, 1, 3), ring(high, 1, 1)
    from_core = swap(attn[2:], "core", 2, 1)
    onward, backward = call(
        functools.partial(gradient_kernel, (1, 3)),
        [pos] + toks + [grads, from_core],
        1,
        [((4, 128, COLS), BF)] * 2,
        grant=20,
        flops=1024 * D * COLS,
        nbytes=9 * MIB,
        n_any=1,
    )
    onward = jnp.concatenate([add(onward[:2], low), onward[2:]], axis=0)
    backward = jnp.concatenate([backward[:2], add(backward[2:], high)], axis=0)
    onward, backward = ring(onward, 1, 3), ring(backward, 1, 1)
    back = swap(jnp.stack([attn[1], from_core[1]], axis=0), "dp", 8, 1)
    (own,) = call(
        functools.partial(gradient_kernel, (0,)),
        [pos] + toks + [grads, from_core],
        1,
        [((4, 128, COLS), BF)],
        grant=20,
        flops=1024 * 512 * COLS,
        nbytes=9 * MIB,
        n_any=1,
    )
    *total, attn_out = call(
        total_kernel,
        [pos, own, onward, backward, attn, from_core, back],
        1,
        [((128, COLS), BF)] * 4 + [((BLOCK, 1024), BF)],
        grant=10,
        nbytes=4 * MIB,
    )
    chip_sum = add(total[0], *[ring(total[step], 0, -step) for step in (1, 2, 3)])
    pair = jnp.stack([chip_sum[:64], swap(chip_sum[64:], "core", 2, 1)], axis=0)
    mine = add(pair[:, :32], same_set_neighbour(pair[:, 32:]))
    mine = add(mine, same_set_far(mine))
    near = same_set_neighbour(mine)
    theirs = swap(mine, "dp", 8, 1)
    beyond = swap(near, "dp", 8, 1)

    (grad_w,) = call(
        place_kernel,
        [pos, mine, near, theirs, beyond],
        1,
        [((3, 64, 1024), F32)],
        grant=6,
        nbytes=3 * MIB,
    )
    return attn_out[None], jnp.transpose(grad_w, (1, 0, 2))


def solution(mesh):
    grid = Mesh(mesh.devices.reshape(4, 4, 2, 8), ("y", "x", "core", "dp"))
    seq = ("y", "x", "core")
    return jax.shard_map(
        per_device,
        mesh=grid,
        in_specs=(P("dp", seq, None), P(seq, None, None), P(), P("dp", seq, None), P("dp", seq, None)),
        out_specs=(P("dp", seq, None), P(seq, None, None)),
        check_vma=False,
    )
```

```python
import functools
import math

import jax
import jax.numpy as jnp
from jax import lax
from jax.experimental import pallas as pl
from jax.experimental.pallas import tpu as pltpu
from jax.sharding import Mesh, PartitionSpec as P

BF = jnp.bfloat16
F32 = jnp.float32
HEAD = 128
QB = 128
BLOCK = 256
D = 2048
COLS = 768
MIB = 1024 * 1024
SETS = 0x66
HALVES = 0xB4


def ring(value, phase, step):
    pairs = []
    for y in range(4):
        for x in range(4):
            for core in range(2):
                at = (y, (x - step) % 4) if core == phase else ((y - step) % 4, x)
                pairs.append(((y * 4 + x) * 2 + core, (at[0] * 4 + at[1]) * 2 + core))
    return lax.ppermute(value, ("y", "x", "core"), pairs)


def swap(value, axis, size, mask):
    return lax.ppermute(value, axis, [(i, i ^ mask) for i in range(size)])


def same_set_neighbour(value):
    return lax.ppermute(value, "dp", [(z, (z + 1 if z % 2 else z - 1) % 8) for z in range(8)])


def same_set_far(value):
    return lax.ppermute(value, "dp", [(z, ((7 if SETS >> z & 1 else 3) - z) % 8) for z in range(8)])


def behind(value, *others, index=None):
    zero = sum(other[0, 0].astype(F32) for other in others) * 0.0
    if index is not None:
        zero = zero + (index[-1, -1] < 0).astype(F32)
    return (value.astype(F32) + zero).astype(value.dtype)


def dot(a, b, ca, cb):
    return lax.dot_general(a, b, (((ca,), (cb,)), ((), ())), preferred_element_type=F32)


def smem():
    return pl.BlockSpec(memory_space=pltpu.SMEM)


def vmem():
    return pl.BlockSpec(memory_space=pltpu.VMEM)


def call(kernel, args, n_smem, outs, scratch=(), grant=16, flops=0, nbytes=0, n_any=0):
    return pl.pallas_call(
        kernel,
        out_shape=[jax.ShapeDtypeStruct(*out) for out in outs],
        in_specs=[smem()] * n_smem
        + [vmem()] * (len(args) - n_smem - n_any)
        + [pl.BlockSpec(memory_space=pl.ANY)] * n_any,
        out_specs=[vmem()] * len(outs),
        scratch_shapes=list(scratch),
        compiler_params=pltpu.CompilerParams(vmem_limit_bytes=grant * MIB),
        cost_estimate=pl.CostEstimate(flops=flops, bytes_accessed=nbytes, transcendentals=0),
    )(*args)


def lanes(start):
    return pl.ds(pl.multiple_of(start, HEAD), HEAD)


def level_coef(pos, idx, table, blk, group, level, head):
    cs = blk // 2
    y, x, core = pos[0], pos[1], pos[2]
    row = idx[blk, group * 6 + level]
    lam = table[row, (core * 2 + pos[4]) * 2 + head]
    if level == 0:
        return lam * (1.0 / math.sqrt(HEAD * BLOCK))
    bit = [(core + cs) & 1, x & 1, (x >> 1) & 1, y & 1, (y >> 1) & 1][level - 1]
    return lam * bit.astype(F32) * (1.0 / math.sqrt(HEAD * 2 ** (level - 1) * BLOCK))


def prepare_kernel(pos, w, w_own, w_core):
    core, kind = pos[2], pos[4]
    mine = pl.multiple_of((core * 2 + kind) * 256, 256)
    other = pl.multiple_of(((1 - core) * 2 + kind) * 256, 256)
    for third in range(3):
        at = slice(third * 256, third * 256 + 256)
        w_own[:, at] = w[third, :, pl.ds(mine, 256)]
        w_core[:, at] = w[third, :, pl.ds(other, 256)]


def split_kernel(pos, cot, own, to_core, to_z):
    core, kind = pos[2], pos[4]

    def columns(cs, zs):
        group = ((core + cs) & 1) * 2 + ((kind + zs) & 1)
        return cot[:, pl.ds(pl.multiple_of(group * 256, 256), 256)]

    own[...] = columns(0, 0)
    to_core[...] = columns(1, 0)
    to_z[:, :256] = columns(0, 1)
    to_z[:, 256:] = columns(1, 1)


def project_kernel(pos, idx, table, t0, t1, t2, t3, c0, c1, c2, c3, *refs):
    toks = (t0, t1, t2, t3)
    parts = (refs[0:2], refs[2:4], refs[6:8], refs[4:6])
    qkv, cots, s1, x0, g1, m2, m3, m4, m5, w = refs[8:]
    y, x, core = pos[0], pos[1], pos[2]
    for slot in range(4):
        for dist in range(4):
            yy = (y + dist + core * (slot - dist)) & 3
            xx = (x + slot + core * (dist - slot)) & 3
            for cs in range(2):
                row = pl.multiple_of((yy * 4 + xx) * 128 + ((core + cs) & 1) * 64, 64)
                start = (slot % 2) * 128 + cs * 64
                w[pl.ds(row, 64), :] = parts[dist][slot // 2][start : start + 64, :]
    for blk, src in enumerate((c0, c1, c2, c3)):
        cots[blk] = src[...]

    @pl.loop(0, 3)
    def _(part):
        cols = pl.ds(pl.multiple_of(part * 256, 256), 256)
        for blk in range(4):
            qkv[blk, :, cols] = dot(toks[blk][...], w[:, cols], 1, 0).astype(BF)

    @pl.loop(0, 4)
    def _(step):
        zs, h = step // 2, step % 2
        total = None
        sums = [None] * 4
        for cs in range(2):
            blk = cs * 2 + zs
            state = dot(qkv[blk, :, lanes(256 + h * HEAD)], qkv[blk, :, lanes(512 + h * HEAD)], 0, 0)
            s1[blk, h] = state.astype(BF)
            total = state if total is None else total + state
            first = None
            for g in range(2):
                rows = slice(g * QB, g * QB + QB)
                outer = dot(qkv[blk, rows, lanes(h * HEAD)], cots[blk, rows, lanes(h * HEAD)], 0, 0)
                term = outer * level_coef(pos, idx, table, blk, g, 1, h)
                first = term if first is None else first + term
                for k in range(4):
                    term = outer * level_coef(pos, idx, table, blk, g, k + 2, h)
                    sums[k] = term if sums[k] is None else sums[k] + term
            g1[blk, h] = first
        x0[zs, h] = total.astype(BF)
        for out, value in zip((m2, m3, m4, m5), sums):
            out[zs, h] = value.astype(out.dtype)


def local_kernel(pos, idx, table, qkv, cots, loc):
    rows = lax.broadcasted_iota(jnp.int32, (BLOCK, BLOCK), 0)
    cols = lax.broadcasted_iota(jnp.int32, (BLOCK, BLOCK), 1)
    causal = rows >= cols
    upper = rows < QB

    @pl.loop(0, 4)
    def _(blk):
        for h in range(2):
            qs = slice(h * HEAD, h * HEAD + HEAD)
            ks = slice(256 + h * HEAD, 256 + h * HEAD + HEAD)
            vs = slice(512 + h * HEAD, 512 + h * HEAD + HEAD)
            q, k, v, c = qkv[blk, :, qs], qkv[blk, :, ks], qkv[blk, :, vs], cots[blk, :, qs]
            scale = jnp.where(
                upper,
                level_coef(pos, idx, table, blk, 0, 0, h),
                level_coef(pos, idx, table, blk, 1, 0, h),
            )
            scale = jnp.where(causal, scale, 0.0)
            scores = (dot(q, k, 1, 1) * scale).astype(BF)
            dscores = (dot(c, v, 1, 1) * scale).astype(BF)
            loc[blk, :, qs] = dot(dscores, k, 1, 0)
            loc[blk, :, ks] = dot(dscores, q, 0, 0)
            loc[blk, :, vs] = dot(scores, c, 0, 0)
            loc[blk, :, 768 + h * HEAD : 768 + h * HEAD + HEAD] = dot(scores, v, 1, 0)


def gradient_pair(pos, toks, grads, dist, first, store):
    y, x, core, half = pos[0], pos[1], pos[2], pos[5]
    at = []
    for slot in (first, first + 1):
        yy = (y + dist + core * (slot - dist)) & 3
        xx = (x + slot + core * (dist - slot)) & 3
        at.append(lanes((yy * 4 + xx) * 128))
    part = None
    for blk in range(4):
        rows = jnp.concatenate([toks[blk][:, at[0]], toks[blk][:, at[1]]], axis=1)
        term = dot(rows, grads[blk], 0, 0)
        part = term if part is None else part + term
    part = part.astype(BF)
    for sub in range(2):
        for c in range(2):
            for piece in range(2):
                row = ((c + core) & 1) * 64 + ((piece + half) & 1) * 32
                start = sub * 128 + c * 64 + piece * 32
                store(sub, pl.ds(pl.multiple_of(row, 32), 32), part[start : start + 32])


def finish_kernel(pos, idx, table, *refs):
    toks = refs[0:4]
    cots, qkv, loc, s1, g1 = refs[4:9]
    cx1, cx2, cx3, cy1, cy2, cy3 = refs[9:15]
    own, r1, r2, r3 = refs[15:19]
    attn, grads, low, high = refs[19:]

    @pl.loop(0, 4)
    def _(step):
        zs, h = step // 2, step % 2
        far = [
            None,
            cx1[zs, h].astype(F32),
            cx2[zs, h].astype(F32) + cx3[zs, h].astype(F32),
            cy1[zs, h].astype(F32),
            cy2[zs, h].astype(F32) + cy3[zs, h].astype(F32),
        ]
        chip = own[zs, h].astype(F32) + r1[zs, h].astype(F32)
        chip = chip + r2[zs, h].astype(F32) + r3[zs, h].astype(F32)
        qs, ks = lanes(h * HEAD), lanes(256 + h * HEAD)
        vs, ats = lanes(512 + h * HEAD), lanes(768 + h * HEAD)
        for cs in range(2):
            blk = cs * 2 + zs
            other = (1 - cs) * 2 + zs
            far[0] = s1[other, h].astype(F32)
            grad = (chip + g1[other, h]).astype(BF)
            for g in range(2):
                rows = slice(g * QB, g * QB + QB)
                mixed = None
                for level in range(1, 6):
                    term = far[level - 1] * level_coef(pos, idx, table, blk, g, level, h)
                    mixed = term if mixed is None else mixed + term
                mixed = mixed.astype(BF)
                out = loc[blk, rows, ats] + dot(qkv[blk, rows, qs], mixed, 1, 0)
                attn[blk, rows, qs] = out.astype(BF)
                dq = loc[blk, rows, qs] + dot(cots[blk, rows, qs], mixed, 1, 1)
                grads[blk, rows, qs] = dq.astype(BF)
            dk = loc[blk, :, ks] + dot(qkv[blk, :, vs], grad, 1, 1)
            grads[blk, :, ks] = dk.astype(BF)
            dv = loc[blk, :, vs] + dot(qkv[blk, :, ks], grad, 1, 0)
            grads[blk, :, vs] = dv.astype(BF)

    for first, out in ((0, low), (2, high)):

        def store(sub, rows, value, out=out):
            out[sub, rows, :] = value

        gradient_pair(pos, toks, grads, 2, first, store)


def gradient_kernel(dists, pos, t0, t1, t2, t3, grads, _, *outs):
    toks = (t0, t1, t2, t3)

    @pl.loop(0, 2)
    def _(pair):
        for dist, out in zip(dists, outs):

            def store(sub, rows, value, out=out):
                out[pair * 2 + sub, rows, :] = value

            gradient_pair(pos, toks, grads, dist, pair * 2, store)


def total_kernel(pos, own, r1, r2, attn, from_core, from_z, t0, t1, t2, t3, attn_out):
    core, kind = pos[2], pos[4]
    for slot, out in enumerate((t0, t1, t2, t3)):
        total = own[slot].astype(F32) + r1[slot].astype(F32) + r2[slot].astype(F32)
        out[...] = total.astype(BF)
    attns = ((attn.at[0], from_z.at[0]), (from_core.at[0], from_z.at[1]))
    for cs in range(2):
        for zs in range(2):
            group = ((core + cs) & 1) * 2 + ((kind + zs) & 1)
            attn_out[:, pl.ds(pl.multiple_of(group * 256, 256), 256)] = attns[cs][zs][...]


def place_kernel(pos, mine, near, theirs, beyond, grad_w):
    core, kind = pos[2], pos[4]
    halves = (pos[5], pos[6])
    for cs in range(2):
        for zs in range(2):
            group = ((core + cs) & 1) * 2 + ((kind + zs) & 1)
            lane = pl.ds(pl.multiple_of(group * 256, 256), 256)
            for piece in range(2):
                part = ((mine, near), (theirs, beyond))[zs][piece]
                row = pl.ds(pl.multiple_of(((halves[zs] + piece) & 1) * 32, 32), 32)
                for third in range(3):
                    grad_w[third, row, lane] = part[
                        cs, :, third * 256 : third * 256 + 256
                    ].astype(F32)


def add(*parts):
    total = parts[0].astype(F32)
    for part in parts[1:]:
        total = total + part.astype(F32)
    return total.astype(BF)


def per_device(tokens, w_qkv, weight_table, weight_index, cotangent):
    y, x, core = lax.axis_index("y"), lax.axis_index("x"), lax.axis_index("core")
    z = lax.axis_index("dp")
    pos = jnp.stack(
        [y, x, core, z, (SETS >> z) & 1, (HALVES >> z) & 1, (HALVES >> (z ^ 1)) & 1]
    ).astype(jnp.int32)
    inputs = tokens[0]

    rows = weight_index.reshape(1, 12)
    rows = jnp.concatenate([rows, swap(rows, "dp", 8, 1)], axis=0)
    idx = jnp.concatenate([rows, swap(rows, "core", 2, 1)], axis=0)
    scalars = [pos, idx, weight_table]

    w_own, w_core = call(
        prepare_kernel,
        [pos, jnp.transpose(w_qkv, (1, 0, 2))],
        1,
        [((64, COLS), BF)] * 2,
        grant=58,
        nbytes=MIB,
    )
    c_own, c_core, c_z = call(
        split_kernel,
        [pos, cotangent[0]],
        1,
        [((BLOCK, 256), BF)] * 2 + [((BLOCK, 512), BF)],
        grant=58,
        nbytes=MIB,
    )

    chunk = jnp.concatenate([w_own, swap(w_core, "core", 2, 1)], axis=0)
    near = [chunk] + [ring(chunk, 0, step) for step in (1, 2, 3)]
    mine = [jnp.concatenate(near[:2], axis=0), jnp.concatenate(near[2:], axis=0)]
    behind_low, ahead_high = ring(mine[0], 1, 3), ring(mine[1], 1, 1)
    far = [ring(behind_low, 1, 3), ring(ahead_high, 1, 1)]
    tok01 = behind(swap(inputs, "dp", 8, 1), behind_low, ahead_high, index=rows)
    ahead_low = ring(behind(mine[0], tok01), 1, 1)
    behind_high = ring(behind(mine[1], tok01), 1, 3)
    gathered = mine + [ahead_low, ahead_high, behind_low, behind_high] + far

    c_core = swap(c_core, "core", 2, 1)
    c_z = swap(behind(c_z, tok01), "dp", 8, 1)
    c_near, c_across = c_z[:, :256], swap(c_z[:, 256:], "core", 2, 1)
    tok10 = swap(inputs, "core", 2, 1)
    tok11 = swap(tok01, "core", 2, 1)
    toks = [inputs, tok01, tok10, tok11]

    tile = (HEAD, HEAD)
    qkv, cots, s1, x0, g1, m2, m3, m4, m5 = call(
        project_kernel,
        scalars + toks + [c_own, c_near, c_core, c_across] + gathered,
        3,
        [
            ((4, BLOCK, COLS), BF),
            ((4, BLOCK, 256), BF),
            ((4, 2) + tile, BF),
            ((2, 2) + tile, BF),
            ((4, 2) + tile, F32),
            ((2, 2) + tile, F32),
            ((2, 2) + tile, F32),
            ((2, 2) + tile, BF),
            ((2, 2) + tile, BF),
        ],
        scratch=[pltpu.VMEM((D, COLS), BF)],
        grant=58,
        flops=2 * 1024 * D * COLS,
        nbytes=10 * MIB,
    )

    cx = [swap(x0, "x", 4, mask) for mask in (1, 2, 3)]
    dy = [swap(m, "y", 4, mask) for mask, m in ((1, m4), (2, m5), (3, m5))]
    (loc,) = call(
        local_kernel,
        scalars + [qkv, cots],
        3,
        [((4, BLOCK, 1024), F32)],
        grant=12,
        flops=8 * 6 * 2 * BLOCK * BLOCK * HEAD,
        nbytes=8 * MIB,
    )
    x1 = add(x0, *cx)
    cy = [swap(x1, "y", 4, mask) for mask in (1, 2, 3)]
    high = dy[0].astype(F32) + dy[1].astype(F32) + dy[2].astype(F32)
    near = (high + m2).astype(BF)
    far = (high + m3).astype(BF)
    dx = [swap(m, "x", 4, mask) for mask, m in ((1, near), (2, far), (3, far))]

    attn, grads, low, high = call(
        finish_kernel,
        scalars + toks + [cots, qkv, loc, s1, g1] + cx + cy + [high.astype(BF)] + dx,
        3,
        [
            ((4, BLOCK, 256), BF),
            ((4, BLOCK, COLS), BF),
            ((2, 128, COLS), BF),
            ((2, 128, COLS), BF),
        ],
        grant=24,
        flops=1024 * D * COLS,
        nbytes=12 * MIB,
    )
    low, high = ring(low, 1, 3), ring(high, 1, 1)
    from_core = swap(attn[2:], "core", 2, 1)
    onward, backward = call(
        functools.partial(gradient_kernel, (1, 3)),
        [pos] + toks + [grads, from_core],
        1,
        [((4, 128, COLS), BF)] * 2,
        grant=20,
        flops=1024 * D * COLS,
        nbytes=9 * MIB,
        n_any=1,
    )
    onward = jnp.concatenate([add(onward[:2], low), onward[2:]], axis=0)
    backward = jnp.concatenate([backward[:2], add(backward[2:], high)], axis=0)
    onward, backward = ring(onward, 1, 3), ring(backward, 1, 1)
    back = swap(jnp.stack([attn[1], from_core[1]], axis=0), "dp", 8, 1)
    (own,) = call(
        functools.partial(gradient_kernel, (0,)),
        [pos] + toks + [grads, from_core],
        1,
        [((4, 128, COLS), BF)],
        grant=20,
        flops=1024 * 512 * COLS,
        nbytes=9 * MIB,
        n_any=1,
    )
    *total, attn_out = call(
        total_kernel,
        [pos, own, onward, backward, attn, from_core, back],
        1,
        [((128, COLS), BF)] * 4 + [((BLOCK, 1024), BF)],
        grant=10,
        nbytes=4 * MIB,
    )
    chip_sum = add(total[0], *[ring(total[step], 0, -step) for step in (1, 2, 3)])
    pair = jnp.stack([chip_sum[:64], swap(chip_sum[64:], "core", 2, 1)], axis=0)
    mine = add(pair[:, :32], same_set_neighbour(pair[:, 32:]))
    mine = add(mine, same_set_far(mine))
    near = same_set_neighbour(mine)
    theirs = swap(mine, "dp", 8, 1)
    beyond = swap(near, "dp", 8, 1)

    (grad_w,) = call(
        place_kernel,
        [pos, mine, near, theirs, beyond],
        1,
        [((3, 64, 1024), F32)],
        grant=6,
        nbytes=3 * MIB,
    )
    return attn_out[None], jnp.transpose(grad_w, (1, 0, 2))


def solution(mesh):
    grid = Mesh(mesh.devices.reshape(4, 4, 2, 8), ("y", "x", "core", "dp"))
    seq = ("y", "x", "core")
    return jax.shard_map(
        per_device,
        mesh=grid,
        in_specs=(P("dp", seq, None), P(seq, None, None), P(), P("dp", seq, None), P("dp", seq, None)),
        out_specs=(P("dp", seq, None), P(seq, None, None)),
        check_vma=False,
    )
```

```python
import functools
import math

import jax
import jax.numpy as jnp
from jax import lax
from jax.experimental import pallas as pl
from jax.experimental.pallas import tpu as pltpu
from jax.sharding import Mesh, PartitionSpec as P

BF = jnp.bfloat16
F32 = jnp.float32
HEAD = 128
QB = 128
BLOCK = 256
D = 2048
COLS = 768
MIB = 1024 * 1024
SETS = 0x66
HALVES = 0xB4


def ring(value, phase, step):
    pairs = []
    for y in range(4):
        for x in range(4):
            for core in range(2):
                at = (y, (x - step) % 4) if core == phase else ((y - step) % 4, x)
                pairs.append(((y * 4 + x) * 2 + core, (at[0] * 4 + at[1]) * 2 + core))
    return lax.ppermute(value, ("y", "x", "core"), pairs)


def swap(value, axis, size, mask):
    return lax.ppermute(value, axis, [(i, i ^ mask) for i in range(size)])


def same_set_neighbour(value):
    return lax.ppermute(value, "dp", [(z, (z + 1 if z % 2 else z - 1) % 8) for z in range(8)])


def same_set_far(value):
    return lax.ppermute(value, "dp", [(z, ((7 if SETS >> z & 1 else 3) - z) % 8) for z in range(8)])


def behind(value, *others, index=None):
    zero = sum(other[0, 0].astype(F32) for other in others) * 0.0
    if index is not None:
        zero = zero + (index[-1, -1] < 0).astype(F32)
    return (value.astype(F32) + zero).astype(value.dtype)


def dot(a, b, ca, cb):
    return lax.dot_general(a, b, (((ca,), (cb,)), ((), ())), preferred_element_type=F32)


def smem():
    return pl.BlockSpec(memory_space=pltpu.SMEM)


def vmem():
    return pl.BlockSpec(memory_space=pltpu.VMEM)


def call(kernel, args, n_smem, outs, scratch=(), grant=16, flops=0, nbytes=0, n_any=0):
    return pl.pallas_call(
        kernel,
        out_shape=[jax.ShapeDtypeStruct(*out) for out in outs],
        in_specs=[smem()] * n_smem
        + [vmem()] * (len(args) - n_smem - n_any)
        + [pl.BlockSpec(memory_space=pl.ANY)] * n_any,
        out_specs=[vmem()] * len(outs),
        scratch_shapes=list(scratch),
        compiler_params=pltpu.CompilerParams(vmem_limit_bytes=grant * MIB),
        cost_estimate=pl.CostEstimate(flops=flops, bytes_accessed=nbytes, transcendentals=0),
    )(*args)


def lanes(start):
    return pl.ds(pl.multiple_of(start, HEAD), HEAD)


def level_coef(pos, idx, table, blk, group, level, head):
    cs = blk // 2
    y, x, core = pos[0], pos[1], pos[2]
    row = idx[blk, group * 6 + level]
    lam = table[row, (core * 2 + pos[4]) * 2 + head]
    if level == 0:
        return lam * (1.0 / math.sqrt(HEAD * BLOCK))
    bit = [(core + cs) & 1, x & 1, (x >> 1) & 1, y & 1, (y >> 1) & 1][level - 1]
    return lam * bit.astype(F32) * (1.0 / math.sqrt(HEAD * 2 ** (level - 1) * BLOCK))


def prepare_kernel(pos, w, w_own, w_core):
    core, kind = pos[2], pos[4]
    mine = pl.multiple_of((core * 2 + kind) * 256, 256)
    other = pl.multiple_of(((1 - core) * 2 + kind) * 256, 256)
    for third in range(3):
        at = slice(third * 256, third * 256 + 256)
        w_own[:, at] = w[third, :, pl.ds(mine, 256)]
        w_core[:, at] = w[third, :, pl.ds(other, 256)]


def split_kernel(pos, cot, own, to_core, to_z):
    core, kind = pos[2], pos[4]

    def columns(cs, zs):
        group = ((core + cs) & 1) * 2 + ((kind + zs) & 1)
        return cot[:, pl.ds(pl.multiple_of(group * 256, 256), 256)]

    own[...] = columns(0, 0)
    to_core[...] = columns(1, 0)
    to_z[:, :256] = columns(0, 1)
    to_z[:, 256:] = columns(1, 1)


def project_kernel(pos, idx, table, t0, t1, t2, t3, c0, c1, c2, c3, *refs):
    toks = (t0, t1, t2, t3)
    parts = (refs[0:2], refs[2:4], refs[6:8], refs[4:6])
    qkv, cots, s1, x0, g1, m2, m3, m4, m5, w = refs[8:]
    y, x, core = pos[0], pos[1], pos[2]
    for slot in range(4):
        for dist in range(4):
            yy = (y + dist + core * (slot - dist)) & 3
            xx = (x + slot + core * (dist - slot)) & 3
            for cs in range(2):
                row = pl.multiple_of((yy * 4 + xx) * 128 + ((core + cs) & 1) * 64, 64)
                start = (slot % 2) * 128 + cs * 64
                w[pl.ds(row, 64), :] = parts[dist][slot // 2][start : start + 64, :]
    for blk, src in enumerate((c0, c1, c2, c3)):
        cots[blk] = src[...]

    @pl.loop(0, 3)
    def _(part):
        cols = pl.ds(pl.multiple_of(part * 256, 256), 256)
        for blk in range(4):
            qkv[blk, :, cols] = dot(toks[blk][...], w[:, cols], 1, 0).astype(BF)

    @pl.loop(0, 4)
    def _(step):
        zs, h = step // 2, step % 2
        total = None
        sums = [None] * 4
        for cs in range(2):
            blk = cs * 2 + zs
            state = dot(qkv[blk, :, lanes(256 + h * HEAD)], qkv[blk, :, lanes(512 + h * HEAD)], 0, 0)
            s1[blk, h] = state.astype(BF)
            total = state if total is None else total + state
            first = None
            for g in range(2):
                rows = slice(g * QB, g * QB + QB)
                outer = dot(qkv[blk, rows, lanes(h * HEAD)], cots[blk, rows, lanes(h * HEAD)], 0, 0)
                term = outer * level_coef(pos, idx, table, blk, g, 1, h)
                first = term if first is None else first + term
                for k in range(4):
                    term = outer * level_coef(pos, idx, table, blk, g, k + 2, h)
                    sums[k] = term if sums[k] is None else sums[k] + term
            g1[blk, h] = first
        x0[zs, h] = total.astype(BF)
        for out, value in zip((m2, m3, m4, m5), sums):
            out[zs, h] = value.astype(out.dtype)


def local_kernel(pos, idx, table, qkv, cots, loc):
    rows = lax.broadcasted_iota(jnp.int32, (BLOCK, BLOCK), 0)
    cols = lax.broadcasted_iota(jnp.int32, (BLOCK, BLOCK), 1)
    causal = rows >= cols
    upper = rows < QB

    @pl.loop(0, 4)
    def _(blk):
        for h in range(2):
            qs = slice(h * HEAD, h * HEAD + HEAD)
            ks = slice(256 + h * HEAD, 256 + h * HEAD + HEAD)
            vs = slice(512 + h * HEAD, 512 + h * HEAD + HEAD)
            q, k, v, c = qkv[blk, :, qs], qkv[blk, :, ks], qkv[blk, :, vs], cots[blk, :, qs]
            scale = jnp.where(
                upper,
                level_coef(pos, idx, table, blk, 0, 0, h),
                level_coef(pos, idx, table, blk, 1, 0, h),
            )
            scale = jnp.where(causal, scale, 0.0)
            scores = (dot(q, k, 1, 1) * scale).astype(BF)
            dscores = (dot(c, v, 1, 1) * scale).astype(BF)
            loc[blk, :, qs] = dot(dscores, k, 1, 0)
            loc[blk, :, ks] = dot(dscores, q, 0, 0)
            loc[blk, :, vs] = dot(scores, c, 0, 0)
            loc[blk, :, 768 + h * HEAD : 768 + h * HEAD + HEAD] = dot(scores, v, 1, 0)


def gradient_pair(pos, toks, grads, dist, first, store):
    y, x, core, half = pos[0], pos[1], pos[2], pos[5]
    at = []
    for slot in (first, first + 1):
        yy = (y + dist + core * (slot - dist)) & 3
        xx = (x + slot + core * (dist - slot)) & 3
        at.append(lanes((yy * 4 + xx) * 128))
    part = None
    for blk in range(4):
        rows = jnp.concatenate([toks[blk][:, at[0]], toks[blk][:, at[1]]], axis=1)
        term = dot(rows, grads[blk], 0, 0)
        part = term if part is None else part + term
    part = part.astype(BF)
    for sub in range(2):
        for c in range(2):
            for piece in range(2):
                row = ((c + core) & 1) * 64 + ((piece + half) & 1) * 32
                start = sub * 128 + c * 64 + piece * 32
                store(sub, pl.ds(pl.multiple_of(row, 32), 32), part[start : start + 32])


def finish_kernel(pos, idx, table, *refs):
    toks = refs[0:4]
    cots, qkv, loc, s1, g1 = refs[4:9]
    cx1, cx2, cx3, cy1, cy2, cy3 = refs[9:15]
    own, r1, r2, r3 = refs[15:19]
    attn, grads, low, high = refs[19:]

    @pl.loop(0, 4)
    def _(step):
        zs, h = step // 2, step % 2
        far = [
            None,
            cx1[zs, h].astype(F32),
            cx2[zs, h].astype(F32) + cx3[zs, h].astype(F32),
            cy1[zs, h].astype(F32),
            cy2[zs, h].astype(F32) + cy3[zs, h].astype(F32),
        ]
        chip = own[zs, h].astype(F32) + r1[zs, h].astype(F32)
        chip = chip + r2[zs, h].astype(F32) + r3[zs, h].astype(F32)
        qs, ks = lanes(h * HEAD), lanes(256 + h * HEAD)
        vs, ats = lanes(512 + h * HEAD), lanes(768 + h * HEAD)
        for cs in range(2):
            blk = cs * 2 + zs
            other = (1 - cs) * 2 + zs
            far[0] = s1[other, h].astype(F32)
            grad = (chip + g1[other, h]).astype(BF)
            for g in range(2):
                rows = slice(g * QB, g * QB + QB)
                mixed = None
                for level in range(1, 6):
                    term = far[level - 1] * level_coef(pos, idx, table, blk, g, level, h)
                    mixed = term if mixed is None else mixed + term
                mixed = mixed.astype(BF)
                out = loc[blk, rows, ats] + dot(qkv[blk, rows, qs], mixed, 1, 0)
                attn[blk, rows, qs] = out.astype(BF)
                dq = loc[blk, rows, qs] + dot(cots[blk, rows, qs], mixed, 1, 1)
                grads[blk, rows, qs] = dq.astype(BF)
            dk = loc[blk, :, ks] + dot(qkv[blk, :, vs], grad, 1, 1)
            grads[blk, :, ks] = dk.astype(BF)
            dv = loc[blk, :, vs] + dot(qkv[blk, :, ks], grad, 1, 0)
            grads[blk, :, vs] = dv.astype(BF)

    for first, out in ((0, low), (2, high)):

        def store(sub, rows, value, out=out):
            out[sub, rows, :] = value

        gradient_pair(pos, toks, grads, 2, first, store)


def gradient_kernel(dists, pos, t0, t1, t2, t3, grads, _, *outs):
    toks = (t0, t1, t2, t3)

    @pl.loop(0, 2)
    def _(pair):
        for dist, out in zip(dists, outs):

            def store(sub, rows, value, out=out):
                out[pair * 2 + sub, rows, :] = value

            gradient_pair(pos, toks, grads, dist, pair * 2, store)


def total_kernel(pos, own, r1, r2, attn, from_core, from_z, t0, t1, t2, t3, attn_out):
    core, kind = pos[2], pos[4]
    for slot, out in enumerate((t0, t1, t2, t3)):
        total = own[slot].astype(F32) + r1[slot].astype(F32) + r2[slot].astype(F32)
        out[...] = total.astype(BF)
    attns = ((attn.at[0], from_z.at[0]), (from_core.at[0], from_z.at[1]))
    for cs in range(2):
        for zs in range(2):
            group = ((core + cs) & 1) * 2 + ((kind + zs) & 1)
            attn_out[:, pl.ds(pl.multiple_of(group * 256, 256), 256)] = attns[cs][zs][...]


def place_kernel(pos, mine, near, theirs, beyond, grad_w):
    core, kind = pos[2], pos[4]
    halves = (pos[5], pos[6])
    for cs in range(2):
        for zs in range(2):
            group = ((core + cs) & 1) * 2 + ((kind + zs) & 1)
            lane = pl.ds(pl.multiple_of(group * 256, 256), 256)
            for piece in range(2):
                part = ((mine, near), (theirs, beyond))[zs][piece]
                row = pl.ds(pl.multiple_of(((halves[zs] + piece) & 1) * 32, 32), 32)
                for third in range(3):
                    grad_w[third, row, lane] = part[
                        cs, :, third * 256 : third * 256 + 256
                    ].astype(F32)


def add(*parts):
    total = parts[0].astype(F32)
    for part in parts[1:]:
        total = total + part.astype(F32)
    return total.astype(BF)


def per_device(tokens, w_qkv, weight_table, weight_index, cotangent):
    y, x, core = lax.axis_index("y"), lax.axis_index("x"), lax.axis_index("core")
    z = lax.axis_index("dp")
    pos = jnp.stack(
        [y, x, core, z, (SETS >> z) & 1, (HALVES >> z) & 1, (HALVES >> (z ^ 1)) & 1]
    ).astype(jnp.int32)
    inputs = tokens[0]

    rows = weight_index.reshape(1, 12)
    rows = jnp.concatenate([rows, swap(rows, "dp", 8, 1)], axis=0)
    idx = jnp.concatenate([rows, swap(rows, "core", 2, 1)], axis=0)
    scalars = [pos, idx, weight_table]

    w_own, w_core = call(
        prepare_kernel,
        [pos, jnp.transpose(w_qkv, (1, 0, 2))],
        1,
        [((64, COLS), BF)] * 2,
        grant=58,
        nbytes=MIB,
    )
    c_own, c_core, c_z = call(
        split_kernel,
        [pos, cotangent[0]],
        1,
        [((BLOCK, 256), BF)] * 2 + [((BLOCK, 512), BF)],
        grant=58,
        nbytes=MIB,
    )

    chunk = jnp.concatenate([w_own, swap(w_core, "core", 2, 1)], axis=0)
    near = [chunk] + [ring(chunk, 0, step) for step in (1, 2, 3)]
    mine = [jnp.concatenate(near[:2], axis=0), jnp.concatenate(near[2:], axis=0)]
    behind_low, ahead_high = ring(mine[0], 1, 3), ring(mine[1], 1, 1)
    far = [ring(behind_low, 1, 3), ring(ahead_high, 1, 1)]
    ahead_low, behind_high = ring(mine[0], 1, 1), ring(mine[1], 1, 3)
    gathered = mine + [ahead_low, ahead_high, behind_low, behind_high] + far

    c_core = swap(c_core, "core", 2, 1)
    c_z = swap(c_z, "dp", 8, 1)
    c_near, c_across = c_z[:, :256], swap(c_z[:, 256:], "core", 2, 1)
    tok10 = swap(inputs, "core", 2, 1)
    tok01 = behind(swap(inputs, "dp", 8, 1), c_across, *far, ahead_low, behind_high, index=idx)
    tok11 = swap(tok01, "core", 2, 1)
    toks = [inputs, tok01, tok10, tok11]

    tile = (HEAD, HEAD)
    qkv, cots, s1, x0, g1, m2, m3, m4, m5 = call(
        project_kernel,
        scalars + toks + [c_own, c_near, c_core, c_across] + gathered,
        3,
        [
            ((4, BLOCK, COLS), BF),
            ((4, BLOCK, 256), BF),
            ((4, 2) + tile, BF),
            ((2, 2) + tile, BF),
            ((4, 2) + tile, F32),
            ((2, 2) + tile, F32),
            ((2, 2) + tile, F32),
            ((2, 2) + tile, BF),
            ((2, 2) + tile, BF),
        ],
        scratch=[pltpu.VMEM((D, COLS), BF)],
        grant=52,
        flops=2 * 1024 * D * COLS,
        nbytes=10 * MIB,
    )

    cx = [swap(x0, "x", 4, mask) for mask in (1, 2, 3)]
    dy = [swap(m, "y", 4, mask) for mask, m in ((1, m4), (2, m5), (3, m5))]
    (loc,) = call(
        local_kernel,
        scalars + [qkv, cots],
        3,
        [((4, BLOCK, 1024), F32)],
        grant=12,
        flops=8 * 6 * 2 * BLOCK * BLOCK * HEAD,
        nbytes=8 * MIB,
    )
    x1 = add(x0, *cx)
    cy = [swap(x1, "y", 4, mask) for mask in (1, 2, 3)]
    high = dy[0].astype(F32) + dy[1].astype(F32) + dy[2].astype(F32)
    near = (high + m2).astype(BF)
    far = (high + m3).astype(BF)
    dx = [swap(m, "x", 4, mask) for mask, m in ((1, near), (2, far), (3, far))]

    attn, grads, low, high = call(
        finish_kernel,
        scalars + toks + [cots, qkv, loc, s1, g1] + cx + cy + [high.astype(BF)] + dx,
        3,
        [
            ((4, BLOCK, 256), BF),
            ((4, BLOCK, COLS), BF),
            ((2, 128, COLS), BF),
            ((2, 128, COLS), BF),
        ],
        grant=24,
        flops=1024 * D * COLS,
        nbytes=12 * MIB,
    )
    low, high = ring(low, 1, 3), ring(high, 1, 1)
    from_core = swap(attn[2:], "core", 2, 1)
    onward, backward = call(
        functools.partial(gradient_kernel, (1, 3)),
        [pos] + toks + [grads, from_core],
        1,
        [((4, 128, COLS), BF)] * 2,
        grant=20,
        flops=1024 * D * COLS,
        nbytes=9 * MIB,
        n_any=1,
    )
    onward = jnp.concatenate([add(onward[:2], low), onward[2:]], axis=0)
    backward = jnp.concatenate([backward[:2], add(backward[2:], high)], axis=0)
    onward, backward = ring(onward, 1, 3), ring(backward, 1, 1)
    back = swap(jnp.stack([attn[1], from_core[1]], axis=0), "dp", 8, 1)
    (own,) = call(
        functools.partial(gradient_kernel, (0,)),
        [pos] + toks + [grads, from_core],
        1,
        [((4, 128, COLS), BF)],
        grant=20,
        flops=1024 * 512 * COLS,
        nbytes=9 * MIB,
        n_any=1,
    )
    *total, attn_out = call(
        total_kernel,
        [pos, own, onward, backward, attn, from_core, back],
        1,
        [((128, COLS), BF)] * 4 + [((BLOCK, 1024), BF)],
        grant=10,
        nbytes=4 * MIB,
    )
    chip_sum = add(total[0], *[ring(total[step], 0, -step) for step in (1, 2, 3)])
    pair = jnp.stack([chip_sum[:64], swap(chip_sum[64:], "core", 2, 1)], axis=0)
    mine = add(pair[:, :32], same_set_neighbour(pair[:, 32:]))
    mine = add(mine, same_set_far(mine))
    near = same_set_neighbour(mine)
    theirs = swap(mine, "dp", 8, 1)
    beyond = swap(near, "dp", 8, 1)

    (grad_w,) = call(
        place_kernel,
        [pos, mine, near, theirs, beyond],
        1,
        [((3, 64, 1024), F32)],
        grant=6,
        nbytes=3 * MIB,
    )
    return attn_out[None], jnp.transpose(grad_w, (1, 0, 2))


def solution(mesh):
    grid = Mesh(mesh.devices.reshape(4, 4, 2, 8), ("y", "x", "core", "dp"))
    seq = ("y", "x", "core")
    return jax.shard_map(
        per_device,
        mesh=grid,
        in_specs=(P("dp", seq, None), P(seq, None, None), P(), P("dp", seq, None), P("dp", seq, None)),
        out_specs=(P("dp", seq, None), P(seq, None, None)),
        check_vma=False,
    )
```

```python
import functools
import math

import jax
import jax.numpy as jnp
from jax import lax
from jax.experimental import pallas as pl
from jax.experimental.pallas import tpu as pltpu
from jax.sharding import Mesh, PartitionSpec as P

BF = jnp.bfloat16
F32 = jnp.float32
HEAD = 128
QB = 128
BLOCK = 256
D = 2048
COLS = 768
MIB = 1024 * 1024
SETS = 0x66
HALVES = 0xB4


def ring(value, phase, step):
    pairs = []
    for y in range(4):
        for x in range(4):
            for core in range(2):
                at = (y, (x - step) % 4) if core == phase else ((y - step) % 4, x)
                pairs.append(((y * 4 + x) * 2 + core, (at[0] * 4 + at[1]) * 2 + core))
    return lax.ppermute(value, ("y", "x", "core"), pairs)


def swap(value, axis, size, mask):
    return lax.ppermute(value, axis, [(i, i ^ mask) for i in range(size)])


def same_set_neighbour(value):
    return lax.ppermute(value, "dp", [(z, (z + 1 if z % 2 else z - 1) % 8) for z in range(8)])


def same_set_far(value):
    return lax.ppermute(value, "dp", [(z, ((7 if SETS >> z & 1 else 3) - z) % 8) for z in range(8)])


def behind(value, *others, index=None):
    zero = sum([other[0, 0].astype(F32) for other in others], jnp.zeros((), F32)) * 0.0
    if index is not None:
        zero = zero + (index[-1, -1] < 0).astype(F32)
    return (value.astype(F32) + zero).astype(value.dtype)


def dot(a, b, ca, cb):
    return lax.dot_general(a, b, (((ca,), (cb,)), ((), ())), preferred_element_type=F32)


def smem():
    return pl.BlockSpec(memory_space=pltpu.SMEM)


def vmem():
    return pl.BlockSpec(memory_space=pltpu.VMEM)


def call(kernel, args, n_smem, outs, scratch=(), grant=16, flops=0, nbytes=0, n_any=0):
    return pl.pallas_call(
        kernel,
        out_shape=[jax.ShapeDtypeStruct(*out) for out in outs],
        in_specs=[smem()] * n_smem
        + [vmem()] * (len(args) - n_smem - n_any)
        + [pl.BlockSpec(memory_space=pl.ANY)] * n_any,
        out_specs=[vmem()] * len(outs),
        scratch_shapes=list(scratch),
        compiler_params=pltpu.CompilerParams(vmem_limit_bytes=grant * MIB),
        cost_estimate=pl.CostEstimate(flops=flops, bytes_accessed=nbytes, transcendentals=0),
    )(*args)


def lanes(start):
    return pl.ds(pl.multiple_of(start, HEAD), HEAD)


def level_coef(pos, idx, table, blk, group, level, head):
    cs = blk // 2
    y, x, core = pos[0], pos[1], pos[2]
    row = idx[blk, group * 6 + level]
    lam = table[row, (core * 2 + pos[4]) * 2 + head]
    if level == 0:
        return lam * (1.0 / math.sqrt(HEAD * BLOCK))
    bit = [(core + cs) & 1, x & 1, (x >> 1) & 1, y & 1, (y >> 1) & 1][level - 1]
    return lam * bit.astype(F32) * (1.0 / math.sqrt(HEAD * 2 ** (level - 1) * BLOCK))


def prepare_kernel(pos, w, w_own, w_core):
    core, kind = pos[2], pos[4]
    mine = pl.multiple_of((core * 2 + kind) * 256, 256)
    other = pl.multiple_of(((1 - core) * 2 + kind) * 256, 256)
    for third in range(3):
        at = slice(third * 256, third * 256 + 256)
        w_own[:, at] = w[third, :, pl.ds(mine, 256)]
        w_core[:, at] = w[third, :, pl.ds(other, 256)]


def split_kernel(pos, cot, own, to_core, to_z):
    core, kind = pos[2], pos[4]

    def columns(cs, zs):
        group = ((core + cs) & 1) * 2 + ((kind + zs) & 1)
        return cot[:, pl.ds(pl.multiple_of(group * 256, 256), 256)]

    own[...] = columns(0, 0)
    to_core[...] = columns(1, 0)
    to_z[:, :256] = columns(0, 1)
    to_z[:, 256:] = columns(1, 1)


def project_kernel(pos, idx, table, t0, t1, t2, t3, c0, c1, c2, c3, *refs):
    toks = (t0, t1, t2, t3)
    parts = (refs[0:2], refs[2:4], refs[6:8], refs[4:6])
    qkv, cots, s1, x0, g1, m2, m3, m4, m5, w = refs[8:]
    y, x, core = pos[0], pos[1], pos[2]
    for slot in range(4):
        for dist in range(4):
            yy = (y + dist + core * (slot - dist)) & 3
            xx = (x + slot + core * (dist - slot)) & 3
            for cs in range(2):
                row = pl.multiple_of((yy * 4 + xx) * 128 + ((core + cs) & 1) * 64, 64)
                start = (slot % 2) * 128 + cs * 64
                w[pl.ds(row, 64), :] = parts[dist][slot // 2][start : start + 64, :]
    for blk, src in enumerate((c0, c1, c2, c3)):
        cots[blk] = src[...]

    @pl.loop(0, 3)
    def _(part):
        cols = pl.ds(pl.multiple_of(part * 256, 256), 256)
        for blk in range(4):
            qkv[blk, :, cols] = dot(toks[blk][...], w[:, cols], 1, 0).astype(BF)

    @pl.loop(0, 4)
    def _(step):
        zs, h = step // 2, step % 2
        total = None
        sums = [None] * 4
        for cs in range(2):
            blk = cs * 2 + zs
            state = dot(qkv[blk, :, lanes(256 + h * HEAD)], qkv[blk, :, lanes(512 + h * HEAD)], 0, 0)
            s1[blk, h] = state.astype(BF)
            total = state if total is None else total + state
            first = None
            for g in range(2):
                rows = slice(g * QB, g * QB + QB)
                outer = dot(qkv[blk, rows, lanes(h * HEAD)], cots[blk, rows, lanes(h * HEAD)], 0, 0)
                term = outer * level_coef(pos, idx, table, blk, g, 1, h)
                first = term if first is None else first + term
                for k in range(4):
                    term = outer * level_coef(pos, idx, table, blk, g, k + 2, h)
                    sums[k] = term if sums[k] is None else sums[k] + term
            g1[blk, h] = first
        x0[zs, h] = total.astype(BF)
        for out, value in zip((m2, m3, m4, m5), sums):
            out[zs, h] = value.astype(out.dtype)


def local_kernel(pos, idx, table, qkv, cots, loc):
    rows = lax.broadcasted_iota(jnp.int32, (BLOCK, BLOCK), 0)
    cols = lax.broadcasted_iota(jnp.int32, (BLOCK, BLOCK), 1)
    causal = rows >= cols
    upper = rows < QB

    @pl.loop(0, 4)
    def _(blk):
        for h in range(2):
            qs = slice(h * HEAD, h * HEAD + HEAD)
            ks = slice(256 + h * HEAD, 256 + h * HEAD + HEAD)
            vs = slice(512 + h * HEAD, 512 + h * HEAD + HEAD)
            q, k, v, c = qkv[blk, :, qs], qkv[blk, :, ks], qkv[blk, :, vs], cots[blk, :, qs]
            scale = jnp.where(
                upper,
                level_coef(pos, idx, table, blk, 0, 0, h),
                level_coef(pos, idx, table, blk, 1, 0, h),
            )
            scale = jnp.where(causal, scale, 0.0)
            scores = (dot(q, k, 1, 1) * scale).astype(BF)
            dscores = (dot(c, v, 1, 1) * scale).astype(BF)
            loc[blk, :, qs] = dot(dscores, k, 1, 0)
            loc[blk, :, ks] = dot(dscores, q, 0, 0)
            loc[blk, :, vs] = dot(scores, c, 0, 0)
            loc[blk, :, 768 + h * HEAD : 768 + h * HEAD + HEAD] = dot(scores, v, 1, 0)


def gradient_pair(pos, toks, grads, dist, first, store):
    y, x, core, half = pos[0], pos[1], pos[2], pos[5]
    at = []
    for slot in (first, first + 1):
        yy = (y + dist + core * (slot - dist)) & 3
        xx = (x + slot + core * (dist - slot)) & 3
        at.append(lanes((yy * 4 + xx) * 128))
    part = None
    for blk in range(4):
        rows = jnp.concatenate([toks[blk][:, at[0]], toks[blk][:, at[1]]], axis=1)
        term = dot(rows, grads[blk], 0, 0)
        part = term if part is None else part + term
    part = part.astype(BF)
    for sub in range(2):
        for c in range(2):
            for piece in range(2):
                row = ((c + core) & 1) * 64 + ((piece + half) & 1) * 32
                start = sub * 128 + c * 64 + piece * 32
                store(sub, pl.ds(pl.multiple_of(row, 32), 32), part[start : start + 32])


def finish_kernel(pos, idx, table, *refs):
    toks = refs[0:4]
    cots, qkv, loc, s1, g1 = refs[4:9]
    cx1, cx2, cx3, cy1, cy2, cy3 = refs[9:15]
    own, r1, r2, r3 = refs[15:19]
    attn, grads, low, high = refs[19:]

    @pl.loop(0, 4)
    def _(step):
        zs, h = step // 2, step % 2
        far = [
            None,
            cx1[zs, h].astype(F32),
            cx2[zs, h].astype(F32) + cx3[zs, h].astype(F32),
            cy1[zs, h].astype(F32),
            cy2[zs, h].astype(F32) + cy3[zs, h].astype(F32),
        ]
        chip = own[zs, h].astype(F32) + r1[zs, h].astype(F32)
        chip = chip + r2[zs, h].astype(F32) + r3[zs, h].astype(F32)
        qs, ks = lanes(h * HEAD), lanes(256 + h * HEAD)
        vs, ats = lanes(512 + h * HEAD), lanes(768 + h * HEAD)
        for cs in range(2):
            blk = cs * 2 + zs
            other = (1 - cs) * 2 + zs
            far[0] = s1[other, h].astype(F32)
            grad = (chip + g1[other, h]).astype(BF)
            for g in range(2):
                rows = slice(g * QB, g * QB + QB)
                mixed = None
                for level in range(1, 6):
                    term = far[level - 1] * level_coef(pos, idx, table, blk, g, level, h)
                    mixed = term if mixed is None else mixed + term
                mixed = mixed.astype(BF)
                out = loc[blk, rows, ats] + dot(qkv[blk, rows, qs], mixed, 1, 0)
                attn[blk, rows, qs] = out.astype(BF)
                dq = loc[blk, rows, qs] + dot(cots[blk, rows, qs], mixed, 1, 1)
                grads[blk, rows, qs] = dq.astype(BF)
            dk = loc[blk, :, ks] + dot(qkv[blk, :, vs], grad, 1, 1)
            grads[blk, :, ks] = dk.astype(BF)
            dv = loc[blk, :, vs] + dot(qkv[blk, :, ks], grad, 1, 0)
            grads[blk, :, vs] = dv.astype(BF)

    for first, out in ((0, low), (2, high)):

        def store(sub, rows, value, out=out):
            out[sub, rows, :] = value

        gradient_pair(pos, toks, grads, 2, first, store)


def gradient_kernel(dists, pos, t0, t1, t2, t3, grads, _, *outs):
    toks = (t0, t1, t2, t3)

    @pl.loop(0, 2)
    def _(pair):
        for dist, out in zip(dists, outs):

            def store(sub, rows, value, out=out):
                out[pair * 2 + sub, rows, :] = value

            gradient_pair(pos, toks, grads, dist, pair * 2, store)


def total_kernel(pos, own, r1, r2, attn, from_core, from_z, t0, t1, t2, t3, attn_out):
    core, kind = pos[2], pos[4]
    for slot, out in enumerate((t0, t1, t2, t3)):
        total = own[slot].astype(F32) + r1[slot].astype(F32) + r2[slot].astype(F32)
        out[...] = total.astype(BF)
    attns = ((attn.at[0], from_z.at[0]), (from_core.at[0], from_z.at[1]))
    for cs in range(2):
        for zs in range(2):
            group = ((core + cs) & 1) * 2 + ((kind + zs) & 1)
            attn_out[:, pl.ds(pl.multiple_of(group * 256, 256), 256)] = attns[cs][zs][...]


def place_kernel(pos, mine, near, theirs, beyond, grad_w):
    core, kind = pos[2], pos[4]
    halves = (pos[5], pos[6])
    for cs in range(2):
        for zs in range(2):
            group = ((core + cs) & 1) * 2 + ((kind + zs) & 1)
            lane = pl.ds(pl.multiple_of(group * 256, 256), 256)
            for piece in range(2):
                part = ((mine, near), (theirs, beyond))[zs][piece]
                row = pl.ds(pl.multiple_of(((halves[zs] + piece) & 1) * 32, 32), 32)
                for third in range(3):
                    grad_w[third, row, lane] = part[
                        cs, :, third * 256 : third * 256 + 256
                    ].astype(F32)


def add(*parts):
    total = parts[0].astype(F32)
    for part in parts[1:]:
        total = total + part.astype(F32)
    return total.astype(BF)


def per_device(tokens, w_qkv, weight_table, weight_index, cotangent):
    y, x, core = lax.axis_index("y"), lax.axis_index("x"), lax.axis_index("core")
    z = lax.axis_index("dp")
    pos = jnp.stack(
        [y, x, core, z, (SETS >> z) & 1, (HALVES >> z) & 1, (HALVES >> (z ^ 1)) & 1]
    ).astype(jnp.int32)
    inputs = tokens[0]

    rows = weight_index.reshape(1, 12)
    rows = jnp.concatenate([rows, swap(rows, "dp", 8, 1)], axis=0)
    idx = jnp.concatenate([rows, swap(rows, "core", 2, 1)], axis=0)
    scalars = [pos, idx, weight_table]

    w_own, w_core = call(
        prepare_kernel,
        [pos, jnp.transpose(w_qkv, (1, 0, 2))],
        1,
        [((64, COLS), BF)] * 2,
        grant=58,
        nbytes=MIB,
    )
    c_own, c_core, c_z = call(
        split_kernel,
        [pos, cotangent[0]],
        1,
        [((BLOCK, 256), BF)] * 2 + [((BLOCK, 512), BF)],
        grant=58,
        nbytes=MIB,
    )

    chunk = jnp.concatenate([w_own, swap(w_core, "core", 2, 1)], axis=0)
    near = [chunk] + [ring(chunk, 0, step) for step in (1, 2, 3)]
    mine = [jnp.concatenate(near[:2], axis=0), jnp.concatenate(near[2:], axis=0)]
    behind_low, ahead_high = ring(mine[0], 1, 3), ring(mine[1], 1, 1)
    far = [ring(behind_low, 1, 3), ring(ahead_high, 1, 1)]
    ahead_low, behind_high = ring(mine[0], 1, 1), ring(mine[1], 1, 3)
    gathered = mine + [ahead_low, ahead_high, behind_low, behind_high] + far

    c_core = swap(c_core, "core", 2, 1)
    c_z = swap(c_z, "dp", 8, 1)
    c_near, c_across = c_z[:, :256], swap(c_z[:, 256:], "core", 2, 1)
    own = behind(inputs, index=rows)
    tok01 = behind(swap(own, "dp", 8, 1), c_across, *far, ahead_low, behind_high)
    tok10, tok11 = swap(own, "core", 2, 1), swap(tok01, "core", 2, 1)
    toks = [own, tok01, tok10, tok11]

    tile = (HEAD, HEAD)
    qkv, cots, s1, x0, g1, m2, m3, m4, m5 = call(
        project_kernel,
        scalars + toks + [c_own, c_near, c_core, c_across] + gathered,
        3,
        [
            ((4, BLOCK, COLS), BF),
            ((4, BLOCK, 256), BF),
            ((4, 2) + tile, BF),
            ((2, 2) + tile, BF),
            ((4, 2) + tile, F32),
            ((2, 2) + tile, F32),
            ((2, 2) + tile, F32),
            ((2, 2) + tile, BF),
            ((2, 2) + tile, BF),
        ],
        scratch=[pltpu.VMEM((D, COLS), BF)],
        grant=52,
        flops=2 * 1024 * D * COLS,
        nbytes=10 * MIB,
    )

    cx = [swap(x0, "x", 4, mask) for mask in (1, 2, 3)]
    dy = [swap(m, "y", 4, mask) for mask, m in ((1, m4), (2, m5), (3, m5))]
    (loc,) = call(
        local_kernel,
        scalars + [qkv, cots],
        3,
        [((4, BLOCK, 1024), F32)],
        grant=12,
        flops=8 * 6 * 2 * BLOCK * BLOCK * HEAD,
        nbytes=8 * MIB,
    )
    x1 = add(x0, *cx)
    cy = [swap(x1, "y", 4, mask) for mask in (1, 2, 3)]
    high = dy[0].astype(F32) + dy[1].astype(F32) + dy[2].astype(F32)
    near = (high + m2).astype(BF)
    far = (high + m3).astype(BF)
    dx = [swap(m, "x", 4, mask) for mask, m in ((1, near), (2, far), (3, far))]

    attn, grads, low, high = call(
        finish_kernel,
        scalars + toks + [cots, qkv, loc, s1, g1] + cx + cy + [high.astype(BF)] + dx,
        3,
        [
            ((4, BLOCK, 256), BF),
            ((4, BLOCK, COLS), BF),
            ((2, 128, COLS), BF),
            ((2, 128, COLS), BF),
        ],
        grant=24,
        flops=1024 * D * COLS,
        nbytes=12 * MIB,
    )
    low, high = ring(low, 1, 3), ring(high, 1, 1)
    from_core = swap(attn[2:], "core", 2, 1)
    onward, backward = call(
        functools.partial(gradient_kernel, (1, 3)),
        [pos] + toks + [grads, from_core],
        1,
        [((4, 128, COLS), BF)] * 2,
        grant=20,
        flops=1024 * D * COLS,
        nbytes=9 * MIB,
        n_any=1,
    )
    onward = jnp.concatenate([add(onward[:2], low), onward[2:]], axis=0)
    backward = jnp.concatenate([backward[:2], add(backward[2:], high)], axis=0)
    onward, backward = ring(onward, 1, 3), ring(backward, 1, 1)
    back = swap(jnp.stack([attn[1], from_core[1]], axis=0), "dp", 8, 1)
    (own,) = call(
        functools.partial(gradient_kernel, (0,)),
        [pos] + toks + [grads, from_core],
        1,
        [((4, 128, COLS), BF)],
        grant=20,
        flops=1024 * 512 * COLS,
        nbytes=9 * MIB,
        n_any=1,
    )
    *total, attn_out = call(
        total_kernel,
        [pos, own, onward, backward, attn, from_core, back],
        1,
        [((128, COLS), BF)] * 4 + [((BLOCK, 1024), BF)],
        grant=10,
        nbytes=4 * MIB,
    )
    chip_sum = add(total[0], *[ring(total[step], 0, -step) for step in (1, 2, 3)])
    pair = jnp.stack([chip_sum[:64], swap(chip_sum[64:], "core", 2, 1)], axis=0)
    mine = add(pair[:, :32], same_set_neighbour(pair[:, 32:]))
    mine = add(mine, same_set_far(mine))
    near = same_set_neighbour(mine)
    theirs = swap(mine, "dp", 8, 1)
    beyond = swap(near, "dp", 8, 1)

    (grad_w,) = call(
        place_kernel,
        [pos, mine, near, theirs, beyond],
        1,
        [((3, 64, 1024), F32)],
        grant=6,
        nbytes=3 * MIB,
    )
    return attn_out[None], jnp.transpose(grad_w, (1, 0, 2))


def solution(mesh):
    grid = Mesh(mesh.devices.reshape(4, 4, 2, 8), ("y", "x", "core", "dp"))
    seq = ("y", "x", "core")
    return jax.shard_map(
        per_device,
        mesh=grid,
        in_specs=(P("dp", seq, None), P(seq, None, None), P(), P("dp", seq, None), P("dp", seq, None)),
        out_specs=(P("dp", seq, None), P(seq, None, None)),
        check_vma=False,
    )
```

```python
import functools
import math

import jax
import jax.numpy as jnp
from jax import lax
from jax.experimental import pallas as pl
from jax.experimental.pallas import tpu as pltpu
from jax.sharding import Mesh, PartitionSpec as P

BF = jnp.bfloat16
F32 = jnp.float32
HEAD = 128
QB = 128
BLOCK = 256
D = 2048
COLS = 768
MIB = 1024 * 1024
SETS = 0x66
HALVES = 0xB4


def ring(value, phase, step):
    pairs = []
    for y in range(4):
        for x in range(4):
            for core in range(2):
                at = (y, (x - step) % 4) if core == phase else ((y - step) % 4, x)
                pairs.append(((y * 4 + x) * 2 + core, (at[0] * 4 + at[1]) * 2 + core))
    return lax.ppermute(value, ("y", "x", "core"), pairs)


def swap(value, axis, size, mask):
    return lax.ppermute(value, axis, [(i, i ^ mask) for i in range(size)])


def same_set_neighbour(value):
    return lax.ppermute(value, "dp", [(z, (z + 1 if z % 2 else z - 1) % 8) for z in range(8)])


def same_set_far(value):
    return lax.ppermute(value, "dp", [(z, ((7 if SETS >> z & 1 else 3) - z) % 8) for z in range(8)])


def behind(value, *others, index=None):
    zero = sum([other[0, 0].astype(F32) for other in others], jnp.zeros((), F32)) * 0.0
    if index is not None:
        zero = zero + (index[-1, -1] < 0).astype(F32)
    return (value.astype(F32) + zero).astype(value.dtype)


def dot(a, b, ca, cb):
    return lax.dot_general(a, b, (((ca,), (cb,)), ((), ())), preferred_element_type=F32)


def smem():
    return pl.BlockSpec(memory_space=pltpu.SMEM)


def vmem():
    return pl.BlockSpec(memory_space=pltpu.VMEM)


def call(kernel, args, n_smem, outs, scratch=(), grant=16, flops=0, nbytes=0, n_any=0):
    return pl.pallas_call(
        kernel,
        out_shape=[jax.ShapeDtypeStruct(*out) for out in outs],
        in_specs=[smem()] * n_smem
        + [vmem()] * (len(args) - n_smem - n_any)
        + [pl.BlockSpec(memory_space=pl.ANY)] * n_any,
        out_specs=[vmem()] * len(outs),
        scratch_shapes=list(scratch),
        compiler_params=pltpu.CompilerParams(vmem_limit_bytes=grant * MIB),
        cost_estimate=pl.CostEstimate(flops=flops, bytes_accessed=nbytes, transcendentals=0),
    )(*args)


def lanes(start):
    return pl.ds(pl.multiple_of(start, HEAD), HEAD)


def level_coef(pos, idx, table, blk, group, level, head):
    cs = blk // 2
    y, x, core = pos[0], pos[1], pos[2]
    row = idx[blk, group * 6 + level]
    lam = table[row, (core * 2 + pos[4]) * 2 + head]
    if level == 0:
        return lam * (1.0 / math.sqrt(HEAD * BLOCK))
    bit = [(core + cs) & 1, x & 1, (x >> 1) & 1, y & 1, (y >> 1) & 1][level - 1]
    return lam * bit.astype(F32) * (1.0 / math.sqrt(HEAD * 2 ** (level - 1) * BLOCK))


def prepare_kernel(pos, w, cot, w_own, w_core, own, to_core, to_z):
    core, kind = pos[2], pos[4]

    def columns(cs, zs):
        group = ((core + cs) & 1) * 2 + ((kind + zs) & 1)
        return pl.ds(pl.multiple_of(group * 256, 256), 256)

    for third in range(3):
        at = slice(third * 256, third * 256 + 256)
        w_own[:, at] = w[third, :, columns(0, 0)]
        w_core[:, at] = w[third, :, columns(1, 0)]
    own[...] = cot[:, columns(0, 0)]
    to_core[...] = cot[:, columns(1, 0)]
    to_z[:, :256] = cot[:, columns(0, 1)]
    to_z[:, 256:] = cot[:, columns(1, 1)]


def project_kernel(pos, idx, table, c0, c1, c2, c3, *refs):
    parts = (refs[0:2], refs[2:4], refs[6:8], refs[4:6])
    qkv, cots, s1, x0, g1, m2, m3, m4, m5, w, toks, sems = refs[12:]
    y, x, core = pos[0], pos[1], pos[2]
    copies = [pltpu.make_async_copy(refs[8 + b], toks.at[b], sems.at[b]) for b in range(4)]
    for copy in copies:
        copy.start()
    for slot in range(4):
        for dist in range(4):
            yy = (y + dist + core * (slot - dist)) & 3
            xx = (x + slot + core * (dist - slot)) & 3
            for cs in range(2):
                row = pl.multiple_of((yy * 4 + xx) * 128 + ((core + cs) & 1) * 64, 64)
                start = (slot % 2) * 128 + cs * 64
                w[pl.ds(row, 64), :] = parts[dist][slot // 2][start : start + 64, :]
    for blk, src in enumerate((c0, c1, c2, c3)):
        cots[blk] = src[...]

    for blk in range(4):
        copies[blk].wait()

        @pl.loop(0, 3)
        def _(part, blk=blk):
            cols = pl.ds(pl.multiple_of(part * 256, 256), 256)
            qkv[blk, :, cols] = dot(toks[blk], w[:, cols], 1, 0).astype(BF)

    @pl.loop(0, 4)
    def _(step):
        zs, h = step // 2, step % 2
        total = None
        sums = [None] * 4
        for cs in range(2):
            blk = cs * 2 + zs
            state = dot(qkv[blk, :, lanes(256 + h * HEAD)], qkv[blk, :, lanes(512 + h * HEAD)], 0, 0)
            s1[blk, h] = state.astype(BF)
            total = state if total is None else total + state
            first = None
            for g in range(2):
                rows = slice(g * QB, g * QB + QB)
                outer = dot(qkv[blk, rows, lanes(h * HEAD)], cots[blk, rows, lanes(h * HEAD)], 0, 0)
                term = outer * level_coef(pos, idx, table, blk, g, 1, h)
                first = term if first is None else first + term
                for k in range(4):
                    term = outer * level_coef(pos, idx, table, blk, g, k + 2, h)
                    sums[k] = term if sums[k] is None else sums[k] + term
            g1[blk, h] = first
        x0[zs, h] = total.astype(BF)
        for out, value in zip((m2, m3, m4, m5), sums):
            out[zs, h] = value.astype(out.dtype)


def local_kernel(pos, idx, table, qkv, cots, loc):
    rows = lax.broadcasted_iota(jnp.int32, (BLOCK, BLOCK), 0)
    cols = lax.broadcasted_iota(jnp.int32, (BLOCK, BLOCK), 1)
    causal = rows >= cols
    upper = rows < QB

    @pl.loop(0, 4)
    def _(blk):
        for h in range(2):
            qs = slice(h * HEAD, h * HEAD + HEAD)
            ks = slice(256 + h * HEAD, 256 + h * HEAD + HEAD)
            vs = slice(512 + h * HEAD, 512 + h * HEAD + HEAD)
            q, k, v, c = qkv[blk, :, qs], qkv[blk, :, ks], qkv[blk, :, vs], cots[blk, :, qs]
            scale = jnp.where(
                upper,
                level_coef(pos, idx, table, blk, 0, 0, h),
                level_coef(pos, idx, table, blk, 1, 0, h),
            )
            scale = jnp.where(causal, scale, 0.0)
            scores = (dot(q, k, 1, 1) * scale).astype(BF)
            dscores = (dot(c, v, 1, 1) * scale).astype(BF)
            loc[blk, :, qs] = dot(dscores, k, 1, 0)
            loc[blk, :, ks] = dot(dscores, q, 0, 0)
            loc[blk, :, vs] = dot(scores, c, 0, 0)
            loc[blk, :, 768 + h * HEAD : 768 + h * HEAD + HEAD] = dot(scores, v, 1, 0)


def gradient_pair(pos, toks, grads, dist, first, store):
    y, x, core, half = pos[0], pos[1], pos[2], pos[5]
    at = []
    for slot in (first, first + 1):
        yy = (y + dist + core * (slot - dist)) & 3
        xx = (x + slot + core * (dist - slot)) & 3
        at.append(lanes((yy * 4 + xx) * 128))
    part = None
    for blk in range(4):
        rows = jnp.concatenate([toks[blk][:, at[0]], toks[blk][:, at[1]]], axis=1)
        term = dot(rows, grads[blk], 0, 0)
        part = term if part is None else part + term
    part = part.astype(BF)
    for sub in range(2):
        for c in range(2):
            for piece in range(2):
                row = ((c + core) & 1) * 64 + ((piece + half) & 1) * 32
                start = sub * 128 + c * 64 + piece * 32
                store(sub, pl.ds(pl.multiple_of(row, 32), 32), part[start : start + 32])


def finish_kernel(pos, idx, table, *refs):
    toks = refs[0:4]
    cots, qkv, loc, s1, g1 = refs[4:9]
    cx1, cx2, cx3, cy1, cy2, cy3 = refs[9:15]
    own, r1, r2, r3 = refs[15:19]
    attn, grads, low, high = refs[19:]

    @pl.loop(0, 4)
    def _(step):
        zs, h = step // 2, step % 2
        far = [
            None,
            cx1[zs, h].astype(F32),
            cx2[zs, h].astype(F32) + cx3[zs, h].astype(F32),
            cy1[zs, h].astype(F32),
            cy2[zs, h].astype(F32) + cy3[zs, h].astype(F32),
        ]
        chip = own[zs, h].astype(F32) + r1[zs, h].astype(F32)
        chip = chip + r2[zs, h].astype(F32) + r3[zs, h].astype(F32)
        qs, ks = lanes(h * HEAD), lanes(256 + h * HEAD)
        vs, ats = lanes(512 + h * HEAD), lanes(768 + h * HEAD)
        for cs in range(2):
            blk = cs * 2 + zs
            other = (1 - cs) * 2 + zs
            far[0] = s1[other, h].astype(F32)
            grad = (chip + g1[other, h]).astype(BF)
            for g in range(2):
                rows = slice(g * QB, g * QB + QB)
                mixed = None
                for level in range(1, 6):
                    term = far[level - 1] * level_coef(pos, idx, table, blk, g, level, h)
                    mixed = term if mixed is None else mixed + term
                mixed = mixed.astype(BF)
                out = loc[blk, rows, ats] + dot(qkv[blk, rows, qs], mixed, 1, 0)
                attn[blk, rows, qs] = out.astype(BF)
                dq = loc[blk, rows, qs] + dot(cots[blk, rows, qs], mixed, 1, 1)
                grads[blk, rows, qs] = dq.astype(BF)
            dk = loc[blk, :, ks] + dot(qkv[blk, :, vs], grad, 1, 1)
            grads[blk, :, ks] = dk.astype(BF)
            dv = loc[blk, :, vs] + dot(qkv[blk, :, ks], grad, 1, 0)
            grads[blk, :, vs] = dv.astype(BF)

    for first, out in ((0, low), (2, high)):

        def store(sub, rows, value, out=out):
            out[sub, rows, :] = value

        gradient_pair(pos, toks, grads, 2, first, store)


def gradient_kernel(dists, pos, t0, t1, t2, t3, grads, _, *outs):
    toks = (t0, t1, t2, t3)

    @pl.loop(0, 2)
    def _(pair):
        for dist, out in zip(dists, outs):

            def store(sub, rows, value, out=out):
                out[pair * 2 + sub, rows, :] = value

            gradient_pair(pos, toks, grads, dist, pair * 2, store)


def total_kernel(pos, own, r1, r2, attn, from_core, from_z, t0, t1, t2, t3, attn_out):
    core, kind = pos[2], pos[4]
    for slot, out in enumerate((t0, t1, t2, t3)):
        total = own[slot].astype(F32) + r1[slot].astype(F32) + r2[slot].astype(F32)
        out[...] = total.astype(BF)
    attns = ((attn.at[0], from_z.at[0]), (from_core.at[0], from_z.at[1]))
    for cs in range(2):
        for zs in range(2):
            group = ((core + cs) & 1) * 2 + ((kind + zs) & 1)
            attn_out[:, pl.ds(pl.multiple_of(group * 256, 256), 256)] = attns[cs][zs][...]


def place_kernel(pos, mine, near, theirs, beyond, grad_w):
    core, kind = pos[2], pos[4]
    halves = (pos[5], pos[6])
    for cs in range(2):
        for zs in range(2):
            group = ((core + cs) & 1) * 2 + ((kind + zs) & 1)
            lane = pl.ds(pl.multiple_of(group * 256, 256), 256)
            for piece in range(2):
                part = ((mine, near), (theirs, beyond))[zs][piece]
                row = pl.ds(pl.multiple_of(((halves[zs] + piece) & 1) * 32, 32), 32)
                for third in range(3):
                    grad_w[third, row, lane] = part[
                        cs, :, third * 256 : third * 256 + 256
                    ].astype(F32)


def add(*parts):
    total = parts[0].astype(F32)
    for part in parts[1:]:
        total = total + part.astype(F32)
    return total.astype(BF)


def per_device(tokens, w_qkv, weight_table, weight_index, cotangent):
    y, x, core = lax.axis_index("y"), lax.axis_index("x"), lax.axis_index("core")
    z = lax.axis_index("dp")
    pos = jnp.stack(
        [y, x, core, z, (SETS >> z) & 1, (HALVES >> z) & 1, (HALVES >> (z ^ 1)) & 1]
    ).astype(jnp.int32)
    inputs = tokens[0]

    rows = weight_index.reshape(1, 12)
    rows = jnp.concatenate([rows, swap(rows, "dp", 8, 1)], axis=0)
    idx = jnp.concatenate([rows, swap(rows, "core", 2, 1)], axis=0)
    scalars = [pos, idx, weight_table]

    w_own, w_core, c_own, c_core, c_z = call(
        prepare_kernel,
        [pos, jnp.transpose(w_qkv, (1, 0, 2)), cotangent[0]],
        1,
        [((64, COLS), BF)] * 2 + [((BLOCK, 256), BF)] * 2 + [((BLOCK, 512), BF)],
        grant=58,
        nbytes=2 * MIB,
    )

    chunk = jnp.concatenate([w_own, swap(w_core, "core", 2, 1)], axis=0)
    near = [chunk] + [ring(chunk, 0, step) for step in (1, 2, 3)]
    mine = [jnp.concatenate(near[:2], axis=0), jnp.concatenate(near[2:], axis=0)]
    behind_low, ahead_high = ring(mine[0], 1, 3), ring(mine[1], 1, 1)
    far = [ring(behind_low, 1, 3), ring(ahead_high, 1, 1)]
    ahead_low, behind_high = ring(mine[0], 1, 1), ring(mine[1], 1, 3)
    gathered = mine + [ahead_low, ahead_high, behind_low, behind_high] + far

    c_core = swap(c_core, "core", 2, 1)
    c_z = swap(c_z, "dp", 8, 1)
    c_near, c_across = c_z[:, :256], swap(c_z[:, 256:], "core", 2, 1)
    own = behind(inputs, index=rows)
    tok01 = behind(swap(own, "dp", 8, 1), c_across, *far, ahead_low, behind_high)
    tok10, tok11 = swap(own, "core", 2, 1), swap(tok01, "core", 2, 1)
    toks = [own, tok01, tok10, tok11]

    tile = (HEAD, HEAD)
    qkv, cots, s1, x0, g1, m2, m3, m4, m5 = call(
        project_kernel,
        scalars + [c_own, c_near, c_core, c_across] + gathered + toks,
        3,
        [
            ((4, BLOCK, COLS), BF),
            ((4, BLOCK, 256), BF),
            ((4, 2) + tile, BF),
            ((2, 2) + tile, BF),
            ((4, 2) + tile, F32),
            ((2, 2) + tile, F32),
            ((2, 2) + tile, F32),
            ((2, 2) + tile, BF),
            ((2, 2) + tile, BF),
        ],
        scratch=[
            pltpu.VMEM((D, COLS), BF),
            pltpu.VMEM((4, BLOCK, D), BF),
            pltpu.SemaphoreType.DMA((4,)),
        ],
        grant=52,
        n_any=4,
        flops=2 * 1024 * D * COLS,
        nbytes=10 * MIB,
    )

    cx = [swap(x0, "x", 4, mask) for mask in (1, 2, 3)]
    dy = [swap(m, "y", 4, mask) for mask, m in ((1, m4), (2, m5), (3, m5))]
    (loc,) = call(
        local_kernel,
        scalars + [qkv, cots],
        3,
        [((4, BLOCK, 1024), F32)],
        grant=12,
        flops=8 * 6 * 2 * BLOCK * BLOCK * HEAD,
        nbytes=8 * MIB,
    )
    x1 = add(x0, *cx)
    cy = [swap(x1, "y", 4, mask) for mask in (1, 2, 3)]
    high = dy[0].astype(F32) + dy[1].astype(F32) + dy[2].astype(F32)
    near = (high + m2).astype(BF)
    far = (high + m3).astype(BF)
    dx = [swap(m, "x", 4, mask) for mask, m in ((1, near), (2, far), (3, far))]

    attn, grads, low, high = call(
        finish_kernel,
        scalars + toks + [cots, qkv, loc, s1, g1] + cx + cy + [high.astype(BF)] + dx,
        3,
        [
            ((4, BLOCK, 256), BF),
            ((4, BLOCK, COLS), BF),
            ((2, 128, COLS), BF),
            ((2, 128, COLS), BF),
        ],
        grant=24,
        flops=1024 * D * COLS,
        nbytes=12 * MIB,
    )
    low, high = ring(low, 1, 3), ring(high, 1, 1)
    from_core = swap(attn[2:], "core", 2, 1)
    onward, backward = call(
        functools.partial(gradient_kernel, (1, 3)),
        [pos] + toks + [grads, from_core],
        1,
        [((4, 128, COLS), BF)] * 2,
        grant=20,
        flops=1024 * D * COLS,
        nbytes=9 * MIB,
        n_any=1,
    )
    onward = jnp.concatenate([add(onward[:2], low), onward[2:]], axis=0)
    backward = jnp.concatenate([backward[:2], add(backward[2:], high)], axis=0)
    onward, backward = ring(onward, 1, 3), ring(backward, 1, 1)
    back = swap(jnp.stack([attn[1], from_core[1]], axis=0), "dp", 8, 1)
    (own,) = call(
        functools.partial(gradient_kernel, (0,)),
        [pos] + toks + [grads, from_core],
        1,
        [((4, 128, COLS), BF)],
        grant=20,
        flops=1024 * 512 * COLS,
        nbytes=9 * MIB,
        n_any=1,
    )
    *total, attn_out = call(
        total_kernel,
        [pos, own, onward, backward, attn, from_core, back],
        1,
        [((128, COLS), BF)] * 4 + [((BLOCK, 1024), BF)],
        grant=10,
        nbytes=4 * MIB,
    )
    chip_sum = add(total[0], *[ring(total[step], 0, -step) for step in (1, 2, 3)])
    pair = jnp.stack([chip_sum[:64], swap(chip_sum[64:], "core", 2, 1)], axis=0)
    mine = add(pair[:, :32], same_set_neighbour(pair[:, 32:]))
    mine = add(mine, same_set_far(mine))
    near = same_set_neighbour(mine)
    theirs = swap(mine, "dp", 8, 1)
    beyond = swap(near, "dp", 8, 1)

    (grad_w,) = call(
        place_kernel,
        [pos, mine, near, theirs, beyond],
        1,
        [((3, 64, 1024), F32)],
        grant=6,
        nbytes=3 * MIB,
    )
    return attn_out[None], jnp.transpose(grad_w, (1, 0, 2))


def solution(mesh):
    grid = Mesh(mesh.devices.reshape(4, 4, 2, 8), ("y", "x", "core", "dp"))
    seq = ("y", "x", "core")
    return jax.shard_map(
        per_device,
        mesh=grid,
        in_specs=(P("dp", seq, None), P(seq, None, None), P(), P("dp", seq, None), P("dp", seq, None)),
        out_specs=(P("dp", seq, None), P(seq, None, None)),
        check_vma=False,
    )
```

```python
import functools
import math

import jax
import jax.numpy as jnp
from jax import lax
from jax.experimental import pallas as pl
from jax.experimental.pallas import tpu as pltpu
from jax.sharding import Mesh, PartitionSpec as P

BF = jnp.bfloat16
F32 = jnp.float32
HEAD = 128
QB = 128
BLOCK = 256
D = 2048
COLS = 768
MIB = 1024 * 1024
SETS = 0x66
HALVES = 0xB4


def ring(value, phase, step):
    pairs = []
    for y in range(4):
        for x in range(4):
            for core in range(2):
                at = (y, (x - step) % 4) if core == phase else ((y - step) % 4, x)
                pairs.append(((y * 4 + x) * 2 + core, (at[0] * 4 + at[1]) * 2 + core))
    return lax.ppermute(value, ("y", "x", "core"), pairs)


def swap(value, axis, size, mask):
    return lax.ppermute(value, axis, [(i, i ^ mask) for i in range(size)])


def same_set_neighbour(value):
    return lax.ppermute(value, "dp", [(z, (z + 1 if z % 2 else z - 1) % 8) for z in range(8)])


def same_set_far(value):
    return lax.ppermute(value, "dp", [(z, ((7 if SETS >> z & 1 else 3) - z) % 8) for z in range(8)])


def behind(value, *others, index=None):
    zero = sum([other[0, 0].astype(F32) for other in others], jnp.zeros((), F32)) * 0.0
    if index is not None:
        zero = zero + (index[-1, -1] < 0).astype(F32)
    return (value.astype(F32) + zero).astype(value.dtype)


def dot(a, b, ca, cb):
    return lax.dot_general(a, b, (((ca,), (cb,)), ((), ())), preferred_element_type=F32)


def smem():
    return pl.BlockSpec(memory_space=pltpu.SMEM)


def vmem():
    return pl.BlockSpec(memory_space=pltpu.VMEM)


def call(kernel, args, n_smem, outs, scratch=(), grant=16, flops=0, nbytes=0, n_any=0):
    return pl.pallas_call(
        kernel,
        out_shape=[jax.ShapeDtypeStruct(*out) for out in outs],
        in_specs=[smem()] * n_smem
        + [vmem()] * (len(args) - n_smem - n_any)
        + [pl.BlockSpec(memory_space=pl.ANY)] * n_any,
        out_specs=[vmem()] * len(outs),
        scratch_shapes=list(scratch),
        compiler_params=pltpu.CompilerParams(vmem_limit_bytes=grant * MIB),
        cost_estimate=pl.CostEstimate(flops=flops, bytes_accessed=nbytes, transcendentals=0),
    )(*args)


def lanes(start):
    return pl.ds(pl.multiple_of(start, HEAD), HEAD)


def level_coef(pos, idx, table, blk, group, level, head):
    cs = blk // 2
    y, x, core = pos[0], pos[1], pos[2]
    row = idx[blk, group * 6 + level]
    lam = table[row, (core * 2 + pos[4]) * 2 + head]
    if level == 0:
        return lam * (1.0 / math.sqrt(HEAD * BLOCK))
    bit = [(core + cs) & 1, x & 1, (x >> 1) & 1, y & 1, (y >> 1) & 1][level - 1]
    return lam * bit.astype(F32) * (1.0 / math.sqrt(HEAD * 2 ** (level - 1) * BLOCK))


def prepare_kernel(pos, w, cot, w_own, w_core, own, to_core, to_z):
    core, kind = pos[2], pos[4]

    def columns(cs, zs):
        group = ((core + cs) & 1) * 2 + ((kind + zs) & 1)
        return pl.ds(pl.multiple_of(group * 256, 256), 256)

    for third in range(3):
        at = slice(third * 256, third * 256 + 256)
        w_own[:, at] = w[third, :, columns(0, 0)]
        w_core[:, at] = w[third, :, columns(1, 0)]
    own[...] = cot[:, columns(0, 0)]
    to_core[...] = cot[:, columns(1, 0)]
    to_z[:, :256] = cot[:, columns(0, 1)]
    to_z[:, 256:] = cot[:, columns(1, 1)]


def project_kernel(pos, idx, table, t0, t1, t2, t3, c0, c1, c2, c3, *refs):
    toks = (t0, t1, t2, t3)
    parts = (refs[0:2], refs[2:4], refs[6:8], refs[4:6])
    qkv, cots, s1, x0, g1, m2, m3, m4, m5, w = refs[8:]
    y, x, core = pos[0], pos[1], pos[2]
    for slot in range(4):
        for dist in range(4):
            yy = (y + dist + core * (slot - dist)) & 3
            xx = (x + slot + core * (dist - slot)) & 3
            for cs in range(2):
                row = pl.multiple_of((yy * 4 + xx) * 128 + ((core + cs) & 1) * 64, 64)
                start = (slot % 2) * 128 + cs * 64
                w[pl.ds(row, 64), :] = parts[dist][slot // 2][start : start + 64, :]
    for blk, src in enumerate((c0, c1, c2, c3)):
        cots[blk] = src[...]

    @pl.loop(0, 3)
    def _(part):
        cols = pl.ds(pl.multiple_of(part * 256, 256), 256)
        for blk in range(4):
            qkv[blk, :, cols] = dot(toks[blk][...], w[:, cols], 1, 0).astype(BF)

    @pl.loop(0, 4)
    def _(step):
        zs, h = step // 2, step % 2
        total = None
        sums = [None] * 4
        for cs in range(2):
            blk = cs * 2 + zs
            state = dot(qkv[blk, :, lanes(256 + h * HEAD)], qkv[blk, :, lanes(512 + h * HEAD)], 0, 0)
            s1[blk, h] = state.astype(BF)
            total = state if total is None else total + state
            first = None
            for g in range(2):
                rows = slice(g * QB, g * QB + QB)
                outer = dot(qkv[blk, rows, lanes(h * HEAD)], cots[blk, rows, lanes(h * HEAD)], 0, 0)
                term = outer * level_coef(pos, idx, table, blk, g, 1, h)
                first = term if first is None else first + term
                for k in range(4):
                    term = outer * level_coef(pos, idx, table, blk, g, k + 2, h)
                    sums[k] = term if sums[k] is None else sums[k] + term
            g1[blk, h] = first
        x0[zs, h] = total.astype(BF)
        for out, value in zip((m2, m3, m4, m5), sums):
            out[zs, h] = value.astype(out.dtype)


def local_kernel(pos, idx, table, qkv, cots, loc):
    rows = lax.broadcasted_iota(jnp.int32, (BLOCK, BLOCK), 0)
    cols = lax.broadcasted_iota(jnp.int32, (BLOCK, BLOCK), 1)
    causal = rows >= cols
    upper = rows < QB

    @pl.loop(0, 4)
    def _(blk):
        for h in range(2):
            qs = slice(h * HEAD, h * HEAD + HEAD)
            ks = slice(256 + h * HEAD, 256 + h * HEAD + HEAD)
            vs = slice(512 + h * HEAD, 512 + h * HEAD + HEAD)
            q, k, v, c = qkv[blk, :, qs], qkv[blk, :, ks], qkv[blk, :, vs], cots[blk, :, qs]
            scale = jnp.where(
                upper,
                level_coef(pos, idx, table, blk, 0, 0, h),
                level_coef(pos, idx, table, blk, 1, 0, h),
            )
            scale = jnp.where(causal, scale, 0.0)
            scores = (dot(q, k, 1, 1) * scale).astype(BF)
            dscores = (dot(c, v, 1, 1) * scale).astype(BF)
            loc[blk, :, qs] = dot(dscores, k, 1, 0)
            loc[blk, :, ks] = dot(dscores, q, 0, 0)
            loc[blk, :, vs] = dot(scores, c, 0, 0)
            loc[blk, :, 768 + h * HEAD : 768 + h * HEAD + HEAD] = dot(scores, v, 1, 0)


def gradient_pair(pos, toks, grads, dist, first, store):
    y, x, core, half = pos[0], pos[1], pos[2], pos[5]
    at = []
    for slot in (first, first + 1):
        yy = (y + dist + core * (slot - dist)) & 3
        xx = (x + slot + core * (dist - slot)) & 3
        at.append(lanes((yy * 4 + xx) * 128))
    part = None
    for blk in range(4):
        rows = jnp.concatenate([toks[blk][:, at[0]], toks[blk][:, at[1]]], axis=1)
        term = dot(rows, grads[blk], 0, 0)
        part = term if part is None else part + term
    part = part.astype(BF)
    for sub in range(2):
        for c in range(2):
            for piece in range(2):
                row = ((c + core) & 1) * 64 + ((piece + half) & 1) * 32
                start = sub * 128 + c * 64 + piece * 32
                store(sub, pl.ds(pl.multiple_of(row, 32), 32), part[start : start + 32])


def finish_kernel(pos, idx, table, *refs):
    toks = refs[0:4]
    cots, qkv, loc, s1, g1 = refs[4:9]
    cx1, cx2, cx3, cy1, cy2, cy3 = refs[9:15]
    own, r1, r2, r3 = refs[15:19]
    attn, grads, low, high = refs[19:]

    @pl.loop(0, 4)
    def _(step):
        zs, h = step // 2, step % 2
        far = [
            None,
            cx1[zs, h].astype(F32),
            cx2[zs, h].astype(F32) + cx3[zs, h].astype(F32),
            cy1[zs, h].astype(F32),
            cy2[zs, h].astype(F32) + cy3[zs, h].astype(F32),
        ]
        chip = own[zs, h].astype(F32) + r1[zs, h].astype(F32)
        chip = chip + r2[zs, h].astype(F32) + r3[zs, h].astype(F32)
        qs, ks = lanes(h * HEAD), lanes(256 + h * HEAD)
        vs, ats = lanes(512 + h * HEAD), lanes(768 + h * HEAD)
        for cs in range(2):
            blk = cs * 2 + zs
            other = (1 - cs) * 2 + zs
            far[0] = s1[other, h].astype(F32)
            grad = (chip + g1[other, h]).astype(BF)
            for g in range(2):
                rows = slice(g * QB, g * QB + QB)
                mixed = None
                for level in range(1, 6):
                    term = far[level - 1] * level_coef(pos, idx, table, blk, g, level, h)
                    mixed = term if mixed is None else mixed + term
                mixed = mixed.astype(BF)
                out = loc[blk, rows, ats] + dot(qkv[blk, rows, qs], mixed, 1, 0)
                attn[blk, rows, qs] = out.astype(BF)
                dq = loc[blk, rows, qs] + dot(cots[blk, rows, qs], mixed, 1, 1)
                grads[blk, rows, qs] = dq.astype(BF)
            dk = loc[blk, :, ks] + dot(qkv[blk, :, vs], grad, 1, 1)
            grads[blk, :, ks] = dk.astype(BF)
            dv = loc[blk, :, vs] + dot(qkv[blk, :, ks], grad, 1, 0)
            grads[blk, :, vs] = dv.astype(BF)

    for first, out in ((0, low), (2, high)):

        def store(sub, rows, value, out=out):
            out[sub, rows, :] = value

        gradient_pair(pos, toks, grads, 2, first, store)


def gradient_kernel(dists, pos, t0, t1, t2, t3, grads, _, *outs):
    toks = (t0, t1, t2, t3)

    @pl.loop(0, 2)
    def _(pair):
        for dist, out in zip(dists, outs):

            def store(sub, rows, value, out=out):
                out[pair * 2 + sub, rows, :] = value

            gradient_pair(pos, toks, grads, dist, pair * 2, store)


def total_kernel(pos, own, r1, r2, attn, from_core, from_z, t0, t1, t2, t3, attn_out):
    core, kind = pos[2], pos[4]
    for slot, out in enumerate((t0, t1, t2, t3)):
        total = own[slot].astype(F32) + r1[slot].astype(F32) + r2[slot].astype(F32)
        out[...] = total.astype(BF)
    attns = ((attn.at[0], from_z.at[0]), (from_core.at[0], from_z.at[1]))
    for cs in range(2):
        for zs in range(2):
            group = ((core + cs) & 1) * 2 + ((kind + zs) & 1)
            attn_out[:, pl.ds(pl.multiple_of(group * 256, 256), 256)] = attns[cs][zs][...]


def place_kernel(pos, mine, near, theirs, beyond, grad_w):
    core, kind = pos[2], pos[4]
    halves = (pos[5], pos[6])
    for cs in range(2):
        for zs in range(2):
            group = ((core + cs) & 1) * 2 + ((kind + zs) & 1)
            lane = pl.ds(pl.multiple_of(group * 256, 256), 256)
            for piece in range(2):
                part = ((mine, near), (theirs, beyond))[zs][piece]
                row = pl.ds(pl.multiple_of(((halves[zs] + piece) & 1) * 32, 32), 32)
                for third in range(3):
                    grad_w[third, row, lane] = part[
                        cs, :, third * 256 : third * 256 + 256
                    ].astype(F32)


def add(*parts):
    total = parts[0].astype(F32)
    for part in parts[1:]:
        total = total + part.astype(F32)
    return total.astype(BF)


def per_device(tokens, w_qkv, weight_table, weight_index, cotangent):
    y, x, core = lax.axis_index("y"), lax.axis_index("x"), lax.axis_index("core")
    z = lax.axis_index("dp")
    pos = jnp.stack(
        [y, x, core, z, (SETS >> z) & 1, (HALVES >> z) & 1, (HALVES >> (z ^ 1)) & 1]
    ).astype(jnp.int32)
    inputs = tokens[0]

    rows = weight_index.reshape(1, 12)
    rows = jnp.concatenate([rows, swap(rows, "dp", 8, 1)], axis=0)
    idx = jnp.concatenate([rows, swap(rows, "core", 2, 1)], axis=0)
    scalars = [pos, idx, weight_table]

    w_own, w_core, c_own, c_core, c_z = call(
        prepare_kernel,
        [pos, jnp.transpose(w_qkv, (1, 0, 2)), cotangent[0]],
        1,
        [((64, COLS), BF)] * 2 + [((BLOCK, 256), BF)] * 2 + [((BLOCK, 512), BF)],
        grant=58,
        nbytes=2 * MIB,
    )

    chunk = jnp.concatenate([w_own, swap(w_core, "core", 2, 1)], axis=0)
    near = [chunk] + [ring(chunk, 0, step) for step in (1, 2, 3)]
    mine = [jnp.concatenate(near[:2], axis=0), jnp.concatenate(near[2:], axis=0)]
    behind_low, ahead_high = ring(mine[0], 1, 3), ring(mine[1], 1, 1)
    far = [ring(behind_low, 1, 3), ring(ahead_high, 1, 1)]
    ahead_low, behind_high = ring(mine[0], 1, 1), ring(mine[1], 1, 3)
    gathered = mine + [ahead_low, ahead_high, behind_low, behind_high] + far

    c_core = swap(c_core, "core", 2, 1)
    c_z = swap(c_z, "dp", 8, 1)
    c_near, c_across = c_z[:, :256], swap(c_z[:, 256:], "core", 2, 1)
    own = behind(inputs, index=rows)
    tok01 = behind(swap(own, "dp", 8, 1), c_across, *far, ahead_low, behind_high)
    tok10, tok11 = swap(own, "core", 2, 1), swap(tok01, "core", 2, 1)
    toks = [own, tok01, tok10, tok11]

    tile = (HEAD, HEAD)
    qkv, cots, s1, x0, g1, m2, m3, m4, m5 = call(
        project_kernel,
        scalars + toks + [c_own, c_near, c_core, c_across] + gathered,
        3,
        [
            ((4, BLOCK, COLS), BF),
            ((4, BLOCK, 256), BF),
            ((4, 2) + tile, BF),
            ((2, 2) + tile, BF),
            ((4, 2) + tile, F32),
            ((2, 2) + tile, F32),
            ((2, 2) + tile, F32),
            ((2, 2) + tile, BF),
            ((2, 2) + tile, BF),
        ],
        scratch=[pltpu.VMEM((D, COLS), BF)],
        grant=52,
        flops=2 * 1024 * D * COLS,
        nbytes=10 * MIB,
    )

    cx = [swap(x0, "x", 4, mask) for mask in (1, 2, 3)]
    dy = [swap(m, "y", 4, mask) for mask, m in ((1, m4), (2, m5), (3, m5))]
    (loc,) = call(
        local_kernel,
        scalars + [qkv, cots],
        3,
        [((4, BLOCK, 1024), F32)],
        grant=12,
        flops=8 * 6 * 2 * BLOCK * BLOCK * HEAD,
        nbytes=8 * MIB,
    )
    x1 = add(x0, *cx)
    cy = [swap(x1, "y", 4, mask) for mask in (1, 2, 3)]
    high = dy[0].astype(F32) + dy[1].astype(F32) + dy[2].astype(F32)
    near = (high + m2).astype(BF)
    far = (high + m3).astype(BF)
    dx = [swap(m, "x", 4, mask) for mask, m in ((1, near), (2, far), (3, far))]

    attn, grads, low, high = call(
        finish_kernel,
        scalars + toks + [cots, qkv, loc, s1, g1] + cx + cy + [high.astype(BF)] + dx,
        3,
        [
            ((4, BLOCK, 256), BF),
            ((4, BLOCK, COLS), BF),
            ((2, 128, COLS), BF),
            ((2, 128, COLS), BF),
        ],
        grant=24,
        flops=1024 * D * COLS,
        nbytes=12 * MIB,
    )
    low, high = ring(low, 1, 3), ring(high, 1, 1)
    from_core = swap(attn[2:], "core", 2, 1)
    onward, backward = call(
        functools.partial(gradient_kernel, (1, 3)),
        [pos] + toks + [grads, from_core],
        1,
        [((4, 128, COLS), BF)] * 2,
        grant=20,
        flops=1024 * D * COLS,
        nbytes=9 * MIB,
        n_any=1,
    )
    onward = jnp.concatenate([add(onward[:2], low), onward[2:]], axis=0)
    backward = jnp.concatenate([backward[:2], add(backward[2:], high)], axis=0)
    onward, backward = ring(onward, 1, 3), ring(backward, 1, 1)
    back = swap(jnp.stack([attn[1], from_core[1]], axis=0), "dp", 8, 1)
    (own,) = call(
        functools.partial(gradient_kernel, (0,)),
        [pos] + toks + [grads, from_core],
        1,
        [((4, 128, COLS), BF)],
        grant=20,
        flops=1024 * 512 * COLS,
        nbytes=9 * MIB,
        n_any=1,
    )
    *total, attn_out = call(
        total_kernel,
        [pos, own, onward, backward, attn, from_core, back],
        1,
        [((128, COLS), BF)] * 4 + [((BLOCK, 1024), BF)],
        grant=10,
        nbytes=4 * MIB,
    )
    chip_sum = add(total[0], *[ring(total[step], 0, -step) for step in (1, 2, 3)])
    pair = jnp.stack([chip_sum[:64], swap(chip_sum[64:], "core", 2, 1)], axis=0)
    mine = add(pair[:, :32], same_set_neighbour(pair[:, 32:]))
    mine = add(mine, same_set_far(mine))
    near = same_set_neighbour(mine)
    theirs = swap(mine, "dp", 8, 1)
    beyond = swap(near, "dp", 8, 1)

    (grad_w,) = call(
        place_kernel,
        [pos, mine, near, theirs, beyond],
        1,
        [((3, 64, 1024), F32)],
        grant=6,
        nbytes=3 * MIB,
    )
    return attn_out[None], jnp.transpose(grad_w, (1, 0, 2))


def solution(mesh):
    grid = Mesh(mesh.devices.reshape(4, 4, 2, 8), ("y", "x", "core", "dp"))
    seq = ("y", "x", "core")
    return jax.shard_map(
        per_device,
        mesh=grid,
        in_specs=(P("dp", seq, None), P(seq, None, None), P(), P("dp", seq, None), P("dp", seq, None)),
        out_specs=(P("dp", seq, None), P(seq, None, None)),
        check_vma=False,
    )
```
